32 devices in a mesh: seq: 4 (over z), exp: 8 (over y, x, core).
Axes of the slice: x: 2, y: 2, z: 4, core: 2. Of those that a mesh axis runs over, the one named last changes fastest.
Arguments:
- byte_embed: bfloat16 [8, 512, 1024], P('exp', 'seq'), may hold values from -16 to 16
- score_weight: float32 [1024], replicated, may hold values from -1 to 1
- norm_gain: float32 [1024], replicated, may hold values from 0.25 to 1.75
- router: bfloat16 [1024, 8], replicated, may hold values from -0.1875 to 0.1875
- routes: int32 [8, 128, 2], P('exp', 'seq'), may hold values from 0 to 7, all different within a row; in each aligned block of 32 rows (0 to 31, 32 to 63, ..., all dimensions but the last counted through in order) at most 12 rows name the same one
- expert_in: bfloat16 [8, 1024, 4096], P('exp', None, 'seq'), may hold values from -0.1875 to 0.1875
- expert_out: bfloat16 [8, 4096, 1024], P('exp', 'seq'), may hold values from -0.09375 to 0.09375
- cotangent: bfloat16 [8, 128, 1024], P('exp', 'seq'), may hold values from -6 to 6
Outputs:
- grad_embed: bfloat16 [8, 512, 1024], P('exp', 'seq')
- grad_in: float32 [8, 1024, 4096], P('exp', None, 'seq')
- grad_out: float32 [8, 4096, 1024], P('exp', 'seq')
The draws below stay inside these ranges and needn't reach their ends.
Inputs may be any that keep to these rules, and one draw needn't show every extreme that they name: `routes`: among the 32 tokens of one device, at most 12 pairs name the same expert, and some device reaches 12 for some expert. The two experts of a token differ.
All inputs are finite; a program needn't handle non-finite values.
Results may differ from the reference program's by a relative error of at most 0.014.
Values may be sent and summed in bfloat16 or wider, within the bound.
No kernel may reach another device: no remote copies, remote signals or barrier semaphores. Data moves between devices by JAX's collectives and lax.ppermute only.
A program may use at most 64 MiB of HBM per device.

```python
import math
import jax
import jax.numpy as jnp
import numpy as np
from jax import lax

D = 1024
FF = 4096
EXPERTS = 8
TOK_DEV = 32
DOCS = 8
LENGTH = 512
TOK_DOC = 128
CAP = 12
N_SEQ = 4


def shared_score(key):
    raw = jax.random.truncated_normal(jax.random.fold_in(key, 11), -4.0, 4.0, (D,), jnp.float32)
    return raw * D ** (-0.5)


def draw_score_weight(key, part):
    return shared_score(key)


def draw_byte_embed(key, part):
    shape = (DOCS, LENGTH, D)
    return jax.random.truncated_normal(jax.random.fold_in(key, 1), -4.0, 4.0, shape, jnp.float32).astype(jnp.bfloat16)


def block_scale(rng, dims, cuts, low, high):
    def one(axis_at, blocks):
        steps = jax.random.uniform(jax.random.fold_in(jax.random.fold_in(rng, 6), axis_at), (blocks,), jnp.float32, low / len(cuts), high / len(cuts))
        return jnp.repeat(jnp.exp(steps), dims[axis_at] // blocks).reshape((-1,) + (1,) * (len(dims) - axis_at - 1))

    level = one(*cuts[0])
    for cut in cuts[1:]:
        level = level * one(*cut)
    return level


def assign_block(own_key, own, number, rows, amount, top, reach, skew):
    order = jax.random.permutation(own_key, amount)
    packed, usual = load_shares(amount, rows * top, reach, skew, True), load_shares(amount, rows * top, reach, skew, False)
    places = jnp.arange(amount)

    def named(lengths, turn):
        used = int((lengths > 0).sum())
        fixed = max(1, used // 4)
        moved = fixed + (places - fixed + turn * (used - fixed)) % max(1, amount - fixed)
        return jnp.zeros((amount,), jnp.int32).at[order[jnp.where(places < fixed, places, moved)]].set(jnp.asarray(lengths, jnp.int32))

    lengths = jnp.where(number % 4 == 0, named(packed, number // 4), named(usual, number - number // 4 - 1))
    mixed = jax.random.permutation(jax.random.fold_in(own, 3), amount)
    giver, taker = mixed[0:amount // 2 * 2:2], mixed[1:amount // 2 * 2:2]
    margin = jnp.minimum(lengths[giver] - 1, reach - lengths[taker]) // 2
    margin = jnp.where((giver == order[0]) | (taker == order[0]) | (lengths[taker] == 0), 0, jnp.maximum(margin, 0))
    moved = jax.random.randint(jax.random.fold_in(own, 4), (amount // 2,), 0, 1 << 20) % (margin + 1)
    lengths = lengths.at[giver].add(-moved).at[taker].add(moved)
    members = jnp.searchsorted(jnp.cumsum(lengths), jnp.arange(rows * top), side="right").astype(jnp.int32)
    grid = members.reshape(top, rows).T
    grid = grid[jax.random.permutation(jax.random.fold_in(own, 1), rows)]
    turn = jax.random.randint(jax.random.fold_in(own, 2), (rows, 1), 0, top)
    return jnp.take_along_axis(grid, (jnp.arange(top)[None, :] + turn) % top, axis=1)


def load_shares(amount, total, bound, slope, full):
    portions = [(1 << 20) // math.isqrt(rank ** slope) + 1 for rank in range(1, amount + 1)]
    largest = bound if full else min(bound, max(-(-total // amount), total * portions[0] // sum(portions)))
    least = 1 if total - largest >= amount - 1 else 0
    given, spare = [largest] + [least] * (amount - 1), total - largest - least * (amount - 1)
    while spare > 0:
        candidates = [i for i in range(1, amount) if given[i] < largest] or [i for i in range(1, amount) if given[i] < bound]
        pool, remaining = sum([portions[i] for i in candidates]), spare
        for i in candidates:
            extra = min(bound - given[i], max(1, remaining * portions[i] // pool), spare)
            given[i] = given[i] + extra
            spare = spare - extra
    return np.array(given)


def gaussian(own_key, shape, spread, reach, cuts=(), held_as=jnp.bfloat16):
    result = jax.random.normal(own_key, shape, jnp.float32) * spread
    if len(cuts) > 0:
        result = block_scale(own_key, shape, cuts, -0.22, 0.18) * result
    return jnp.clip(result, min=-reach, max=reach).astype(held_as)


def setup_inputs(seed: int = 0) -> dict:
    seeds = jax.random.split(jax.random.key(seed), 9)
    byte_embed = draw_byte_embed(jax.random.fold_in(seeds[8], 71), 0)
    score_weight = draw_score_weight(jax.random.fold_in(seeds[8], 71), 0)
    norm_gain = jnp.clip(1.0 + 0.15 * jax.random.normal(seeds[2], (D,), jnp.float32), 0.25, 1.75)
    router = gaussian(seeds[3], (D, EXPERTS), D ** -0.5, 0.1875)
    routes_keys = jax.random.split(jax.random.fold_in(seeds[4], 1), DOCS * TOK_DOC // TOK_DEV)
    routes_turns = jax.random.permutation(jax.random.fold_in(seeds[4], 3), DOCS * TOK_DOC // TOK_DEV)
    routes = jax.vmap(lambda own, number: assign_block(jax.random.fold_in(seeds[4], 2), own, number, TOK_DEV, EXPERTS, 2, CAP, 2))(routes_keys, routes_turns).reshape((DOCS, TOK_DOC, 2))
    expert_in = gaussian(seeds[5], (EXPERTS, D, FF), D ** -0.5, 0.1875, ((0, 8), (2, 4)))
    expert_out = gaussian(seeds[6], (EXPERTS, FF, D), FF ** -0.5, 0.09375, ((0, 8), (1, 4)))
    cotangent = gaussian(seeds[7], (DOCS, TOK_DOC, D), 1.0, 6.0, ((0, 8), (1, 4)))
    return dict(byte_embed=byte_embed, score_weight=score_weight, norm_gain=norm_gain, router=router, routes=routes, expert_in=expert_in, expert_out=expert_out, cotangent=cotangent)


SQRT_HALF = 0.7071067811865476
INV_ROOT_TWO_PI = 0.3989422804014327

def front(inputs, norm_gain, score_weight, router, routes):
    batches, length, features = inputs.shape
    highest = lax.Precision.HIGHEST
    quartets = inputs.reshape(batches, length // 4, 4, features)
    pair_means = quartets.reshape(batches, length // 4, 2, 2, features).mean(axis=3)
    quad_mean = quartets.mean(axis=2)
    score_one = jnp.einsum('btqd,d->btq', quartets, score_weight, precision=highest)
    score_two = jnp.repeat(jnp.einsum('btpd,d->btp', pair_means, score_weight, precision=highest), 2, axis=2)
    score_four = jnp.broadcast_to(jnp.einsum('btd,d->bt', quad_mean, score_weight, precision=highest)[:, :, None], score_one.shape)
    largest = jnp.maximum(jnp.maximum(score_one, score_two), score_four)
    weight_one = jnp.exp(score_one - largest)
    weight_two = jnp.exp(score_two - largest)
    weight_four = jnp.exp(score_four - largest)
    denominator = weight_one + weight_two + weight_four
    pair_full = jnp.repeat(pair_means, 2, axis=2)
    blended = (weight_one[..., None] * quartets + weight_two[..., None] * pair_full + weight_four[..., None] * quad_mean[:, :, None, :]) / denominator[..., None]
    tokens = blended.mean(axis=2)
    mean_square = lax.optimization_barrier(jnp.mean(tokens * tokens, axis=-1, keepdims=True))
    normed = tokens * lax.rsqrt(mean_square + 1e-06) * norm_gain
    logits = jnp.einsum('btd,de->bte', normed, router.astype(jnp.float32), precision=highest)
    experts = logits.shape[-1]
    sigmoid_all = 1.0 / (1.0 + jnp.exp(-logits))
    chosen = (routes[..., None] == jnp.arange(experts, dtype=jnp.int32)).astype(jnp.float32)
    picked = lax.optimization_barrier(jnp.sum(chosen * sigmoid_all[:, :, None, :], axis=-1))
    gate_values = picked / lax.optimization_barrier(jnp.sum(picked, axis=-1, keepdims=True))
    return (tokens, normed, gate_values)

def reference(byte_embed, score_weight, norm_gain, router, routes, expert_in, expert_out, cotangent):
    blocks = DOCS * N_SEQ
    slot_total = EXPERTS * blocks * CAP

    def forward_doc(pieces):
        embed_doc, routes_doc = pieces
        tokens, normed, gate_values = front(embed_doc[None].astype(jnp.float32), norm_gain, score_weight, router, routes_doc[None])
        return (normed[0].astype(jnp.bfloat16), gate_values[0])
    normed_all, gate_all = lax.map(forward_doc, (byte_embed, routes))
    token_count = DOCS * TOK_DOC
    normed_flat = normed_all.reshape(token_count, D)
    gate_flat = gate_all.reshape(token_count, 2)
    route_flat = routes.reshape(token_count, 2).astype(jnp.int32)
    cot_flat = cotangent.reshape(token_count, D)
    onehot = (route_flat[:, :, None] == jnp.arange(EXPERTS, dtype=jnp.int32)).astype(jnp.int32)
    running = jnp.cumsum(onehot.reshape(blocks, 2 * TOK_DEV, EXPERTS), axis=1).astype(jnp.int32)
    running = running.reshape(token_count, 2, EXPERTS)
    position = lax.optimization_barrier(jnp.sum(onehot * (running - 1), axis=2)).astype(jnp.int32)
    block_index = (jnp.arange(token_count, dtype=jnp.int32) // TOK_DEV).astype(jnp.int32)
    target = (route_flat * (blocks * CAP) + block_index[:, None] * CAP + position).reshape(-1).astype(jnp.int32)
    source = jnp.repeat(jnp.arange(token_count, dtype=jnp.int32), 2)
    slot_token = jnp.zeros((slot_total,), jnp.int32).at[target].set(source)
    slot_live = jnp.zeros((slot_total,), jnp.float32).at[target].set(1.0)
    slot_gate = jnp.zeros((slot_total,), jnp.float32).at[target].set(gate_flat.reshape(-1)).astype(jnp.bfloat16)
    hidden_share = FF // N_SEQ

    def expert_step(pieces):
        indices, live, gate_rows, weight_in, weight_out = pieces
        row_mask = live.astype(jnp.bfloat16)[:, None]
        token_rows = normed_flat[indices] * row_mask
        cot_rows = cot_flat[indices] * row_mask
        preact = jnp.dot(token_rows, weight_in, preferred_element_type=jnp.float32)
        normal_cdf = 0.5 * (1.0 + jax.scipy.special.erf(preact * SQRT_HALF))
        normal_pdf = INV_ROOT_TWO_PI * jnp.exp(-0.5 * preact * preact)
        hidden = preact * normal_cdf
        upstream = jnp.dot(cot_rows, weight_out.T, preferred_element_type=jnp.float32)
        gate_terms = lax.optimization_barrier(jnp.sum(hidden * upstream, axis=1))
        gate_column = gate_rows.astype(jnp.float32)[:, None]
        hidden_grad = (gate_column * upstream * (normal_cdf + preact * normal_pdf)).astype(jnp.bfloat16)
        gated_hidden = (gate_column * hidden).astype(jnp.bfloat16)
        grad_out = jnp.dot(gated_hidden.T, cot_rows, preferred_element_type=jnp.float32)
        grad_in = jnp.dot(token_rows.T, hidden_grad, preferred_element_type=jnp.float32)
        split_grad = hidden_grad.astype(jnp.float32).reshape(-1, N_SEQ, hidden_share)
        split_weight = weight_in.astype(jnp.float32).reshape(D, N_SEQ, hidden_share)
        partial_rows = jnp.einsum('rsf,dsf->rsd', split_grad, split_weight, precision=lax.Precision.HIGHEST)
        rounded = lax.optimization_barrier(partial_rows.astype(jnp.bfloat16))
        input_rows = lax.optimization_barrier(jnp.sum(rounded.astype(jnp.float32), axis=1)).astype(jnp.bfloat16)
        return (grad_in, grad_out, input_rows, gate_terms.astype(jnp.bfloat16))
    grad_in_all, grad_out_all, input_slots, gate_slots = lax.map(expert_step, (slot_token.reshape(EXPERTS, -1), slot_live.reshape(EXPERTS, -1), slot_gate.reshape(EXPERTS, -1), expert_in, expert_out))
    back_rows = input_slots.reshape(-1, D)[target].reshape(token_count, 2, D)
    normed_grad = lax.optimization_barrier(jnp.sum(back_rows.astype(jnp.float32), axis=1))
    gate_grad = gate_slots.reshape(-1)[target].reshape(token_count, 2).astype(jnp.float32)

    def backward_doc(pieces):
        embed_doc, routes_doc, cot_doc, normed_doc, gate_doc = pieces

        def local_front(values):
            return front(values, norm_gain, score_weight, router, routes_doc[None])
        outputs, pullback = jax.vjp(local_front, embed_doc[None].astype(jnp.float32))
        embed_grad, = pullback((cot_doc[None].astype(jnp.float32), normed_doc[None], gate_doc[None]))
        return embed_grad[0].astype(jnp.bfloat16)
    grad_embed = lax.map(backward_doc, (byte_embed, routes, cotangent, normed_grad.reshape(DOCS, TOK_DOC, D), gate_grad.reshape(DOCS, TOK_DOC, 2)))
    return (grad_embed, grad_in_all, grad_out_all)
```

```python
import functools
import jax
import jax.numpy as jnp
from jax import lax
from jax.experimental import pallas as pl
from jax.experimental.pallas import tpu as pltpu
from jax.sharding import PartitionSpec as P

SQRT_HALF = 0.7071067811865476
INV_ROOT_TWO_PI = 0.3989422804014327
LANES = 128
HALF = LANES // 2
BF = jnp.bfloat16
F32 = jnp.float32
HIGHEST = lax.Precision.HIGHEST
ROWS_T = (((0,), (0,)), ((), ()))
COLS = (((1,), (1,)), ((), ()))
VMEM_LIMIT = 56 * 1024 * 1024


def call(body, name, outs, args, scratch=(), flops=0, nbytes=0, **kwargs):
    return pl.pallas_call(
        body,
        name=name,
        out_shape=outs,
        scratch_shapes=list(scratch),
        compiler_params=pltpu.CompilerParams(vmem_limit_bytes=VMEM_LIMIT),
        cost_estimate=pl.CostEstimate(flops=flops, bytes_accessed=nbytes, transcendentals=0),
        **kwargs,
    )(*args)


def route_mask(routes_t, k, wrap):
    count = routes_t.shape[1]
    lane = lax.broadcasted_iota(jnp.int32, (LANES, count), 0)
    if wrap:
        lane = lane & (HALF - 1)
    mask_t = (lane == routes_t[k : k + 1, :]).astype(F32).astype(BF)
    row = lax.broadcasted_iota(jnp.int32, (count, count), 0)
    col = lax.broadcasted_iota(jnp.int32, (count, count), 1)
    eye = (row == col).astype(F32).astype(BF)
    return lax.dot_general(eye, mask_t, COLS, preferred_element_type=F32)


def cot_payload_kernel(cot_ref, routes_ref, out_ref):
    width = cot_ref.shape[1]
    routes_t = routes_ref[...]
    mask = route_mask(routes_t, 0, False) + route_mask(routes_t, 1, False)
    out_ref[:, :width] = cot_ref[...]
    out_ref[:, width:] = mask.astype(BF)


def quartet_order(count):
    row = lax.broadcasted_iota(jnp.int32, (4 * count, 4 * count), 0)
    col = lax.broadcasted_iota(jnp.int32, (4 * count, 4 * count), 1)
    return (4 * (row % count) + row // count == col).astype(F32).astype(BF)


def quartet_values(embed, count):
    ordered = jnp.dot(quartet_order(count), embed, preferred_element_type=F32)
    return [ordered[q * count : (q + 1) * count, :] for q in range(4)]


def quartet_scores(values, weight):
    ones = [jnp.sum(v * weight, axis=1, keepdims=True) for v in values]
    pairs = [0.5 * (ones[0] + ones[1]), 0.5 * (ones[2] + ones[3])]
    four = 0.5 * (pairs[0] + pairs[1])
    shares = []
    for q in range(4):
        scores = (ones[q], pairs[q // 2], four)
        largest = jnp.maximum(jnp.maximum(scores[0], scores[1]), scores[2])
        weights = [jnp.exp(s - largest) for s in scores]
        denominator = weights[0] + weights[1] + weights[2]
        shares.append([w / denominator for w in weights])
    return shares


def front_kernel(embed_ref, score_ref, gain_ref, router_ref, routes_ref, pay_ref, tok_ref, keep_ref, logit):
    count, width = tok_ref.shape
    experts = router_ref.shape[0]
    values = quartet_values(embed_ref[...], count)
    shares = quartet_scores(values, score_ref[...])
    whole = 0.25 * (shares[0][2] + shares[1][2] + shares[2][2] + shares[3][2])
    coefs = []
    for q in range(4):
        pair = 0.5 * (shares[q][1] + shares[q ^ 1][1])
        coefs.append(0.25 * (shares[q][0] + pair + whole))
    tokens = coefs[0] * values[0] + coefs[1] * values[1] + coefs[2] * values[2] + coefs[3] * values[3]
    tok_ref[...] = tokens
    scale = lax.rsqrt(jnp.mean(tokens * tokens, axis=1, keepdims=True) + 1e-06)
    normed = tokens * scale * gain_ref[...]
    logit[...] = jnp.zeros_like(logit)
    logit[:, :experts] = lax.dot_general(
        normed, router_ref[...].astype(F32), COLS, precision=HIGHEST, preferred_element_type=F32
    )
    logits = logit[...]
    sigmoid = 1.0 / (1.0 + jnp.exp(-logits))
    rest = 1.0 / (1.0 + jnp.exp(logits))
    routes_t = routes_ref[...]
    masks = [route_mask(routes_t, k, False) for k in range(2)]
    picked = [jnp.sum(m * sigmoid, axis=1, keepdims=True) for m in masks]
    others = [jnp.sum(m * rest, axis=1, keepdims=True) for m in masks]
    total = picked[0] + picked[1]
    gates = [p / total for p in picked]
    pay_ref[:, :width] = normed.astype(BF)
    pay_ref[:, width:] = (masks[0] * gates[0] + masks[1] * gates[1]).astype(BF)
    lane = lax.broadcasted_iota(jnp.int32, keep_ref.shape, 1)
    columns = coefs + [s for share in shares for s in share] + [scale] + gates + others
    kept = jnp.zeros(keep_ref.shape, F32)
    for i, column in enumerate(columns):
        kept = jnp.where(lane == i, column, kept)
    keep_ref[...] = kept


def cot_pick_kernel(pieces, chunks, rows, capacity, my_ref, *refs):
    ins, outs, pick_ref = refs[:pieces], refs[pieces : pieces + chunks], refs[pieces + chunks]
    count, full = ins[0].shape
    width = full - LANES
    tokens = pieces * count
    stacked = jnp.concatenate([r[...] for r in ins], axis=0)
    lane_row = lax.broadcasted_iota(jnp.int32, (LANES, LANES), 0)
    lane_col = lax.broadcasted_iota(jnp.int32, (LANES, LANES), 1)
    order = ((lane_row == (lane_col ^ my_ref[0])) & (lane_col < chunks)).astype(F32).astype(BF)
    named = jnp.dot(stacked[:, width:], order, preferred_element_type=F32).astype(BF)
    row = lax.broadcasted_iota(jnp.int32, (tokens, tokens), 0)
    col = lax.broadcasted_iota(jnp.int32, (tokens, tokens), 1)
    eye = (row == col).astype(F32).astype(BF)
    before = ((row < col) & (row // count == col // count)).astype(F32).astype(BF)
    named_t = lax.dot_general(named, eye, ROWS_T, preferred_element_type=F32)
    place_t = lax.dot_general(named, before, ROWS_T, preferred_element_type=F32)
    block = lax.broadcasted_iota(jnp.int32, (LANES, tokens), 1) // count
    place_t = jnp.where(named_t > 0.5, place_t + (block * capacity).astype(F32), -1.0)
    slot = lax.broadcasted_iota(jnp.int32, (rows, tokens), 0).astype(F32)
    for m in range(chunks):
        pick = (place_t[m : m + 1, :] == slot).astype(F32).astype(BF)
        pick_ref[m * rows : (m + 1) * rows, :] = pick
    chosen = jnp.dot(pick_ref[...], stacked[:, :width], preferred_element_type=F32).astype(BF)
    for m in range(chunks):
        outs[m][...] = chosen[m * rows : (m + 1) * rows, :]


def token_pick_kernel(pieces, chunks, rows, pick_ref, *refs):
    ins, outs = refs[:pieces], refs[pieces:]
    stacked = jnp.concatenate([r[...] for r in ins], axis=0)
    chosen = jnp.dot(pick_ref[...], stacked, preferred_element_type=F32).astype(BF)
    for m in range(chunks):
        outs[m][...] = chosen[m * rows : (m + 1) * rows, :]


def upstream_kernel(chunks, rows, *refs):
    ins, weight_ref, out_ref, rows_ref = refs[:chunks], refs[chunks], refs[chunks + 1], refs[chunks + 2]

    @pl.when(pl.program_id(0) == 0)
    def _():
        for m in range(chunks):
            rows_ref[m * rows : (m + 1) * rows, :] = ins[m][...]

    out_ref[...] = lax.dot_general(rows_ref[...], weight_ref[...], COLS, preferred_element_type=F32)


def expert_kernel(chunks, rows, my_ref, *refs):
    ins = refs[:chunks]
    upstream_ref, weight_ref = refs[chunks : chunks + 2]
    outs = refs[chunks + 2 : 2 * chunks + 2]
    rows_ref, gated_ref, grad_ref, total, terms, gate = refs[2 * chunks + 2 :]
    step = pl.program_id(0)
    width = rows_ref.shape[1]
    lane = lax.broadcasted_iota(jnp.int32, (rows, LANES), 1)

    @pl.when(step == 0)
    def _():
        for m in range(chunks):
            at = slice(m * rows, (m + 1) * rows)
            rows_ref[at, :] = ins[m][:, :width]
            tail = ins[m][:, width:].astype(F32)
            gate[at, :] = jnp.sum(jnp.where(lane == my_ref[0], tail, 0.0), axis=1, keepdims=True)

    preact = jnp.dot(rows_ref[...], weight_ref[...], preferred_element_type=F32)
    upstream = upstream_ref[...]
    normal_cdf = 0.5 * (1.0 + lax.erf(preact * SQRT_HALF))
    normal_pdf = INV_ROOT_TWO_PI * jnp.exp(-0.5 * preact * preact)
    hidden = preact * normal_cdf
    scale = gate[...]
    term = jnp.sum(hidden * upstream, axis=1, keepdims=True)
    hidden_grad = (scale * upstream * (normal_cdf + preact * normal_pdf)).astype(BF)
    grad_ref[...] = hidden_grad
    gated_ref[...] = (scale * hidden).astype(BF)
    part = lax.dot_general(hidden_grad, weight_ref[...], COLS, preferred_element_type=F32)

    @pl.when(step == 0)
    def _():
        total[...] = part
        terms[...] = term

    @pl.when(step > 0)
    def _():
        total[...] += part
        terms[...] += term

    @pl.when(step == pl.num_programs(0) - 1)
    def _():
        for m in range(chunks):
            at = slice(m * rows, (m + 1) * rows)
            outs[m][:, :width] = total[at, :].astype(BF)
            exact = terms[at, :]
            high = exact.astype(BF).astype(F32)
            tail = jnp.where(lane == my_ref[0], high, 0.0)
            tail = jnp.where(lane == my_ref[0] + HALF, exact - high, tail)
            outs[m][:, width:] = tail.astype(BF)


def combine_kernel(pieces, chunks, pick_ref, *refs):
    ins, outs = refs[:chunks], refs[chunks:]
    stacked = jnp.concatenate([r[...] for r in ins], axis=0)
    back = lax.dot_general(pick_ref[...], stacked, ROWS_T, preferred_element_type=F32).astype(BF)
    count = back.shape[0] // pieces
    for k in range(pieces):
        outs[k][...] = back[k * count : (k + 1) * count, :]


def back_kernel(pieces, embed_ref, score_ref, gain_ref, router_ref, routes_ref, tok_ref, keep_ref, cot_ref, *refs):
    parts, out_ref = refs[:pieces], refs[pieces]
    count, width = tok_ref.shape
    experts = router_ref.shape[0]
    values = quartet_values(embed_ref[...], count)
    kept = keep_ref[...]
    column = [kept[:, i : i + 1] for i in range(21)]
    coefs = column[:4]
    shares = [column[4 + 3 * q : 7 + 3 * q] for q in range(4)]
    scale, gates, others = column[16], column[17:19], column[19:21]
    summed = parts[0][...].astype(F32)
    for part in parts[1:]:
        summed = summed + part[...].astype(F32)
    routes_t = routes_ref[...]
    masks = [route_mask(routes_t, k, True) for k in range(2)]
    tail = summed[:, width:]
    gate_grad = [jnp.sum(m * tail, axis=1, keepdims=True) for m in masks]
    pull = gates[0] * gates[1] * (gate_grad[0] - gate_grad[1])
    logit_grad = pull * (masks[0] * others[0] - masks[1] * others[1])
    normed_grad = summed[:, :width] + jnp.dot(
        logit_grad[:, :experts], router_ref[...].astype(F32), precision=HIGHEST, preferred_element_type=F32
    )
    tokens = tok_ref[...]
    scaled = gain_ref[...] * normed_grad
    inner = jnp.mean(tokens * scaled, axis=1, keepdims=True)
    token_grad = cot_ref[...].astype(F32) + scale * scaled - tokens * (scale * scale * scale * inner)
    dots = [jnp.sum(token_grad * v, axis=1, keepdims=True) for v in values]
    pairs = [dots[0] + dots[1], dots[2] + dots[3]]
    four = 0.0625 * (pairs[0] + pairs[1])
    score_grads = []
    for q in range(4):
        share = shares[q]
        grads = (0.25 * dots[q], 0.125 * pairs[q // 2], four)
        average = share[0] * grads[0] + share[1] * grads[1] + share[2] * grads[2]
        score_grads.append([s * (g - average) for s, g in zip(share, grads)])
    all_four = 0.25 * (score_grads[0][2] + score_grads[1][2] + score_grads[2][2] + score_grads[3][2])
    weight = score_ref[...]
    ordered = []
    for q in range(4):
        pair = 0.5 * (score_grads[q][1] + score_grads[q ^ 1][1])
        slope = score_grads[q][0] + pair + all_four
        ordered.append((coefs[q] * token_grad + slope * weight).astype(BF))
    out_ref[...] = lax.dot_general(
        quartet_order(count), jnp.concatenate(ordered, axis=0), ROWS_T, preferred_element_type=F32
    ).astype(BF)


def per_device(byte_embed, score_weight, norm_gain, router, routes, expert_in, expert_out, cotangent):
    experts = router.shape[1]
    count = routes.shape[1]
    width = byte_embed.shape[2]
    full = width + LANES
    capacity = max(2, 3 * count // experts)
    pieces = lax.axis_size("seq")
    chunks = lax.axis_size("exp")
    rows = pieces * capacity
    slots = chunks * rows
    tokens = pieces * count
    hidden = expert_in.shape[2]
    tile = min(256, hidden)
    steps = hidden // tile
    my = lax.axis_index("exp").astype(jnp.int32).reshape(1)
    embed = byte_embed[0]
    cot = cotangent[0]
    score_row = score_weight.reshape(1, width)
    gain_row = norm_gain.reshape(1, width)
    router_t = router.T
    routes_t = routes[0].T
    weight_in = expert_in[0]
    weight_out = expert_out[0]
    smem = pl.BlockSpec(memory_space=pltpu.SMEM)
    vmem = pl.BlockSpec()

    def shape(*dims, dtype=BF):
        return jax.ShapeDtypeStruct(dims, dtype)

    def over_seq(values, sign):
        moved = [values[0]]
        for k in range(1, pieces):
            pairs = [(i, (i + sign * k) % pieces) for i in range(pieces)]
            moved.append(lax.ppermute(values[k], "seq", pairs))
        return moved

    def over_exp(values):
        moved = [values[0]]
        for m in range(1, chunks):
            moved.append(lax.ppermute(values[m], "exp", [(i, i ^ m) for i in range(chunks)]))
        return moved

    cot_pay = call(cot_payload_kernel, "cot_payload", shape(count, full), (cot, routes_t))
    cot_all = over_seq([cot_pay] * pieces, 1)
    pay, tok, keep = call(
        front_kernel,
        "front",
        (shape(count, full), shape(count, width, dtype=F32), shape(count, LANES, dtype=F32)),
        (embed, score_row, gain_row, router_t, routes_t),
        scratch=[pltpu.VMEM((count, LANES), F32)],
    )
    pay_all = over_seq([pay] * pieces, 1)
    *cot_chunks, pick = call(
        functools.partial(cot_pick_kernel, pieces, chunks, rows, capacity),
        "cot_pick",
        [shape(rows, width)] * chunks + [shape(slots, tokens)],
        (my, *cot_all),
        in_specs=[smem] + [vmem] * pieces,
    )
    cot_rows = over_exp(cot_chunks)
    pay_chunks = call(
        functools.partial(token_pick_kernel, pieces, chunks, rows),
        "token_pick",
        [shape(rows, full)] * chunks,
        (pick, *pay_all),
    )
    pay_rows = over_exp(pay_chunks)

    def fixed(*dims):
        return pl.BlockSpec(dims, lambda i: (0, 0))

    upstream, cot_slots = call(
        functools.partial(upstream_kernel, chunks, rows),
        "upstream",
        (shape(slots, hidden, dtype=F32), shape(slots, width)),
        (*cot_rows, weight_out),
        grid=(steps,),
        in_specs=[fixed(rows, width)] * chunks + [pl.BlockSpec((tile, width), lambda i: (i, 0))],
        out_specs=(pl.BlockSpec((slots, tile), lambda i: (0, i)), fixed(slots, width)),
    )
    *back_chunks, token_slots, gated_hidden, hidden_grad = call(
        functools.partial(expert_kernel, chunks, rows),
        "expert",
        [shape(rows, full)] * chunks + [shape(slots, width), shape(slots, hidden), shape(slots, hidden)],
        (my, *pay_rows, upstream, weight_in),
        scratch=[pltpu.VMEM((slots, width), F32), pltpu.VMEM((slots, 1), F32), pltpu.VMEM((slots, 1), F32)],
        grid=(steps,),
        in_specs=[smem]
        + [fixed(rows, full)] * chunks
        + [pl.BlockSpec((slots, tile), lambda i: (0, i)), pl.BlockSpec((width, tile), lambda i: (0, i))],
        out_specs=[fixed(rows, full)] * chunks
        + [fixed(slots, width)]
        + [pl.BlockSpec((slots, tile), lambda i: (0, i))] * 2,
    )
    returned = over_exp(back_chunks)
    grad_out = lax.dot_general(gated_hidden, cot_slots, ROWS_T, preferred_element_type=F32)
    grad_in = lax.dot_general(token_slots, hidden_grad, ROWS_T, preferred_element_type=F32)
    partial_rows = call(
        functools.partial(combine_kernel, pieces, chunks),
        "combine",
        [shape(count, full)] * pieces,
        (pick, *returned),
    )
    parts = over_seq(partial_rows, -1)
    embed_grad = call(
        functools.partial(back_kernel, pieces),
        "back",
        shape(4 * count, width),
        (embed, score_row, gain_row, router_t, routes_t, tok, keep, cot, *parts),
    )
    return (embed_grad[None], grad_in[None], grad_out[None])


def solution(mesh):
    in_specs = (
        P("exp", "seq", None),
        P(),
        P(),
        P(),
        P("exp", "seq", None),
        P("exp", None, "seq"),
        P("exp", "seq", None),
        P("exp", "seq", None),
    )
    out_specs = (P("exp", "seq", None), P("exp", None, "seq"), P("exp", "seq", None))
    return jax.shard_map(
        per_device, mesh=mesh, in_specs=in_specs, out_specs=out_specs, check_vma=False
    )
```

```python
import functools
import jax
import jax.numpy as jnp
from jax import lax
from jax.experimental import pallas as pl
from jax.experimental.pallas import tpu as pltpu
from jax.sharding import PartitionSpec as P

SQRT_HALF = 0.7071067811865476
INV_ROOT_TWO_PI = 0.3989422804014327
LANES = 128
HALF = LANES // 2
BF = jnp.bfloat16
F32 = jnp.float32
HIGHEST = lax.Precision.HIGHEST
ROWS_T = (((0,), (0,)), ((), ()))
COLS = (((1,), (1,)), ((), ()))
MIB = 1024 * 1024
BYTES_PER_US = 0


def call(body, name, outs, args, us, scratch=(), limit=8, scalars=0, held=True):
    vmem = pl.BlockSpec(memory_space=pltpu.VMEM)
    smem = pl.BlockSpec(memory_space=pltpu.SMEM)
    rest = vmem if held else pl.BlockSpec(memory_space=pltpu.HBM)
    return pl.pallas_call(
        body,
        name=name,
        out_shape=outs,
        in_specs=[smem] * scalars + [rest] * (len(args) - scalars),
        out_specs=jax.tree.map(lambda _: vmem, outs),
        scratch_shapes=list(scratch),
        compiler_params=pltpu.CompilerParams(vmem_limit_bytes=limit * MIB),
        cost_estimate=pl.CostEstimate(flops=0, bytes_accessed=int(us * BYTES_PER_US), transcendentals=0),
    )(*args)


def route_mask(routes_t, k, wrap):
    count = routes_t.shape[1]
    lane = lax.broadcasted_iota(jnp.int32, (LANES, count), 0)
    if wrap:
        lane = lane & (HALF - 1)
    mask_t = (lane == routes_t[k : k + 1, :]).astype(F32).astype(BF)
    row = lax.broadcasted_iota(jnp.int32, (count, count), 0)
    col = lax.broadcasted_iota(jnp.int32, (count, count), 1)
    eye = (row == col).astype(F32).astype(BF)
    return lax.dot_general(eye, mask_t, COLS, preferred_element_type=F32)


def quartet_order(count):
    row = lax.broadcasted_iota(jnp.int32, (4 * count, 4 * count), 0)
    col = lax.broadcasted_iota(jnp.int32, (4 * count, 4 * count), 1)
    return (4 * (row % count) + row // count == col).astype(F32).astype(BF)


def quartet_values(embed, count):
    ordered = jnp.dot(quartet_order(count), embed, preferred_element_type=F32)
    return [ordered[q * count : (q + 1) * count, :] for q in range(4)]


def quartet_scores(values, weight):
    ones = [jnp.sum(v * weight, axis=1, keepdims=True) for v in values]
    pairs = [0.5 * (ones[0] + ones[1]), 0.5 * (ones[2] + ones[3])]
    four = 0.5 * (pairs[0] + pairs[1])
    shares = []
    for q in range(4):
        scores = (ones[q], pairs[q // 2], four)
        largest = jnp.maximum(jnp.maximum(scores[0], scores[1]), scores[2])
        weights = [jnp.exp(s - largest) for s in scores]
        denominator = weights[0] + weights[1] + weights[2]
        shares.append([w / denominator for w in weights])
    return shares


def front_kernel(*refs):
    far, outs, near, logit, arrived = refs[:6], refs[6:10], refs[10:16], refs[16], refs[17]
    copies = [pltpu.make_async_copy(a, b, arrived.at[i]) for i, (a, b) in enumerate(zip(far, near))]
    for copy in copies:
        copy.start()
    embed_ref, score_ref, gain_ref, router_ref, routes_ref, cot_ref = near
    both_ref, pay_ref, tok_ref, keep_ref = outs
    for copy in copies:
        copy.wait()
    count, width = tok_ref.shape
    experts = router_ref.shape[0]
    values = quartet_values(embed_ref[...], count)
    shares = quartet_scores(values, score_ref[...])
    whole = 0.25 * (shares[0][2] + shares[1][2] + shares[2][2] + shares[3][2])
    coefs = []
    for q in range(4):
        pair = 0.5 * (shares[q][1] + shares[q ^ 1][1])
        coefs.append(0.25 * (shares[q][0] + pair + whole))
    tokens = coefs[0] * values[0] + coefs[1] * values[1] + coefs[2] * values[2] + coefs[3] * values[3]
    tok_ref[...] = tokens
    scale = lax.rsqrt(jnp.mean(tokens * tokens, axis=1, keepdims=True) + 1e-06)
    normed = tokens * scale * gain_ref[...]
    logit[...] = jnp.zeros_like(logit)
    logit[:, :experts] = lax.dot_general(
        normed, router_ref[...].astype(F32), COLS, precision=HIGHEST, preferred_element_type=F32
    )
    logits = logit[...]
    sigmoid = 1.0 / (1.0 + jnp.exp(-logits))
    rest = 1.0 / (1.0 + jnp.exp(logits))
    routes_t = routes_ref[...]
    masks = [route_mask(routes_t, k, False) for k in range(2)]
    picked = [jnp.sum(m * sigmoid, axis=1, keepdims=True) for m in masks]
    others = [jnp.sum(m * rest, axis=1, keepdims=True) for m in masks]
    total = picked[0] + picked[1]
    gates = [p / total for p in picked]
    named = masks[0] + masks[1]
    wide_masks = [route_mask(routes_t, k, True) for k in range(2)]
    gated = wide_masks[0] * gates[0] + wide_masks[1] * gates[1]
    first_half = lax.broadcasted_iota(jnp.int32, named.shape, 1) < HALF
    pay_ref[:, :width] = normed.astype(BF)
    pay_ref[:, width:] = jnp.where(first_half, named, gated).astype(BF)
    both_ref[:, :width] = cot_ref[...]
    both_ref[:, width:] = pay_ref[...]
    lane = lax.broadcasted_iota(jnp.int32, keep_ref.shape, 1)
    columns = coefs + [s for share in shares for s in share] + [scale] + gates + others
    kept = jnp.zeros(keep_ref.shape, F32)
    for i, column in enumerate(columns):
        kept = jnp.where(lane == i, column, kept)
    keep_ref[...] = kept


def gather_kernel(*refs):
    ins, out_ref = refs[:-1], refs[-1]
    at = 0
    for r in ins:
        out_ref[at : at + r.shape[0], :] = r[...]
        at += r.shape[0]


def slot_places(tail, chunks, capacity, count, blocks, halves, my):
    tokens = tail.shape[0]
    lane_row = lax.broadcasted_iota(jnp.int32, (LANES, LANES), 0)
    lane_col = lax.broadcasted_iota(jnp.int32, (LANES, LANES), 1)
    named_lane = (2 * lane_col) ^ my
    live = lane_col < chunks
    order = ((lane_row == named_lane) & live).astype(F32).astype(BF)
    gate_order = ((lane_row == named_lane + HALF) & live).astype(F32).astype(BF)
    named = jnp.dot(tail, order, preferred_element_type=F32).astype(BF)
    gates = jnp.dot(tail, gate_order, preferred_element_type=F32).astype(BF)
    row = lax.broadcasted_iota(jnp.int32, (tokens, tokens), 0)
    col = lax.broadcasted_iota(jnp.int32, (tokens, tokens), 1)
    eye = (row == col).astype(F32).astype(BF)
    before = ((row < col) & (row // count == col // count)).astype(F32).astype(BF)
    named_t = lax.dot_general(named, eye, ROWS_T, preferred_element_type=F32)
    gates_t = lax.dot_general(gates, eye, ROWS_T, preferred_element_type=F32)
    place_t = lax.dot_general(named, before, ROWS_T, preferred_element_type=F32)
    block = lax.broadcasted_iota(jnp.int32, (LANES, tokens), 1) // count
    share = blocks // halves
    doc, block = block // blocks, block % blocks
    base = ((block // share * 2 + doc) * share + block % share) * capacity
    return jnp.where(named_t > 0.5, place_t + base.astype(F32), -1.0), gates_t


def near_gather_kernel(*refs):
    ins, out_ref = refs[:-1], refs[-1]
    count = ins[0].shape[0]
    full = out_ref.shape[1]
    width = full - LANES
    shared = len(ins) // 2
    for i, r in enumerate(ins[:shared]):
        cot_at = slice(i * count, (i + 1) * count)
        token_at = slice((shared + i) * count, (shared + i + 1) * count)
        out_ref[cot_at, :width] = r[:, :width]
        out_ref[cot_at, width:] = r[:, 2 * width :]
        out_ref[token_at, :] = r[:, width:]
    for i, r in enumerate(ins[shared:]):
        at = (2 * shared + i) * count
        out_ref[at : at + count, :] = r[...]


def pick_kernel(blocks, chunks, rows, capacity, my_ref, own_ref, other_ref, *refs):
    cot_outs, outs, pick_ref = refs[:chunks], refs[chunks : 2 * chunks], refs[2 * chunks]
    width = outs[0].shape[1]
    count = own_ref.shape[0] // (blocks + blocks // 2)
    cots = blocks // 2 * count
    half = rows // 2
    for first, last, held, halves in ((0, cots, half, 1), (cots, own_ref.shape[0], rows, 2)):
        stacked = jnp.concatenate([own_ref[first:last, :], other_ref[first:last, :]], axis=0)
        share = blocks // (3 - halves)
        places, gates = slot_places(stacked[:, width:], chunks, capacity, count, share, halves, my_ref[0])
        slot = lax.broadcasted_iota(jnp.int32, (held, stacked.shape[0]), 0).astype(F32)
        picks = []
        for m in range(chunks):
            value = gates[m : m + 1, :] if halves == 1 else jnp.ones_like(gates[m : m + 1, :])
            picks.append(jnp.where(places[m : m + 1, :] == slot, value, 0.0).astype(BF))
        picks = jnp.concatenate(picks, axis=0)
        chosen = jnp.dot(picks, stacked[:, :width], preferred_element_type=F32).astype(BF)
        for m in range(chunks):
            (cot_outs if halves == 1 else outs)[m][...] = chosen[m * held : (m + 1) * held, :]
    pick_ref[...] = picks


def upstream_kernel(rows_ref, weight_ref, out_ref):
    out_ref[...] = lax.dot_general(rows_ref[...], weight_ref[...], COLS, preferred_element_type=F32)


def expert_kernel(chunks, rows, tile, my_ref, *refs):
    ins = refs[:chunks]
    upstream_refs, weight_ref = refs[chunks : chunks + 2], refs[chunks + 2]
    outs = refs[chunks + 3 : 2 * chunks + 3]
    rows_ref, hidden_ref, grad_ref = refs[2 * chunks + 3 :]
    slots, width = rows_ref.shape
    half = rows // 2
    for m in range(chunks):
        rows_ref[m * rows : (m + 1) * rows, :] = ins[m][...]
    token_rows = rows_ref[...]
    terms = jnp.zeros((slots, LANES), F32)
    for f in range(weight_ref.shape[1] // tile):
        part = slice(f * tile, (f + 1) * tile)
        preact = jnp.dot(token_rows, weight_ref[:, part], preferred_element_type=F32)
        upstream = jnp.concatenate(
            [r[m * half : (m + 1) * half, part] for m in range(chunks) for r in upstream_refs], axis=0
        )
        normal_cdf = 0.5 * (1.0 + lax.erf(preact * SQRT_HALF))
        normal_pdf = INV_ROOT_TWO_PI * jnp.exp(-0.5 * preact * preact)
        hidden = preact * normal_cdf
        products = hidden * upstream
        for k in range(tile // LANES):
            terms = terms + products[:, k * LANES : (k + 1) * LANES]
        grad_ref[:, part] = (upstream * (normal_cdf + preact * normal_pdf)).astype(BF)
        hidden_ref[:, part] = hidden.astype(BF)
    back = lax.dot_general(grad_ref[...], weight_ref[...], COLS, preferred_element_type=F32).astype(BF)
    exact = jnp.sum(terms, axis=1, keepdims=True)
    high = exact.astype(BF).astype(F32)
    lane = lax.broadcasted_iota(jnp.int32, (slots, LANES), 1)
    tail = jnp.where(lane == my_ref[0], high, 0.0)
    tail = jnp.where(lane == my_ref[0] + HALF, exact - high, tail).astype(BF)
    for m in range(chunks):
        outs[m][:, :width] = back[m * rows : (m + 1) * rows, :]
        outs[m][:, width:] = tail[m * rows : (m + 1) * rows, :]


def cot_order_kernel(chunks, cot_a_ref, cot_b_ref, out_ref):
    half = cot_a_ref.shape[0] // chunks
    for m in range(chunks):
        for i, r in enumerate((cot_a_ref, cot_b_ref)):
            at = (2 * m + i) * half
            out_ref[at : at + half, :] = r[m * half : (m + 1) * half, :]


def combine_other_kernel(chunks, rows, pick_ref, *refs):
    ins, out_ref = refs[:chunks], refs[chunks]
    tokens = out_ref.shape[0]
    stacked = jnp.concatenate([r[...] for r in ins], axis=0)
    out_ref[...] = lax.dot_general(
        pick_ref[:, tokens:], stacked, ROWS_T, preferred_element_type=F32
    ).astype(BF)


def combine_own_kernel(pieces, chunks, pick_ref, *refs):
    ins, other_ref, outs = refs[:chunks], refs[chunks], refs[chunks + 1 :]
    tokens = other_ref.shape[0]
    count = tokens // pieces
    stacked = jnp.concatenate([r[...] for r in ins], axis=0)
    back = lax.dot_general(pick_ref[:, :tokens], stacked, ROWS_T, preferred_element_type=F32)
    back = (back + other_ref[...].astype(F32)).astype(BF)
    for k in range(pieces):
        outs[k][...] = back[k * count : (k + 1) * count, :]


def back_kernel(pieces, embed_ref, score_ref, gain_ref, router_ref, routes_ref, tok_ref, keep_ref, cot_ref, *refs):
    parts, out_ref = refs[:pieces], refs[pieces]
    count, width = tok_ref.shape
    experts = router_ref.shape[0]
    values = quartet_values(embed_ref[...], count)
    kept = keep_ref[...]
    column = [kept[:, i : i + 1] for i in range(21)]
    coefs = column[:4]
    shares = [column[4 + 3 * q : 7 + 3 * q] for q in range(4)]
    scale, gates, others = column[16], column[17:19], column[19:21]
    summed = parts[0][...].astype(F32)
    for part in parts[1:]:
        summed = summed + part[...].astype(F32)
    routes_t = routes_ref[...]
    masks = [route_mask(routes_t, k, True) for k in range(2)]
    tail = summed[:, width:]
    gate_grad = [jnp.sum(m * tail, axis=1, keepdims=True) for m in masks]
    pull = gate_grad[0] * gates[1] - gate_grad[1] * gates[0]
    logit_grad = pull * (masks[0] * others[0] - masks[1] * others[1])
    normed_grad = summed[:, :width] + jnp.dot(
        logit_grad[:, :experts], router_ref[...].astype(F32), precision=HIGHEST, preferred_element_type=F32
    )
    tokens = tok_ref[...]
    scaled = gain_ref[...] * normed_grad
    inner = jnp.mean(tokens * scaled, axis=1, keepdims=True)
    token_grad = cot_ref[...].astype(F32) + scale * scaled - tokens * (scale * scale * scale * inner)
    dots = [jnp.sum(token_grad * v, axis=1, keepdims=True) for v in values]
    pairs = [dots[0] + dots[1], dots[2] + dots[3]]
    four = 0.0625 * (pairs[0] + pairs[1])
    score_grads = []
    for q in range(4):
        share = shares[q]
        grads = (0.25 * dots[q], 0.125 * pairs[q // 2], four)
        average = share[0] * grads[0] + share[1] * grads[1] + share[2] * grads[2]
        score_grads.append([s * (g - average) for s, g in zip(share, grads)])
    all_four = 0.25 * (score_grads[0][2] + score_grads[1][2] + score_grads[2][2] + score_grads[3][2])
    weight = score_ref[...]
    ordered = []
    for q in range(4):
        pair = 0.5 * (score_grads[q][1] + score_grads[q ^ 1][1])
        slope = score_grads[q][0] + pair + all_four
        ordered.append((coefs[q] * token_grad + slope * weight).astype(BF))
    out_ref[...] = lax.dot_general(
        quartet_order(count), jnp.concatenate(ordered, axis=0), ROWS_T, preferred_element_type=F32
    ).astype(BF)


def per_device(byte_embed, score_weight, norm_gain, router, routes, expert_in, expert_out, cotangent):
    experts = router.shape[1]
    count = routes.shape[1]
    width = byte_embed.shape[2]
    full = width + LANES
    capacity = max(2, 3 * count // experts)
    pieces = lax.axis_size("seq")
    owners = lax.axis_size("exp")
    chunks = owners // 2
    rows = 2 * pieces * capacity
    slots = chunks * rows
    tokens = pieces * count
    hidden = expert_in.shape[2]
    tile = min(256, hidden)
    my = lax.axis_index("exp").astype(jnp.int32).reshape(1)
    embed = byte_embed[0]
    cot = cotangent[0]
    score_row = score_weight.reshape(1, width)
    gain_row = norm_gain.reshape(1, width)
    router_t = router.T
    routes_t = routes[0].T
    weight_in = expert_in[0]
    weight_out = expert_out[0]

    def shape(*dims, dtype=BF):
        return jax.ShapeDtypeStruct(dims, dtype)

    def over_seq(value, k):
        return lax.ppermute(value, "seq", [(i, i ^ k) for i in range(pieces)])

    def over_cores(value):
        return lax.ppermute(value, "exp", [(i, i ^ 1) for i in range(owners)])

    def over_chips(values):
        moved = [values[0]]
        for m in range(1, chunks):
            moved.append(lax.ppermute(values[m], "exp", [(i, i ^ (2 * m)) for i in range(owners)]))
        return moved

    half = pieces // 2
    places = list(range(0, pieces, 2)) + list(range(1, pieces, 2))
    front_args = (embed, score_row, gain_row, router_t, routes_t, cot)
    both, pay, tok, keep = call(
        front_kernel,
        "front",
        (
            shape(count, full + width),
            shape(count, full),
            shape(count, width, dtype=F32),
            shape(count, LANES, dtype=F32),
        ),
        front_args,
        2.0,
        scratch=[pltpu.VMEM(a.shape, a.dtype) for a in front_args]
        + [pltpu.VMEM((count, LANES), F32), pltpu.SemaphoreType.DMA((len(front_args),))],
        limit=56,
        held=False,
    )
    near = [both] + [over_seq(both, k) for k in places[1:half]] + [over_seq(pay, k) for k in places[half:]]
    own = call(near_gather_kernel, "near_gather", shape(half * count + tokens, full), near, 0.3)
    *chosen, pick = call(
        functools.partial(pick_kernel, pieces, chunks, rows, capacity),
        "pick",
        [shape(rows // 2, width)] * chunks + [shape(rows, width)] * chunks + [shape(slots, 2 * tokens)],
        (my, own, over_cores(own)),
        1.0,
        scalars=1,
        limit=16,
    )
    cot_a = call(gather_kernel, "cot_slots", shape(slots // 2, width), over_chips(chosen[:chunks]), 0.3)
    cot_b = over_seq(cot_a, 1)
    pay_rows = over_chips(chosen[chunks:])

    upstream_a, upstream_b = [
        call(upstream_kernel, "upstream", shape(slots // 2, hidden, dtype=F32), (c, weight_out), 1.5, limit=16)
        for c in (cot_a, cot_b)
    ]
    *back_chunks, token_slots, hidden_rows, hidden_grad = call(
        functools.partial(expert_kernel, chunks, rows, tile),
        "expert",
        [shape(rows, full)] * chunks + [shape(slots, width), shape(slots, hidden), shape(slots, hidden)],
        (my, *pay_rows, upstream_a, upstream_b, weight_in),
        4.0,
        scalars=1,
        limit=24,
    )
    cot_slots = call(
        functools.partial(cot_order_kernel, chunks), "cot_order", shape(slots, width), (cot_a, cot_b), 0.5
    )
    grad_out = lax.dot_general(hidden_rows, cot_slots, ROWS_T, preferred_element_type=F32)
    grad_in = lax.dot_general(token_slots, hidden_grad, ROWS_T, preferred_element_type=F32)
    *returned, grad_out = lax.optimization_barrier((*over_chips(back_chunks), grad_out))
    other_rows = over_cores(
        call(
            functools.partial(combine_other_kernel, chunks, rows),
            "combine_other",
            shape(tokens, full),
            (pick, *returned),
            1.0,
            limit=16,
        )
    )
    partial_rows = call(
        functools.partial(combine_own_kernel, pieces, chunks),
        "combine_own",
        [shape(count, full)] * pieces,
        (pick, *returned, other_rows),
        1.0,
        limit=16,
    )
    parts = list(partial_rows[:1]) + [over_seq(v, k) for v, k in zip(partial_rows[1:], places[1:])]
    embed_grad = call(
        functools.partial(back_kernel, pieces),
        "back",
        shape(4 * count, width),
        (embed, score_row, gain_row, router_t, routes_t, tok, keep, cot, *parts),
        2.0,
    )
    return (embed_grad[None], grad_in[None], grad_out[None])


def solution(mesh):
    in_specs = (
        P("exp", "seq", None),
        P(),
        P(),
        P(),
        P("exp", "seq", None),
        P("exp", None, "seq"),
        P("exp", "seq", None),
        P("exp", "seq", None),
    )
    out_specs = (P("exp", "seq", None), P("exp", None, "seq"), P("exp", "seq", None))
    return jax.shard_map(
        per_device, mesh=mesh, in_specs=in_specs, out_specs=out_specs, check_vma=False
    )
```

```python
import functools
import jax
import jax.numpy as jnp
from jax import lax
from jax.experimental import pallas as pl
from jax.experimental.pallas import tpu as pltpu
from jax.sharding import PartitionSpec as P

SQRT_HALF = 0.7071067811865476
INV_ROOT_TWO_PI = 0.3989422804014327
LANES = 128
GROUP = LANES // 4
BF = jnp.bfloat16
F32 = jnp.float32
HIGHEST = lax.Precision.HIGHEST
ROWS_T = (((0,), (0,)), ((), ()))
COLS = (((1,), (1,)), ((), ()))
MIB = 1024 * 1024
BYTES_PER_US = 3_000_000


def call(body, name, outs, args, us=0.0, scratch=(), limit=8, scalars=0, held=True):
    vmem = pl.BlockSpec(memory_space=pltpu.VMEM)
    smem = pl.BlockSpec(memory_space=pltpu.SMEM)
    rest = vmem if held else pl.BlockSpec(memory_space=pltpu.HBM)
    return pl.pallas_call(
        body,
        name=name,
        out_shape=outs,
        in_specs=[smem] * scalars + [rest] * (len(args) - scalars),
        out_specs=jax.tree.map(lambda _: vmem, outs),
        scratch_shapes=list(scratch),
        compiler_params=pltpu.CompilerParams(vmem_limit_bytes=limit * MIB),
        cost_estimate=pl.CostEstimate(flops=0, bytes_accessed=int(us * BYTES_PER_US), transcendentals=0),
    )(*args)


def route_mask(routes_t, k):
    count = routes_t.shape[1]
    lane = lax.broadcasted_iota(jnp.int32, (LANES, count), 0) % GROUP
    mask_t = (lane == routes_t[k : k + 1, :]).astype(F32).astype(BF)
    row = lax.broadcasted_iota(jnp.int32, (count, count), 0)
    col = lax.broadcasted_iota(jnp.int32, (count, count), 1)
    eye = (row == col).astype(F32).astype(BF)
    return lax.dot_general(eye, mask_t, COLS, preferred_element_type=F32)


def quartet_order(count):
    row = lax.broadcasted_iota(jnp.int32, (4 * count, 4 * count), 0)
    col = lax.broadcasted_iota(jnp.int32, (4 * count, 4 * count), 1)
    return (4 * (row % count) + row // count == col).astype(F32).astype(BF)


def quartet_values(embed, count):
    ordered = jnp.dot(quartet_order(count), embed, preferred_element_type=F32)
    return [ordered[q * count : (q + 1) * count, :] for q in range(4)]


def quartet_scores(values, weight):
    ones = [jnp.sum(v * weight, axis=1, keepdims=True) for v in values]
    pairs = [0.5 * (ones[0] + ones[1]), 0.5 * (ones[2] + ones[3])]
    four = 0.5 * (pairs[0] + pairs[1])
    shares = []
    for q in range(4):
        scores = (ones[q], pairs[q // 2], four)
        largest = jnp.maximum(jnp.maximum(scores[0], scores[1]), scores[2])
        weights = [jnp.exp(s - largest) for s in scores]
        denominator = weights[0] + weights[1] + weights[2]
        shares.append([w / denominator for w in weights])
    return shares


def front_kernel(*refs):
    far, outs, near, logit, arrived = refs[:5], refs[5:8], refs[8:13], refs[13], refs[14]
    copies = [pltpu.make_async_copy(a, b, arrived.at[i]) for i, (a, b) in enumerate(zip(far, near))]
    for copy in copies:
        copy.start()
    embed_ref, score_ref, gain_ref, router_ref, routes_ref = near
    pay_ref, tok_ref, keep_ref = outs
    for copy in copies:
        copy.wait()
    count, width = tok_ref.shape
    experts = router_ref.shape[0]
    values = quartet_values(embed_ref[...], count)
    shares = quartet_scores(values, score_ref[...])
    whole = 0.25 * (shares[0][2] + shares[1][2] + shares[2][2] + shares[3][2])
    coefs = []
    for q in range(4):
        pair = 0.5 * (shares[q][1] + shares[q ^ 1][1])
        coefs.append(0.25 * (shares[q][0] + pair + whole))
    tokens = coefs[0] * values[0] + coefs[1] * values[1] + coefs[2] * values[2] + coefs[3] * values[3]
    tok_ref[...] = tokens
    scale = lax.rsqrt(jnp.mean(tokens * tokens, axis=1, keepdims=True) + 1e-06)
    normed = tokens * scale * gain_ref[...]
    logit[...] = jnp.zeros_like(logit)
    logit[:, :experts] = lax.dot_general(
        normed, router_ref[...].astype(F32), COLS, precision=HIGHEST, preferred_element_type=F32
    )
    logits = logit[...]
    sigmoid = 1.0 / (1.0 + jnp.exp(-logits))
    rest = 1.0 / (1.0 + jnp.exp(logits))
    routes_t = routes_ref[...]
    masks = [route_mask(routes_t, k) for k in range(2)]
    group = lax.broadcasted_iota(jnp.int32, masks[0].shape, 1) // GROUP
    once = [jnp.where(group == 0, m, 0.0) for m in masks]
    picked = [jnp.sum(m * sigmoid, axis=1, keepdims=True) for m in once]
    others = [jnp.sum(m * rest, axis=1, keepdims=True) for m in once]
    total = picked[0] + picked[1]
    tail = jnp.zeros_like(masks[0])
    for mask, sig, other in zip(masks, picked, others):
        value = jnp.where(group == 0, 1.0, jnp.where(group == 1, other, jnp.where(group == 2, sig / total, 0.0)))
        tail = tail + mask * value
    pay_ref[:, :width] = normed.astype(BF)
    pay_ref[:, width:] = tail.astype(BF)
    lane = lax.broadcasted_iota(jnp.int32, keep_ref.shape, 1)
    columns = coefs + [s for share in shares for s in share] + [scale]
    kept = jnp.zeros(keep_ref.shape, F32)
    for i, column in enumerate(columns):
        kept = jnp.where(lane == i, column, kept)
    keep_ref[...] = kept


def gather_kernel(skipped, *refs):
    ins, out_ref = refs[skipped:-1], refs[-1]
    at = 0
    for r in ins:
        out_ref[at : at + r.shape[0], :] = r[...]
        at += r.shape[0]


def slot_places(tail, columns, step, count, capacity, my):
    tokens = tail.shape[0]
    lane_row = lax.broadcasted_iota(jnp.int32, (LANES, LANES), 0)
    lane_col = lax.broadcasted_iota(jnp.int32, (LANES, LANES), 1)
    lane = (step * (lane_col % GROUP)) ^ my
    lane = jnp.where(lane_col < GROUP, lane, lane + 2 * GROUP)
    live = (lane_col % GROUP < columns) & (lane_col < 2 * GROUP)
    order = ((lane_row == lane) & live).astype(F32).astype(BF)
    ordered = jnp.dot(tail, order, preferred_element_type=F32).astype(BF)
    row = lax.broadcasted_iota(jnp.int32, (tokens, tokens), 0)
    col = lax.broadcasted_iota(jnp.int32, (tokens, tokens), 1)
    eye = (row == col).astype(F32).astype(BF)
    before = ((row < col) & (row // count == col // count)).astype(F32).astype(BF)
    ordered_t = lax.dot_general(ordered, eye, ROWS_T, preferred_element_type=F32)
    place_t = lax.dot_general(ordered, before, ROWS_T, preferred_element_type=F32)[:GROUP, :]
    block = lax.broadcasted_iota(jnp.int32, (GROUP, tokens), 1) // count
    place_t = place_t + (block * capacity).astype(F32)
    return jnp.where(ordered_t[:GROUP, :] > 0.5, place_t, -1.0), ordered_t[GROUP : 2 * GROUP, :]


def selection(places, values, columns, rows):
    slot = lax.broadcasted_iota(jnp.int32, (rows, places.shape[1]), 0).astype(F32)
    picks = [jnp.where(places[m : m + 1, :] == slot, values[m : m + 1, :], 0.0) for m in range(columns)]
    return jnp.concatenate(picks, axis=0).astype(BF)


def pick_kernel(pieces, chunks, capacity, my_ref, cot_ref, token_ref, other_cot_ref, other_token_ref, *refs):
    cot_outs, outs = refs[:chunks], refs[chunks:]
    tokens, full = token_ref.shape
    width = full - LANES
    count = tokens // pieces
    cots = cot_ref.shape[0]
    near = pieces // 2
    my = my_ref[0]

    tail = jnp.concatenate([token_ref[:cots, width:], other_token_ref[:cots, width:]], axis=0)
    places, gates = slot_places(tail, chunks, 2, count, capacity, my)
    picks = selection(places, gates, chunks, 2 * near * capacity)
    cot_rows = jnp.concatenate([cot_ref[...], other_cot_ref[...]], axis=0)
    chosen = jnp.dot(picks, cot_rows, preferred_element_type=F32).astype(BF)
    for m, out in enumerate(cot_outs):
        out[...] = chosen[m * out.shape[0] : (m + 1) * out.shape[0], :]

    token_rows = jnp.concatenate([token_ref[...], other_token_ref[...]], axis=0)
    places, gates = slot_places(token_rows[:, width:], chunks, 2, count, capacity, my)
    picks = selection(places, jnp.ones_like(gates), chunks, 2 * pieces * capacity)
    chosen = jnp.dot(picks, token_rows, preferred_element_type=F32).astype(BF)
    for m, out in enumerate(outs):
        out[...] = chosen[m * out.shape[0] : (m + 1) * out.shape[0], :]


def back_pick_kernel(owners, count, capacity, my_ref, token_ref, out_ref):
    tail = token_ref[:, token_ref.shape[1] - LANES :]
    places, gates = slot_places(tail, owners, 1, count, capacity, my_ref[0])
    out_ref[...] = selection(places, jnp.ones_like(gates), owners, out_ref.shape[0] // owners)


def interleave(near, far, owners):
    share = near.shape[0] // owners
    return jnp.concatenate([r[d * share : (d + 1) * share, :] for d in range(owners) for r in (near, far)], axis=0)


def upstream_kernel(owners, near_ref, far_ref, weight_ref, out_ref):
    rows = jnp.concatenate([near_ref[...], far_ref[...]], axis=0)
    upstream = lax.dot_general(rows, weight_ref[...], COLS, preferred_element_type=F32)
    half = near_ref.shape[0]
    out_ref[...] = interleave(upstream[:half, :], upstream[half:, :], owners)


def expert_kernel(chunks, owners, tile, waits, my_ref, *refs):
    refs = refs[waits:]
    ins, refs = refs[:chunks], refs[chunks:]
    upstream_ref, weight_ref, router_ref = refs[:3]
    outs, (rows_ref, hidden_ref, grad_ref) = refs[3 : 3 + owners], refs[3 + owners :]
    slots, width = rows_ref.shape
    experts = router_ref.shape[0]
    rows = slots // owners
    token_rows = jnp.concatenate([r[:, :width] for r in ins], axis=0)
    rows_ref[...] = token_rows
    terms = jnp.zeros((slots, LANES), F32)
    for f in range(weight_ref.shape[1] // tile):
        part = slice(f * tile, (f + 1) * tile)
        preact = jnp.dot(token_rows, weight_ref[:, part], preferred_element_type=F32)
        upstream = upstream_ref[:, part]
        normal_cdf = 0.5 * (1.0 + lax.erf(preact * SQRT_HALF))
        normal_pdf = INV_ROOT_TWO_PI * jnp.exp(-0.5 * preact * preact)
        hidden = preact * normal_cdf
        products = hidden * upstream
        for k in range(tile // LANES):
            terms = terms + products[:, k * LANES : (k + 1) * LANES]
        grad_ref[:, part] = (upstream * (normal_cdf + preact * normal_pdf)).astype(BF)
        hidden_ref[:, part] = hidden.astype(BF)
    term = jnp.sum(terms, axis=1, keepdims=True)
    tail = jnp.concatenate([r[:, width:] for r in ins], axis=0).astype(F32)
    lane = lax.broadcasted_iota(jnp.int32, (slots, LANES), 1)
    mine = lane % GROUP == my_ref[0]
    other_gate = jnp.sum(jnp.where((lane // GROUP == 2) & ~mine, tail, 0.0), axis=1, keepdims=True)
    spread = jnp.where(lane // GROUP == 1, jnp.where(mine, tail, -tail), 0.0) * (term * other_gate)
    high = spread.astype(BF)
    low = (spread - high.astype(F32)).astype(BF)
    router = router_ref[...].astype(F32)
    blank = jnp.zeros((GROUP, width), F32)
    padded = [router] if experts == GROUP else [router, jnp.zeros((GROUP - experts, width), F32)]
    router = jnp.concatenate([blank, *padded, blank, blank], axis=0).astype(BF)
    back = lax.dot_general(grad_ref[...], weight_ref[...], COLS, preferred_element_type=F32)
    back = back + jnp.dot(high, router, preferred_element_type=F32) + jnp.dot(low, router, preferred_element_type=F32)
    back = back.astype(BF)
    for m, out in enumerate(outs):
        out[...] = back[m * rows : (m + 1) * rows, :]


def stack_kernel(owners, *refs):
    ins, outs = refs[:10], refs[10:]
    half = outs[0].shape[0] // 2
    for g in range(2):
        near_ref, far_ref, *others = ins[5 * g : 5 * g + 5]
        at = slice(g * half, (g + 1) * half)
        outs[0][at, :] = interleave(near_ref[...].astype(F32), far_ref[...].astype(F32), owners).astype(BF)
        for r, out in zip(others, outs[1:]):
            out[at, :] = r[...]


def combine_kernel(owners, pick_ref, *refs):
    ins, outs = refs[:owners], refs[owners:]
    stacked = jnp.concatenate([r[...] for r in ins], axis=0)
    back = lax.dot_general(pick_ref[...], stacked, ROWS_T, preferred_element_type=F32).astype(BF)
    count = outs[0].shape[0]
    for k, out in enumerate(outs):
        out[...] = back[k * count : (k + 1) * count, :]


def back_kernel(pieces, embed_ref, score_ref, gain_ref, tok_ref, keep_ref, cot_ref, *refs):
    parts, out_ref = refs[:pieces], refs[pieces]
    count, width = tok_ref.shape
    values = quartet_values(embed_ref[...], count)
    kept = keep_ref[...]
    column = [kept[:, i : i + 1] for i in range(17)]
    coefs = column[:4]
    shares = [column[4 + 3 * q : 7 + 3 * q] for q in range(4)]
    scale = column[16]
    normed_grad = parts[0][...].astype(F32)
    for part in parts[1:]:
        normed_grad = normed_grad + part[...].astype(F32)
    tokens = tok_ref[...]
    scaled = gain_ref[...] * normed_grad
    inner = jnp.mean(tokens * scaled, axis=1, keepdims=True)
    token_grad = cot_ref[...].astype(F32) + scale * scaled - tokens * (scale * scale * scale * inner)
    dots = [jnp.sum(token_grad * v, axis=1, keepdims=True) for v in values]
    pairs = [dots[0] + dots[1], dots[2] + dots[3]]
    four = 0.0625 * (pairs[0] + pairs[1])
    score_grads = []
    for q in range(4):
        share = shares[q]
        grads = (0.25 * dots[q], 0.125 * pairs[q // 2], four)
        average = share[0] * grads[0] + share[1] * grads[1] + share[2] * grads[2]
        score_grads.append([s * (g - average) for s, g in zip(share, grads)])
    all_four = 0.25 * (score_grads[0][2] + score_grads[1][2] + score_grads[2][2] + score_grads[3][2])
    weight = score_ref[...]
    ordered = []
    for q in range(4):
        pair = 0.5 * (score_grads[q][1] + score_grads[q ^ 1][1])
        slope = score_grads[q][0] + pair + all_four
        ordered.append((coefs[q] * token_grad + slope * weight).astype(BF))
    out_ref[...] = lax.dot_general(
        quartet_order(count), jnp.concatenate(ordered, axis=0), ROWS_T, preferred_element_type=F32
    ).astype(BF)


def per_device(byte_embed, score_weight, norm_gain, router, routes, expert_in, expert_out, cotangent):
    experts = router.shape[1]
    count = routes.shape[1]
    width = byte_embed.shape[2]
    full = width + LANES
    capacity = max(2, 3 * count // experts)
    pieces = lax.axis_size("seq")
    owners = lax.axis_size("exp")
    chunks = owners // 2
    rows = 2 * pieces * capacity
    slots = chunks * rows
    tokens = pieces * count
    hidden = expert_in.shape[2]
    tile = min(256, hidden)
    my = lax.axis_index("exp").astype(jnp.int32).reshape(1)
    embed = byte_embed[0]
    cot = cotangent[0]
    score_row = score_weight.reshape(1, width)
    gain_row = norm_gain.reshape(1, width)
    router_t = router.T
    routes_t = routes[0].T
    weight_in = expert_in[0]
    weight_out = expert_out[0]

    def shape(*dims, dtype=BF):
        return jax.ShapeDtypeStruct(dims, dtype)

    def over_seq(value, k):
        return lax.ppermute(value, "seq", [(i, i ^ k) for i in range(pieces)])

    def over_exp(values, step):
        moved = list(values)
        for m in sorted(range(1, len(values)), key=lambda m: (m & (2 // step - 1), -m)):
            moved[m] = lax.ppermute(values[m], "exp", [(i, i ^ (m * step)) for i in range(owners)])
        return moved

    def over_cores(value):
        return lax.ppermute(value, "exp", [(i, i ^ 1) for i in range(owners)])

    half = pieces // 2
    places = list(range(0, pieces, 2)) + list(range(1, pieces, 2))
    front_args = (embed, score_row, gain_row, router_t, routes_t)
    cot_far = [over_seq(cot, k) for k in places[1:half]]
    pay, tok, keep = call(
        front_kernel,
        "front",
        (shape(count, full), shape(count, width, dtype=F32), shape(count, LANES, dtype=F32)),
        front_args,
        us=2.0,
        scratch=[pltpu.VMEM(a.shape, a.dtype) for a in front_args]
        + [pltpu.VMEM((count, LANES), F32), pltpu.SemaphoreType.DMA((len(front_args),))],
        limit=56,
        held=False,
    )
    held_cot = call(functools.partial(gather_kernel, 0), "hold_cot", shape(count, width), (cot,), us=1.0)
    cot_near = call(
        functools.partial(gather_kernel, 0), "cot_near", shape(half * count, width), (held_cot, *cot_far), us=5.0
    )
    held = call(functools.partial(gather_kernel, 0), "hold_own", shape(count, full), (pay,), us=1.0)
    held_out = call(functools.partial(gather_kernel, 0), "hold_weight", shape(hidden, width), (weight_out,), us=2.0)
    token_near = call(
        functools.partial(gather_kernel, 1),
        "token_near",
        shape(tokens, full),
        (cot_near, held, *[over_seq(pay, k) for k in places[1:]]),
    )
    chosen = call(
        functools.partial(pick_kernel, pieces, chunks, capacity),
        "pick",
        [shape(rows // 2, width)] * chunks + [shape(rows, full)] * chunks,
        (my, cot_near, token_near, over_cores(cot_near), over_cores(token_near)),
        scalars=1,
        limit=16,
    )
    back_pick = call(
        functools.partial(back_pick_kernel, owners, count, capacity),
        "back_pick",
        shape(slots, tokens),
        (my, token_near),
        us=1.0,
        scalars=1,
        limit=16,
    )
    cot_chunks = over_exp(chosen[:chunks], 2)
    token_chunks = over_exp(chosen[chunks:], 2)
    order = [0, *range(chunks - 1, 0, -1)]
    stacked, back_rows = [], [None] * owners
    groups = (order[: chunks // 2], order[chunks // 2 :])
    part = slots // 2
    near, far, upstream = [], [], []
    for group in groups:
        cot_a = call(
            functools.partial(gather_kernel, 0), "cot_slots", shape(part // 2, width), [cot_chunks[m] for m in group]
        )
        near.append(cot_a)
        far.append(over_seq(cot_a, 1))
    for cot_a, cot_b in zip(near, far):
        upstream.append(
            call(
                functools.partial(upstream_kernel, chunks),
                "upstream",
                shape(part, hidden, dtype=F32),
                (cot_a, cot_b, held_out),
                limit=16,
            )
        )
    for g, group in enumerate(groups):
        shares = 2 * len(group)
        waits = upstream[1:] if g == 0 else []
        *outs, token_rows, hidden_rows, hidden_grad = call(
            functools.partial(expert_kernel, len(group), shares, tile, len(waits)),
            "expert",
            [shape(rows // 2, width)] * shares + [shape(part, width), shape(part, hidden), shape(part, hidden)],
            (my, *waits, *[token_chunks[m] for m in group], upstream[g], weight_in, router_t),
            scalars=1,
            limit=24,
        )
        for i, out in enumerate(outs):
            back_rows[2 * group[i // 2] + i % 2] = out
        stacked += [near[g], far[g], hidden_rows, token_rows, hidden_grad]
    cot_slots, hidden_rows, token_slots, hidden_grad = call(
        functools.partial(stack_kernel, chunks),
        "stack",
        (shape(slots, width), shape(slots, hidden), shape(slots, width), shape(slots, hidden)),
        stacked,
        limit=16,
    )
    grad_out = lax.dot_general(hidden_rows, cot_slots, ROWS_T, preferred_element_type=F32)
    grad_in = lax.dot_general(token_slots, hidden_grad, ROWS_T, preferred_element_type=F32)
    *returned, grad_out = lax.optimization_barrier((*over_exp(back_rows, 1), grad_out))
    partial_rows = call(
        functools.partial(combine_kernel, owners),
        "combine",
        [shape(count, width)] * pieces,
        (back_pick, *returned),
        limit=16,
    )
    parts = [partial_rows[0]] + [over_seq(partial_rows[i], places[i]) for i in range(pieces - 1, 0, -1)]
    embed_grad = call(
        functools.partial(back_kernel, pieces),
        "back",
        shape(4 * count, width),
        (embed, score_row, gain_row, tok, keep, cot, *parts),
    )
    return (embed_grad[None], grad_in[None], grad_out[None])


def solution(mesh):
    in_specs = (
        P("exp", "seq", None),
        P(),
        P(),
        P(),
        P("exp", "seq", None),
        P("exp", None, "seq"),
        P("exp", "seq", None),
        P("exp", "seq", None),
    )
    out_specs = (P("exp", "seq", None), P("exp", None, "seq"), P("exp", "seq", None))
    return jax.shard_map(
        per_device, mesh=mesh, in_specs=in_specs, out_specs=out_specs, check_vma=False
    )
```

```python
import functools
import jax
import jax.numpy as jnp
from jax import lax
from jax.experimental import pallas as pl
from jax.experimental.pallas import tpu as pltpu
from jax.sharding import PartitionSpec as P

SQRT_HALF = 0.7071067811865476
INV_ROOT_TWO_PI = 0.3989422804014327
LANES = 128
GROUP = LANES // 4
BF = jnp.bfloat16
F32 = jnp.float32
HIGHEST = lax.Precision.HIGHEST
ROWS_T = (((0,), (0,)), ((), ()))
COLS = (((1,), (1,)), ((), ()))
MIB = 1024 * 1024
BYTES_PER_US = 3_000_000


def call(body, name, outs, args, us=0.0, scratch=(), limit=8, scalars=0, held=True):
    vmem = pl.BlockSpec(memory_space=pltpu.VMEM)
    smem = pl.BlockSpec(memory_space=pltpu.SMEM)
    rest = vmem if held else pl.BlockSpec(memory_space=pltpu.HBM)
    return pl.pallas_call(
        body,
        name=name,
        out_shape=outs,
        in_specs=[smem] * scalars + [rest] * (len(args) - scalars),
        out_specs=jax.tree.map(lambda _: vmem, outs),
        scratch_shapes=list(scratch),
        compiler_params=pltpu.CompilerParams(vmem_limit_bytes=limit * MIB),
        cost_estimate=pl.CostEstimate(flops=0, bytes_accessed=int(us * BYTES_PER_US), transcendentals=0),
    )(*args)


def route_mask(routes_t, k):
    count = routes_t.shape[1]
    lane = lax.broadcasted_iota(jnp.int32, (LANES, count), 0) % GROUP
    mask_t = (lane == routes_t[k : k + 1, :]).astype(F32).astype(BF)
    row = lax.broadcasted_iota(jnp.int32, (count, count), 0)
    col = lax.broadcasted_iota(jnp.int32, (count, count), 1)
    eye = (row == col).astype(F32).astype(BF)
    return lax.dot_general(eye, mask_t, COLS, preferred_element_type=F32)


def quartet_order(count):
    row = lax.broadcasted_iota(jnp.int32, (4 * count, 4 * count), 0)
    col = lax.broadcasted_iota(jnp.int32, (4 * count, 4 * count), 1)
    return (4 * (row % count) + row // count == col).astype(F32).astype(BF)


def quartet_values(embed, count):
    ordered = jnp.dot(quartet_order(count), embed, preferred_element_type=F32)
    return [ordered[q * count : (q + 1) * count, :] for q in range(4)]


def quartet_scores(values, weight):
    ones = [jnp.sum(v * weight, axis=1, keepdims=True) for v in values]
    pairs = [0.5 * (ones[0] + ones[1]), 0.5 * (ones[2] + ones[3])]
    four = 0.5 * (pairs[0] + pairs[1])
    shares = []
    for q in range(4):
        scores = (ones[q], pairs[q // 2], four)
        largest = jnp.maximum(jnp.maximum(scores[0], scores[1]), scores[2])
        weights = [jnp.exp(s - largest) for s in scores]
        denominator = weights[0] + weights[1] + weights[2]
        shares.append([w / denominator for w in weights])
    return shares


def front_kernel(*refs):
    far, outs, near, logit, arrived = refs[:5], refs[5:8], refs[8:13], refs[13], refs[14]
    copies = [pltpu.make_async_copy(a, b, arrived.at[i]) for i, (a, b) in enumerate(zip(far, near))]
    for copy in copies:
        copy.start()
    embed_ref, score_ref, gain_ref, router_ref, routes_ref = near
    pay_ref, tok_ref, keep_ref = outs
    for copy in copies:
        copy.wait()
    count, width = tok_ref.shape
    experts = router_ref.shape[0]
    values = quartet_values(embed_ref[...], count)
    shares = quartet_scores(values, score_ref[...])
    whole = 0.25 * (shares[0][2] + shares[1][2] + shares[2][2] + shares[3][2])
    coefs = []
    for q in range(4):
        pair = 0.5 * (shares[q][1] + shares[q ^ 1][1])
        coefs.append(0.25 * (shares[q][0] + pair + whole))
    tokens = coefs[0] * values[0] + coefs[1] * values[1] + coefs[2] * values[2] + coefs[3] * values[3]
    tok_ref[...] = tokens
    scale = lax.rsqrt(jnp.mean(tokens * tokens, axis=1, keepdims=True) + 1e-06)
    normed = tokens * scale * gain_ref[...]
    logit[...] = jnp.zeros_like(logit)
    logit[:, :experts] = lax.dot_general(
        normed, router_ref[...].astype(F32), COLS, precision=HIGHEST, preferred_element_type=F32
    )
    logits = logit[...]
    sigmoid = 1.0 / (1.0 + jnp.exp(-logits))
    rest = 1.0 / (1.0 + jnp.exp(logits))
    routes_t = routes_ref[...]
    masks = [route_mask(routes_t, k) for k in range(2)]
    group = lax.broadcasted_iota(jnp.int32, masks[0].shape, 1) // GROUP
    once = [jnp.where(group == 0, m, 0.0) for m in masks]
    picked = [jnp.sum(m * sigmoid, axis=1, keepdims=True) for m in once]
    others = [jnp.sum(m * rest, axis=1, keepdims=True) for m in once]
    total = picked[0] + picked[1]
    tail = jnp.zeros_like(masks[0])
    for mask, sig, other in zip(masks, picked, others):
        value = jnp.where(group == 0, 1.0, jnp.where(group == 1, other, jnp.where(group == 2, sig / total, 0.0)))
        tail = tail + mask * value
    pay_ref[:, :width] = normed.astype(BF)
    pay_ref[:, width:] = tail.astype(BF)
    lane = lax.broadcasted_iota(jnp.int32, keep_ref.shape, 1)
    columns = coefs + [s for share in shares for s in share] + [scale]
    kept = jnp.zeros(keep_ref.shape, F32)
    for i, column in enumerate(columns):
        kept = jnp.where(lane == i, column, kept)
    keep_ref[...] = kept


def gather_kernel(skipped, *refs):
    ins, out_ref = refs[skipped:-1], refs[-1]
    at = 0
    for r in ins:
        out_ref[at : at + r.shape[0], :] = r[...]
        at += r.shape[0]


def slot_places(tail, columns, count, capacity, my):
    tokens = tail.shape[0]
    lane_row = lax.broadcasted_iota(jnp.int32, (LANES, LANES), 0)
    lane_col = lax.broadcasted_iota(jnp.int32, (LANES, LANES), 1)
    lane = (2 * (lane_col % GROUP)) ^ my
    lane = jnp.where(lane_col < GROUP, lane, lane + 2 * GROUP)
    live = (lane_col % GROUP < columns) & (lane_col < 2 * GROUP)
    order = ((lane_row == lane) & live).astype(F32).astype(BF)
    ordered = jnp.dot(tail, order, preferred_element_type=F32).astype(BF)
    row = lax.broadcasted_iota(jnp.int32, (tokens, tokens), 0)
    col = lax.broadcasted_iota(jnp.int32, (tokens, tokens), 1)
    eye = (row == col).astype(F32).astype(BF)
    before = ((row < col) & (row // count == col // count)).astype(F32).astype(BF)
    ordered_t = lax.dot_general(ordered, eye, ROWS_T, preferred_element_type=F32)
    place_t = lax.dot_general(ordered, before, ROWS_T, preferred_element_type=F32)[:GROUP, :]
    block = lax.broadcasted_iota(jnp.int32, (GROUP, tokens), 1) // count
    place_t = place_t + (block * capacity).astype(F32)
    return jnp.where(ordered_t[:GROUP, :] > 0.5, place_t, -1.0), ordered_t[GROUP : 2 * GROUP, :]


def selection(places, values, columns, rows):
    slot = lax.broadcasted_iota(jnp.int32, (rows, places.shape[1]), 0).astype(F32)
    picks = [jnp.where(places[m : m + 1, :] == slot, values[m : m + 1, :], 0.0) for m in range(columns)]
    return jnp.concatenate(picks, axis=0).astype(BF)


def pick_kernel(pieces, chunks, capacity, my_ref, cot_ref, token_ref, other_cot_ref, other_token_ref, *refs):
    cot_outs, outs, pick_ref = refs[:chunks], refs[chunks : 2 * chunks], refs[2 * chunks]
    tokens, full = token_ref.shape
    width = full - LANES
    count = tokens // pieces
    cots = cot_ref.shape[0]
    near = pieces // 2
    my = my_ref[0]

    tail = jnp.concatenate([token_ref[:cots, width:], other_token_ref[:cots, width:]], axis=0)
    places, gates = slot_places(tail, chunks, count, capacity, my)
    picks = selection(places, gates, chunks, 2 * near * capacity)
    cot_rows = jnp.concatenate([cot_ref[...], other_cot_ref[...]], axis=0)
    chosen = jnp.dot(picks, cot_rows, preferred_element_type=F32).astype(BF)
    for m, out in enumerate(cot_outs):
        out[...] = chosen[m * out.shape[0] : (m + 1) * out.shape[0], :]

    token_rows = jnp.concatenate([token_ref[...], other_token_ref[...]], axis=0)
    places, gates = slot_places(token_rows[:, width:], chunks, count, capacity, my)
    picks = selection(places, jnp.ones_like(gates), chunks, 2 * pieces * capacity)
    pick_ref[...] = picks
    chosen = jnp.dot(picks, token_rows, preferred_element_type=F32).astype(BF)
    for m, out in enumerate(outs):
        out[...] = chosen[m * out.shape[0] : (m + 1) * out.shape[0], :]


def interleave(near, far, owners):
    share = near.shape[0] // owners
    return jnp.concatenate([r[d * share : (d + 1) * share, :] for d in range(owners) for r in (near, far)], axis=0)


def upstream_kernel(owners, near_ref, far_ref, weight_ref, out_ref):
    rows = jnp.concatenate([near_ref[...], far_ref[...]], axis=0)
    upstream = lax.dot_general(rows, weight_ref[...], COLS, preferred_element_type=F32)
    half = near_ref.shape[0]
    out_ref[...] = interleave(upstream[:half, :], upstream[half:, :], owners)


def expert_kernel(chunks, tile, waits, my_ref, *refs):
    refs = refs[waits:]
    ins, refs = refs[:chunks], refs[chunks:]
    upstream_ref, weight_ref, router_ref = refs[:3]
    outs, (rows_ref, hidden_ref, grad_ref) = refs[3 : 3 + chunks], refs[3 + chunks :]
    slots, width = rows_ref.shape
    experts = router_ref.shape[0]
    rows = slots // chunks
    token_rows = jnp.concatenate([r[:, :width] for r in ins], axis=0)
    rows_ref[...] = token_rows
    terms = jnp.zeros((slots, LANES), F32)
    for f in range(weight_ref.shape[1] // tile):
        part = slice(f * tile, (f + 1) * tile)
        preact = jnp.dot(token_rows, weight_ref[:, part], preferred_element_type=F32)
        upstream = upstream_ref[:, part]
        normal_cdf = 0.5 * (1.0 + lax.erf(preact * SQRT_HALF))
        normal_pdf = INV_ROOT_TWO_PI * jnp.exp(-0.5 * preact * preact)
        hidden = preact * normal_cdf
        products = hidden * upstream
        for k in range(tile // LANES):
            terms = terms + products[:, k * LANES : (k + 1) * LANES]
        grad_ref[:, part] = (upstream * (normal_cdf + preact * normal_pdf)).astype(BF)
        hidden_ref[:, part] = hidden.astype(BF)
    term = jnp.sum(terms, axis=1, keepdims=True)
    tail = jnp.concatenate([r[:, width:] for r in ins], axis=0).astype(F32)
    lane = lax.broadcasted_iota(jnp.int32, (slots, LANES), 1)
    mine = lane % GROUP == my_ref[0]
    other_gate = jnp.sum(jnp.where((lane // GROUP == 2) & ~mine, tail, 0.0), axis=1, keepdims=True)
    spread = jnp.where(lane // GROUP == 1, jnp.where(mine, tail, -tail), 0.0) * (term * other_gate)
    high = spread.astype(BF)
    low = (spread - high.astype(F32)).astype(BF)
    router = router_ref[...].astype(F32)
    blank = jnp.zeros((GROUP, width), F32)
    padded = [router] if experts == GROUP else [router, jnp.zeros((GROUP - experts, width), F32)]
    router = jnp.concatenate([blank, *padded, blank, blank], axis=0).astype(BF)
    back = lax.dot_general(grad_ref[...], weight_ref[...], COLS, preferred_element_type=F32)
    back = back + jnp.dot(high, router, preferred_element_type=F32) + jnp.dot(low, router, preferred_element_type=F32)
    back = back.astype(BF)
    for m, out in enumerate(outs):
        out[...] = back[m * rows : (m + 1) * rows, :]


def stack_kernel(owners, *refs):
    ins, outs = refs[:-4], refs[-4:]
    cots = [interleave(a[...].astype(F32), b[...].astype(F32), owners) for a, b in zip(ins[::5], ins[1::5])]
    outs[0][...] = jnp.concatenate(cots, axis=0).astype(BF)
    for i, out in enumerate(outs[1:]):
        out[...] = jnp.concatenate([r[...] for r in ins[2 + i :: 5]], axis=0)


def combine_other_kernel(pick_ref, *refs):
    ins, out_ref = refs[:-1], refs[-1]
    tokens = out_ref.shape[0]
    rows = jnp.concatenate([r[...] for r in ins], axis=0)
    out_ref[...] = lax.dot_general(pick_ref[:, tokens:], rows, ROWS_T, preferred_element_type=F32).astype(BF)


def combine_own_kernel(chunks, pick_ref, *refs):
    ins, other_ref, outs = refs[:chunks], refs[chunks], refs[chunks + 1 :]
    tokens = other_ref.shape[0]
    count = outs[0].shape[0]
    rows = jnp.concatenate([r[...] for r in ins], axis=0)
    back = lax.dot_general(pick_ref[:, :tokens], rows, ROWS_T, preferred_element_type=F32)
    back = (back + other_ref[...].astype(F32)).astype(BF)
    for k, out in enumerate(outs):
        out[...] = back[k * count : (k + 1) * count, :]


def back_kernel(pieces, embed_ref, score_ref, gain_ref, tok_ref, keep_ref, cot_ref, *refs):
    parts, out_ref = refs[:pieces], refs[pieces]
    count, width = tok_ref.shape
    values = quartet_values(embed_ref[...], count)
    kept = keep_ref[...]
    column = [kept[:, i : i + 1] for i in range(17)]
    coefs = column[:4]
    shares = [column[4 + 3 * q : 7 + 3 * q] for q in range(4)]
    scale = column[16]
    normed_grad = parts[0][...].astype(F32)
    for part in parts[1:]:
        normed_grad = normed_grad + part[...].astype(F32)
    tokens = tok_ref[...]
    scaled = gain_ref[...] * normed_grad
    inner = jnp.mean(tokens * scaled, axis=1, keepdims=True)
    token_grad = cot_ref[...].astype(F32) + scale * scaled - tokens * (scale * scale * scale * inner)
    dots = [jnp.sum(token_grad * v, axis=1, keepdims=True) for v in values]
    pairs = [dots[0] + dots[1], dots[2] + dots[3]]
    four = 0.0625 * (pairs[0] + pairs[1])
    score_grads = []
    for q in range(4):
        share = shares[q]
        grads = (0.25 * dots[q], 0.125 * pairs[q // 2], four)
        average = share[0] * grads[0] + share[1] * grads[1] + share[2] * grads[2]
        score_grads.append([s * (g - average) for s, g in zip(share, grads)])
    all_four = 0.25 * (score_grads[0][2] + score_grads[1][2] + score_grads[2][2] + score_grads[3][2])
    weight = score_ref[...]
    ordered = []
    for q in range(4):
        pair = 0.5 * (score_grads[q][1] + score_grads[q ^ 1][1])
        slope = score_grads[q][0] + pair + all_four
        ordered.append((coefs[q] * token_grad + slope * weight).astype(BF))
    out_ref[...] = lax.dot_general(
        quartet_order(count), jnp.concatenate(ordered, axis=0), ROWS_T, preferred_element_type=F32
    ).astype(BF)


def per_device(byte_embed, score_weight, norm_gain, router, routes, expert_in, expert_out, cotangent):
    experts = router.shape[1]
    count = routes.shape[1]
    width = byte_embed.shape[2]
    full = width + LANES
    capacity = max(2, 3 * count // experts)
    pieces = lax.axis_size("seq")
    owners = lax.axis_size("exp")
    chunks = owners // 2
    rows = 2 * pieces * capacity
    slots = chunks * rows
    tokens = pieces * count
    hidden = expert_in.shape[2]
    tile = min(256, hidden)
    my = lax.axis_index("exp").astype(jnp.int32).reshape(1)
    embed = byte_embed[0]
    cot = cotangent[0]
    score_row = score_weight.reshape(1, width)
    gain_row = norm_gain.reshape(1, width)
    router_t = router.T
    routes_t = routes[0].T
    weight_in = expert_in[0]
    weight_out = expert_out[0]

    def shape(*dims, dtype=BF):
        return jax.ShapeDtypeStruct(dims, dtype)

    def over_seq(value, k):
        return lax.ppermute(value, "seq", [(i, i ^ k) for i in range(pieces)])

    def over_exp(values, step):
        moved = list(values)
        for m in sorted(range(1, len(values)), key=lambda m: (m & (2 // step - 1), -m)):
            moved[m] = lax.ppermute(values[m], "exp", [(i, i ^ (m * step)) for i in range(owners)])
        return moved

    def over_cores(value):
        return lax.ppermute(value, "exp", [(i, i ^ 1) for i in range(owners)])

    half = pieces // 2
    places = list(range(0, pieces, 2)) + list(range(1, pieces, 2))
    front_args = (embed, score_row, gain_row, router_t, routes_t)
    cot_far = [over_seq(cot, k) for k in places[1:half]]
    pay, tok, keep = call(
        front_kernel,
        "front",
        (shape(count, full), shape(count, width, dtype=F32), shape(count, LANES, dtype=F32)),
        front_args,
        us=2.0,
        scratch=[pltpu.VMEM(a.shape, a.dtype) for a in front_args]
        + [pltpu.VMEM((count, LANES), F32), pltpu.SemaphoreType.DMA((len(front_args),))],
        limit=56,
        held=False,
    )
    held_cot = call(functools.partial(gather_kernel, 0), "hold_cot", shape(count, width), (cot,), us=1.0)
    cot_near = call(
        functools.partial(gather_kernel, 0), "cot_near", shape(half * count, width), (held_cot, *cot_far), us=5.0
    )
    held = call(functools.partial(gather_kernel, 0), "hold_own", shape(count, full), (pay,), us=1.0)
    held_out = call(functools.partial(gather_kernel, 0), "hold_weight", shape(hidden, width), (weight_out,), us=2.0)
    token_near = call(
        functools.partial(gather_kernel, 1),
        "token_near",
        shape(tokens, full),
        (cot_near, held, *[over_seq(pay, k) for k in places[1:]]),
    )
    *chosen, pick = call(
        functools.partial(pick_kernel, pieces, chunks, capacity),
        "pick",
        [shape(rows // 2, width)] * chunks + [shape(rows, full)] * chunks + [shape(slots, 2 * tokens)],
        (my, cot_near, token_near, over_cores(cot_near), over_cores(token_near)),
        scalars=1,
        limit=16,
    )
    cot_chunks = over_exp(chosen[:chunks], 2)
    token_chunks = over_exp(chosen[chunks:], 2)
    order = [0, *range(chunks - 1, 0, -1)]
    groups = (order[: chunks // 2], order[chunks // 2 :])
    part = slots // 2
    near, far, upstream = [], [], []
    for group in groups:
        cot_a = call(
            functools.partial(gather_kernel, 0), "cot_slots", shape(part // 2, width), [cot_chunks[m] for m in group]
        )
        near.append(cot_a)
        far.append(over_seq(cot_a, 1))
    for cot_a, cot_b in zip(near, far):
        upstream.append(
            call(
                functools.partial(upstream_kernel, chunks),
                "upstream",
                shape(part, hidden, dtype=F32),
                (cot_a, cot_b, held_out),
                limit=16,
            )
        )
    stacked, back_rows = [], [None] * chunks
    for g, group in enumerate(groups):
        waits = upstream[1:] if g == 0 else []
        *outs, token_rows, hidden_rows, hidden_grad = call(
            functools.partial(expert_kernel, len(group), tile, len(waits)),
            "expert",
            [shape(rows, width)] * len(group) + [shape(part, width), shape(part, hidden), shape(part, hidden)],
            (my, *waits, *[token_chunks[m] for m in group], upstream[g], weight_in, router_t),
            scalars=1,
            limit=24,
        )
        for m, out in zip(group, outs):
            back_rows[m] = out
        stacked += [near[g], far[g], hidden_rows, token_rows, hidden_grad]
    cot_slots, hidden_rows, token_slots, hidden_grad = call(
        functools.partial(stack_kernel, chunks),
        "stack",
        (shape(slots, width), shape(slots, hidden), shape(slots, width), shape(slots, hidden)),
        stacked,
        limit=16,
    )
    grad_out = lax.dot_general(hidden_rows, cot_slots, ROWS_T, preferred_element_type=F32)
    grad_in = lax.dot_general(token_slots, hidden_grad, ROWS_T, preferred_element_type=F32)
    returned = over_exp(back_rows, 2)
    *returned, grad_out = lax.optimization_barrier((*returned, grad_out))
    other_rows = call(combine_other_kernel, "combine_other", shape(tokens, width), (pick, *returned), limit=16)
    partial_rows = call(
        functools.partial(combine_own_kernel, chunks),
        "combine_own",
        [shape(count, width)] * pieces,
        (pick, *returned, over_cores(other_rows)),
        limit=16,
    )
    parts = [partial_rows[0]] + [over_seq(partial_rows[i], places[i]) for i in range(pieces - 1, 0, -1)]
    embed_grad = call(
        functools.partial(back_kernel, pieces),
        "back",
        shape(4 * count, width),
        (embed, score_row, gain_row, tok, keep, cot, *parts),
    )
    return (embed_grad[None], grad_in[None], grad_out[None])


def solution(mesh):
    in_specs = (
        P("exp", "seq", None),
        P(),
        P(),
        P(),
        P("exp", "seq", None),
        P("exp", None, "seq"),
        P("exp", "seq", None),
        P("exp", "seq", None),
    )
    out_specs = (P("exp", "seq", None), P("exp", None, "seq"), P("exp", "seq", None))
    return jax.shard_map(
        per_device, mesh=mesh, in_specs=in_specs, out_specs=out_specs, check_vma=False
    )
```

```python
import functools
import jax
import jax.numpy as jnp
from jax import lax
from jax.experimental import pallas as pl
from jax.experimental.pallas import tpu as pltpu
from jax.sharding import PartitionSpec as P

SQRT_HALF = 0.7071067811865476
INV_ROOT_TWO_PI = 0.3989422804014327
LANES = 128
GROUP = LANES // 4
BF = jnp.bfloat16
F32 = jnp.float32
HIGHEST = lax.Precision.HIGHEST
ROWS_T = (((0,), (0,)), ((), ()))
COLS = (((1,), (1,)), ((), ()))
MIB = 1024 * 1024
BYTES_PER_US = 3_000_000


def call(body, name, outs, args, us=0.0, scratch=(), limit=8, scalars=0, held=True):
    vmem = pl.BlockSpec(memory_space=pltpu.VMEM)
    smem = pl.BlockSpec(memory_space=pltpu.SMEM)
    rest = vmem if held else pl.BlockSpec(memory_space=pltpu.HBM)
    return pl.pallas_call(
        body,
        name=name,
        out_shape=outs,
        in_specs=[smem] * scalars + [rest] * (len(args) - scalars),
        out_specs=jax.tree.map(lambda _: vmem, outs),
        scratch_shapes=list(scratch),
        compiler_params=pltpu.CompilerParams(vmem_limit_bytes=limit * MIB),
        cost_estimate=pl.CostEstimate(flops=0, bytes_accessed=int(us * BYTES_PER_US), transcendentals=0),
    )(*args)


def route_mask(routes_t, k):
    count = routes_t.shape[1]
    lane = lax.broadcasted_iota(jnp.int32, (LANES, count), 0) % GROUP
    mask_t = (lane == routes_t[k : k + 1, :]).astype(F32).astype(BF)
    row = lax.broadcasted_iota(jnp.int32, (count, count), 0)
    col = lax.broadcasted_iota(jnp.int32, (count, count), 1)
    eye = (row == col).astype(F32).astype(BF)
    return lax.dot_general(eye, mask_t, COLS, preferred_element_type=F32)


def quartet_order(count):
    row = lax.broadcasted_iota(jnp.int32, (4 * count, 4 * count), 0)
    col = lax.broadcasted_iota(jnp.int32, (4 * count, 4 * count), 1)
    return (4 * (row % count) + row // count == col).astype(F32).astype(BF)


def quartet_values(embed, count):
    ordered = jnp.dot(quartet_order(count), embed, preferred_element_type=F32)
    return [ordered[q * count : (q + 1) * count, :] for q in range(4)]


def quartet_scores(values, weight):
    ones = [jnp.sum(v * weight, axis=1, keepdims=True) for v in values]
    pairs = [0.5 * (ones[0] + ones[1]), 0.5 * (ones[2] + ones[3])]
    four = 0.5 * (pairs[0] + pairs[1])
    shares = []
    for q in range(4):
        scores = (ones[q], pairs[q // 2], four)
        largest = jnp.maximum(jnp.maximum(scores[0], scores[1]), scores[2])
        weights = [jnp.exp(s - largest) for s in scores]
        denominator = weights[0] + weights[1] + weights[2]
        shares.append([w / denominator for w in weights])
    return shares


def pooled(values, weight):
    shares = quartet_scores(values, weight)
    whole = 0.25 * (shares[0][2] + shares[1][2] + shares[2][2] + shares[3][2])
    coefs = []
    for q in range(4):
        pair = 0.5 * (shares[q][1] + shares[q ^ 1][1])
        coefs.append(0.25 * (shares[q][0] + pair + whole))
    tokens = coefs[0] * values[0] + coefs[1] * values[1] + coefs[2] * values[2] + coefs[3] * values[3]
    scale = lax.rsqrt(jnp.mean(tokens * tokens, axis=1, keepdims=True) + 1e-06)
    return shares, coefs, tokens, scale


def front_kernel(*refs):
    far, pay_ref, near, logit, arrived = refs[:5], refs[5], refs[6:11], refs[11], refs[12]
    copies = [pltpu.make_async_copy(a, b, arrived.at[i]) for i, (a, b) in enumerate(zip(far, near))]
    for copy in copies:
        copy.start()
    embed_ref, score_ref, gain_ref, router_ref, routes_ref = near
    for copy in copies:
        copy.wait()
    count = pay_ref.shape[0]
    experts, width = router_ref.shape
    _, _, tokens, scale = pooled(quartet_values(embed_ref[...], count), score_ref[...])
    normed = tokens * scale * gain_ref[...]
    high = normed.astype(BF)
    rest = normed - high.astype(F32)
    middle = rest.astype(BF)
    low = (rest - middle.astype(F32)).astype(BF)
    products = lax.dot_general(
        jnp.concatenate([high, middle, low], axis=0), router_ref[...], COLS, preferred_element_type=F32
    )
    logit[...] = jnp.zeros_like(logit)
    logit[:, :experts] = products[:count, :] + (products[count : 2 * count, :] + products[2 * count :, :])
    logits = logit[...]
    sigmoid = 1.0 / (1.0 + jnp.exp(-logits))
    rest = 1.0 / (1.0 + jnp.exp(logits))
    routes_t = routes_ref[...]
    masks = [route_mask(routes_t, k) for k in range(2)]
    group = lax.broadcasted_iota(jnp.int32, masks[0].shape, 1) // GROUP
    once = [jnp.where(group == 0, m, 0.0) for m in masks]
    picked = [jnp.sum(m * sigmoid, axis=1, keepdims=True) for m in once]
    others = [jnp.sum(m * rest, axis=1, keepdims=True) for m in once]
    total = picked[0] + picked[1]
    tail = jnp.zeros_like(masks[0])
    for mask, sig, other in zip(masks, picked, others):
        value = jnp.where(group == 0, 1.0, jnp.where(group == 1, other, jnp.where(group == 2, sig / total, 0.0)))
        tail = tail + mask * value
    pay_ref[:, :width] = high
    pay_ref[:, width:] = tail.astype(BF)


def keep_kernel(embed_ref, score_ref, tok_ref, keep_ref):
    count = tok_ref.shape[0]
    shares, coefs, tokens, scale = pooled(quartet_values(embed_ref[...], count), score_ref[...])
    tok_ref[...] = tokens
    columns = coefs + [s for share in shares for s in share] + [scale]
    lane = lax.broadcasted_iota(jnp.int32, keep_ref.shape, 1)
    kept = jnp.zeros(keep_ref.shape, F32)
    for i, column in enumerate(columns):
        kept = jnp.where(lane == i, column, kept)
    keep_ref[...] = kept


def transpose_kernel(in_ref, out_ref):
    out_ref[...] = in_ref[...].T


def gather_kernel(skipped, *refs):
    ins, out_ref = refs[skipped:-1], refs[-1]
    at = 0
    for r in ins:
        out_ref[at : at + r.shape[0], :] = r[...]
        at += r.shape[0]


def slot_places(tail, columns, count, capacity, my):
    tokens = tail.shape[0]
    lane_row = lax.broadcasted_iota(jnp.int32, (LANES, LANES), 0)
    lane_col = lax.broadcasted_iota(jnp.int32, (LANES, LANES), 1)
    lane = (2 * (lane_col % GROUP)) ^ my
    lane = jnp.where(lane_col < GROUP, lane, lane + 2 * GROUP)
    live = (lane_col % GROUP < columns) & (lane_col < 2 * GROUP)
    order = ((lane_row == lane) & live).astype(F32).astype(BF)
    ordered = jnp.dot(tail, order, preferred_element_type=F32).astype(BF)
    row = lax.broadcasted_iota(jnp.int32, (tokens, tokens), 0)
    col = lax.broadcasted_iota(jnp.int32, (tokens, tokens), 1)
    eye = (row == col).astype(F32).astype(BF)
    before = ((row < col) & (row // count == col // count)).astype(F32).astype(BF)
    ordered_t = lax.dot_general(ordered, eye, ROWS_T, preferred_element_type=F32)
    place_t = lax.dot_general(ordered, before, ROWS_T, preferred_element_type=F32)[:GROUP, :]
    block = lax.broadcasted_iota(jnp.int32, (GROUP, tokens), 1) // count
    place_t = place_t + (block * capacity).astype(F32)
    return jnp.where(ordered_t[:GROUP, :] > 0.5, place_t, -1.0), ordered_t[GROUP : 2 * GROUP, :]


def selection(places, values, columns, rows):
    slot = lax.broadcasted_iota(jnp.int32, (rows, places.shape[1]), 0).astype(F32)
    picks = [jnp.where(places[m : m + 1, :] == slot, values[m : m + 1, :], 0.0) for m in range(columns)]
    return jnp.concatenate(picks, axis=0).astype(BF)


def pick_kernel(pieces, chunks, capacity, my_ref, cot_ref, token_ref, other_cot_ref, other_token_ref, *refs):
    cot_outs, outs, pick_ref = refs[:chunks], refs[chunks : 2 * chunks], refs[2 * chunks]
    tokens, full = token_ref.shape
    width = full - LANES
    count = tokens // pieces
    cots = cot_ref.shape[0]
    near = pieces // 2
    my = my_ref[0]

    tail = jnp.concatenate([token_ref[:cots, width:], other_token_ref[:cots, width:]], axis=0)
    places, gates = slot_places(tail, chunks, count, capacity, my)
    picks = selection(places, gates, chunks, 2 * near * capacity)
    cot_rows = jnp.concatenate([cot_ref[...], other_cot_ref[...]], axis=0)
    chosen = jnp.dot(picks, cot_rows, preferred_element_type=F32).astype(BF)
    for m, out in enumerate(cot_outs):
        out[...] = chosen[m * out.shape[0] : (m + 1) * out.shape[0], :]

    token_rows = jnp.concatenate([token_ref[...], other_token_ref[...]], axis=0)
    places, gates = slot_places(token_rows[:, width:], chunks, count, capacity, my)
    picks = selection(places, jnp.ones_like(gates), chunks, 2 * pieces * capacity)
    pick_ref[...] = picks
    chosen = jnp.dot(picks, token_rows, preferred_element_type=F32).astype(BF)
    for m, out in enumerate(outs):
        out[...] = chosen[m * out.shape[0] : (m + 1) * out.shape[0], :]


def interleave(near, far, owners):
    share = near.shape[0] // owners
    return jnp.concatenate([r[d * share : (d + 1) * share, :] for d in range(owners) for r in (near, far)], axis=0)


def upstream_kernel(owners, waits, *refs):
    near_ref, far_ref, weight_ref, out_ref = refs[waits:]
    rows = jnp.concatenate([near_ref[...], far_ref[...]], axis=0)
    upstream = jnp.dot(rows, weight_ref[...], preferred_element_type=F32)
    half = near_ref.shape[0]
    out_ref[...] = interleave(upstream[:half, :], upstream[half:, :], owners)


def hidden_kernel(chunks, tile, waits, *refs):
    refs = refs[waits:]
    ins, (weight_ref, rows_ref, tail_ref, hidden_ref, slope_ref) = refs[:chunks], refs[chunks:]
    width = rows_ref.shape[1]
    token_rows = jnp.concatenate([r[:, :width] for r in ins], axis=0)
    rows_ref[...] = token_rows
    tail_ref[...] = jnp.concatenate([r[:, width:] for r in ins], axis=0)
    for f in range(weight_ref.shape[1] // tile):
        part = slice(f * tile, (f + 1) * tile)
        preact = jnp.dot(token_rows, weight_ref[:, part], preferred_element_type=F32)
        normal_cdf = 0.5 * (1.0 + lax.erf(preact * SQRT_HALF))
        normal_pdf = INV_ROOT_TWO_PI * jnp.exp(-0.5 * preact * preact)
        hidden_ref[:, part] = (preact * normal_cdf).astype(BF)
        slope_ref[:, part] = normal_cdf + preact * normal_pdf


def grad_kernel(chunks, waits, my_ref, *refs):
    hidden_ref, slope_ref, tail_ref, upstream_ref, weight_ref, router_ref = refs[waits : waits + 6]
    outs, grad_ref = refs[waits + 6 : -1], refs[-1]
    slots = hidden_ref.shape[0]
    experts, width = router_ref.shape
    rows = slots // chunks
    terms = jnp.zeros((slots, LANES), F32)
    for k in range(hidden_ref.shape[1] // LANES):
        part = slice(k * LANES, (k + 1) * LANES)
        upstream = upstream_ref[:, part]
        terms = terms + hidden_ref[:, part].astype(F32) * upstream
        grad_ref[:, part] = (upstream * slope_ref[:, part]).astype(BF)
    term = jnp.sum(terms, axis=1, keepdims=True)
    tail = tail_ref[...].astype(F32)
    lane = lax.broadcasted_iota(jnp.int32, (slots, LANES), 1)
    mine = lane % GROUP == my_ref[0]
    other_gate = jnp.sum(jnp.where((lane // GROUP == 2) & ~mine, tail, 0.0), axis=1, keepdims=True)
    spread = jnp.where(lane // GROUP == 1, jnp.where(mine, tail, -tail), 0.0) * (term * other_gate)
    high = spread.astype(BF)
    low = (spread - high.astype(F32)).astype(BF)
    router = router_ref[...].astype(F32)
    blank = jnp.zeros((GROUP, width), F32)
    padded = [router] if experts == GROUP else [router, jnp.zeros((GROUP - experts, width), F32)]
    router = jnp.concatenate([blank, *padded, blank, blank], axis=0).astype(BF)
    back = jnp.dot(grad_ref[...], weight_ref[...], preferred_element_type=F32)
    back = back + jnp.dot(high, router, preferred_element_type=F32) + jnp.dot(low, router, preferred_element_type=F32)
    back = back.astype(BF)
    for m, out in enumerate(outs):
        out[...] = back[m * rows : (m + 1) * rows, :]


def stack_kernel(owners, *refs):
    ins, outs = refs[:-4], refs[-4:]
    cots = [interleave(a[...].astype(F32), b[...].astype(F32), owners) for a, b in zip(ins[::5], ins[1::5])]
    outs[0][...] = jnp.concatenate(cots, axis=0).astype(BF)
    for i, out in enumerate(outs[1:]):
        out[...] = jnp.concatenate([r[...] for r in ins[2 + i :: 5]], axis=0)


def combine_other_kernel(pick_ref, *refs):
    ins, out_ref = refs[:-1], refs[-1]
    tokens = out_ref.shape[0]
    rows = jnp.concatenate([r[...] for r in ins], axis=0)
    out_ref[...] = lax.dot_general(pick_ref[:, tokens:], rows, ROWS_T, preferred_element_type=F32).astype(BF)


def combine_own_kernel(chunks, pick_ref, *refs):
    ins, other_ref, outs = refs[:chunks], refs[chunks], refs[chunks + 1 :]
    tokens = other_ref.shape[0]
    count = outs[0].shape[0]
    rows = jnp.concatenate([r[...] for r in ins], axis=0)
    back = lax.dot_general(pick_ref[:, :tokens], rows, ROWS_T, preferred_element_type=F32)
    back = (back + other_ref[...].astype(F32)).astype(BF)
    for k, out in enumerate(outs):
        out[...] = back[k * count : (k + 1) * count, :]


def back_kernel(pieces, embed_ref, score_ref, gain_ref, tok_ref, keep_ref, cot_ref, *refs):
    parts, out_ref = refs[:pieces], refs[pieces]
    count, width = tok_ref.shape
    values = quartet_values(embed_ref[...], count)
    kept = keep_ref[...]
    column = [kept[:, i : i + 1] for i in range(17)]
    coefs = column[:4]
    shares = [column[4 + 3 * q : 7 + 3 * q] for q in range(4)]
    scale = column[16]
    normed_grad = parts[0][...].astype(F32)
    for part in parts[1:]:
        normed_grad = normed_grad + part[...].astype(F32)
    tokens = tok_ref[...]
    scaled = gain_ref[...] * normed_grad
    inner = jnp.mean(tokens * scaled, axis=1, keepdims=True)
    token_grad = cot_ref[...].astype(F32) + scale * scaled - tokens * (scale * scale * scale * inner)
    dots = [jnp.sum(token_grad * v, axis=1, keepdims=True) for v in values]
    pairs = [dots[0] + dots[1], dots[2] + dots[3]]
    four = 0.0625 * (pairs[0] + pairs[1])
    score_grads = []
    for q in range(4):
        share = shares[q]
        grads = (0.25 * dots[q], 0.125 * pairs[q // 2], four)
        average = share[0] * grads[0] + share[1] * grads[1] + share[2] * grads[2]
        score_grads.append([s * (g - average) for s, g in zip(share, grads)])
    all_four = 0.25 * (score_grads[0][2] + score_grads[1][2] + score_grads[2][2] + score_grads[3][2])
    weight = score_ref[...]
    ordered = []
    for q in range(4):
        pair = 0.5 * (score_grads[q][1] + score_grads[q ^ 1][1])
        slope = score_grads[q][0] + pair + all_four
        ordered.append((coefs[q] * token_grad + slope * weight).astype(BF))
    out_ref[...] = lax.dot_general(
        quartet_order(count), jnp.concatenate(ordered, axis=0), ROWS_T, preferred_element_type=F32
    ).astype(BF)


def per_device(byte_embed, score_weight, norm_gain, router, routes, expert_in, expert_out, cotangent):
    experts = router.shape[1]
    count = routes.shape[1]
    width = byte_embed.shape[2]
    full = width + LANES
    capacity = max(2, 3 * count // experts)
    pieces = lax.axis_size("seq")
    owners = lax.axis_size("exp")
    chunks = owners // 2
    rows = 2 * pieces * capacity
    slots = chunks * rows
    tokens = pieces * count
    hidden = expert_in.shape[2]
    tile = min(256, hidden)
    my = lax.axis_index("exp").astype(jnp.int32).reshape(1)
    embed = byte_embed[0]
    cot = cotangent[0]
    score_row = score_weight.reshape(1, width)
    gain_row = norm_gain.reshape(1, width)
    router_t = router.T
    routes_t = routes[0].T
    weight_in = expert_in[0]
    weight_out = expert_out[0]

    def shape(*dims, dtype=BF):
        return jax.ShapeDtypeStruct(dims, dtype)

    def over_seq(value, k):
        return lax.ppermute(value, "seq", [(i, i ^ k) for i in range(pieces)])

    def over_exp(values, step):
        moved = list(values)
        for m in sorted(range(1, len(values)), key=lambda m: (m & (2 // step - 1), -m)):
            moved[m] = lax.ppermute(values[m], "exp", [(i, i ^ (m * step)) for i in range(owners)])
        return moved

    def over_cores(value):
        return lax.ppermute(value, "exp", [(i, i ^ 1) for i in range(owners)])

    half = pieces // 2
    places = list(range(0, pieces, 2)) + list(range(1, pieces, 2))
    front_args = (embed, score_row, gain_row, router_t, routes_t)
    cot_far = [over_seq(cot, k) for k in places[1:half]]
    pay = call(
        front_kernel,
        "front",
        shape(count, full),
        front_args,
        us=2.0,
        scratch=[pltpu.VMEM(a.shape, a.dtype) for a in front_args]
        + [pltpu.VMEM((count, LANES), F32), pltpu.SemaphoreType.DMA((len(front_args),))],
        limit=56,
        held=False,
    )
    tok, keep = call(
        keep_kernel,
        "keep",
        (shape(count, width, dtype=F32), shape(count, LANES, dtype=F32)),
        (embed, score_row),
        us=2.0,
    )
    held_cot = call(functools.partial(gather_kernel, 0), "hold_cot", shape(count, width), (cot,), us=1.0)
    cot_near = call(
        functools.partial(gather_kernel, 0), "cot_near", shape(half * count, width), (held_cot, *cot_far), us=5.0
    )
    held = call(functools.partial(gather_kernel, 0), "hold_own", shape(count, full), (pay,), us=1.0)
    in_across = call(transpose_kernel, "across", shape(hidden, width), (weight_in,), us=2.0, limit=16)
    out_across = call(transpose_kernel, "across", shape(width, hidden), (weight_out,), us=2.0, limit=16)
    token_near = call(
        functools.partial(gather_kernel, 1),
        "token_near",
        shape(tokens, full),
        (cot_near, held, *[over_seq(pay, k) for k in places[1:]]),
    )
    *chosen, pick = call(
        functools.partial(pick_kernel, pieces, chunks, capacity),
        "pick",
        [shape(rows // 2, width)] * chunks + [shape(rows, full)] * chunks + [shape(slots, 2 * tokens)],
        (my, cot_near, token_near, over_cores(cot_near), over_cores(token_near)),
        scalars=1,
        limit=16,
    )
    cot_chunks = over_exp(chosen[:chunks], 2)
    token_chunks = over_exp(chosen[chunks:], 2)
    order = [0, *range(chunks - 1, 0, -1)]
    groups = (order[: chunks // 2], order[chunks // 2 :])
    part = slots // 2
    near, far, upstream = [], [], []
    for group in groups:
        cot_a = call(
            functools.partial(gather_kernel, 0), "cot_slots", shape(part // 2, width), [cot_chunks[m] for m in group]
        )
        near.append(cot_a)
        far.append(over_seq(cot_a, 1))
    hiddens, upstream = [], []
    for cot_a, cot_b in zip(near, far):
        upstream.append(
            call(
                functools.partial(upstream_kernel, chunks, 0),
                "upstream",
                shape(part, hidden, dtype=F32),
                (cot_a, cot_b, out_across),
                limit=16,
            )
        )
    for g, group in enumerate(groups):
        waits = upstream[1:] if g else []
        hiddens.append(
            call(
                functools.partial(hidden_kernel, len(group), tile, len(waits)),
                "hidden",
                (shape(part, width), shape(part, LANES), shape(part, hidden), shape(part, hidden, dtype=F32)),
                (*waits, *[token_chunks[m] for m in group], weight_in),
                limit=16,
                us=1.0,
            )
        )
    stacked, back_rows = [], [None] * chunks
    for g, group in enumerate(groups):
        waits = upstream[1:] if g == 0 else []
        token_rows, tail, hidden_rows, slope = hiddens[g]
        *outs, hidden_grad = call(
            functools.partial(grad_kernel, len(group), len(waits)),
            "grads",
            [shape(rows, width)] * len(group) + [shape(part, hidden)],
            (my, *waits, hidden_rows, slope, tail, upstream[g], in_across, router_t),
            scalars=1,
            limit=16,
        )
        for m, out in zip(group, outs):
            back_rows[m] = out
        stacked += [near[g], far[g], hidden_rows, token_rows, hidden_grad]
    cot_slots, hidden_rows, token_slots, hidden_grad = call(
        functools.partial(stack_kernel, chunks),
        "stack",
        (shape(slots, width), shape(slots, hidden), shape(slots, width), shape(slots, hidden)),
        stacked,
        limit=16,
    )
    grad_out = lax.dot_general(hidden_rows, cot_slots, ROWS_T, preferred_element_type=F32)
    grad_in = lax.dot_general(token_slots, hidden_grad, ROWS_T, preferred_element_type=F32)
    returned = over_exp(back_rows, 2)
    *returned, grad_out = lax.optimization_barrier((*returned, grad_out))
    other_rows = call(combine_other_kernel, "combine_other", shape(tokens, width), (pick, *returned), limit=16)
    partial_rows = call(
        functools.partial(combine_own_kernel, chunks),
        "combine_own",
        [shape(count, width)] * pieces,
        (pick, *returned, over_cores(other_rows)),
        limit=16,
    )
    parts = [partial_rows[0]] + [over_seq(partial_rows[i], places[i]) for i in range(pieces - 1, 0, -1)]
    embed_grad = call(
        functools.partial(back_kernel, pieces),
        "back",
        shape(4 * count, width),
        (embed, score_row, gain_row, tok, keep, cot, *parts),
    )
    return (embed_grad[None], grad_in[None], grad_out[None])


def solution(mesh):
    in_specs = (
        P("exp", "seq", None),
        P(),
        P(),
        P(),
        P("exp", "seq", None),
        P("exp", None, "seq"),
        P("exp", "seq", None),
        P("exp", "seq", None),
    )
    out_specs = (P("exp", "seq", None), P("exp", None, "seq"), P("exp", "seq", None))
    return jax.shard_map(
        per_device, mesh=mesh, in_specs=in_specs, out_specs=out_specs, check_vma=False
    )
```

```python
import functools
import jax
import jax.numpy as jnp
from jax import lax
from jax.experimental import pallas as pl
from jax.experimental.pallas import tpu as pltpu
from jax.sharding import PartitionSpec as P

SQRT_HALF = 0.7071067811865476
INV_ROOT_TWO_PI = 0.3989422804014327
LANES = 128
GROUP = LANES // 4
BF = jnp.bfloat16
F32 = jnp.float32
HIGHEST = lax.Precision.HIGHEST
ROWS_T = (((0,), (0,)), ((), ()))
COLS = (((1,), (1,)), ((), ()))
MIB = 1024 * 1024
BYTES_PER_US = 3_000_000


def call(body, name, outs, args, us=0.0, scratch=(), limit=8, scalars=0, held=True):
    vmem = pl.BlockSpec(memory_space=pltpu.VMEM)
    smem = pl.BlockSpec(memory_space=pltpu.SMEM)
    rest = vmem if held else pl.BlockSpec()
    return pl.pallas_call(
        body,
        name=name,
        out_shape=outs,
        in_specs=[smem] * scalars + [rest] * (len(args) - scalars),
        out_specs=jax.tree.map(lambda _: vmem, outs),
        scratch_shapes=list(scratch),
        compiler_params=pltpu.CompilerParams(vmem_limit_bytes=limit * MIB),
        cost_estimate=pl.CostEstimate(flops=0, bytes_accessed=int(us * BYTES_PER_US), transcendentals=0),
    )(*args)


def route_mask(routes_t, k):
    count = routes_t.shape[1]
    lane = lax.broadcasted_iota(jnp.int32, (LANES, count), 0) % GROUP
    mask_t = (lane == routes_t[k : k + 1, :]).astype(F32).astype(BF)
    row = lax.broadcasted_iota(jnp.int32, (count, count), 0)
    col = lax.broadcasted_iota(jnp.int32, (count, count), 1)
    eye = (row == col).astype(F32).astype(BF)
    return lax.dot_general(eye, mask_t, COLS, preferred_element_type=F32)


def quartet_order(count):
    row = lax.broadcasted_iota(jnp.int32, (4 * count, 4 * count), 0)
    col = lax.broadcasted_iota(jnp.int32, (4 * count, 4 * count), 1)
    return (4 * (row % count) + row // count == col).astype(F32).astype(BF)


def quartet_values(embed, count):
    ordered = jnp.dot(quartet_order(count), embed, preferred_element_type=F32)
    return [ordered[q * count : (q + 1) * count, :] for q in range(4)]


def quartet_scores(values, weight):
    ones = [jnp.sum(v * weight, axis=1, keepdims=True) for v in values]
    pairs = [0.5 * (ones[0] + ones[1]), 0.5 * (ones[2] + ones[3])]
    four = 0.5 * (pairs[0] + pairs[1])
    shares = []
    for q in range(4):
        scores = (ones[q], pairs[q // 2], four)
        largest = jnp.maximum(jnp.maximum(scores[0], scores[1]), scores[2])
        weights = [jnp.exp(s - largest) for s in scores]
        denominator = weights[0] + weights[1] + weights[2]
        shares.append([w / denominator for w in weights])
    return shares


def pooled(values, weight):
    shares = quartet_scores(values, weight)
    whole = 0.25 * (shares[0][2] + shares[1][2] + shares[2][2] + shares[3][2])
    coefs = []
    for q in range(4):
        pair = 0.5 * (shares[q][1] + shares[q ^ 1][1])
        coefs.append(0.25 * (shares[q][0] + pair + whole))
    tokens = coefs[0] * values[0] + coefs[1] * values[1] + coefs[2] * values[2] + coefs[3] * values[3]
    scale = lax.rsqrt(jnp.mean(tokens * tokens, axis=1, keepdims=True) + 1e-06)
    return shares, coefs, tokens, scale


def front_kernel(embed_ref, score_ref, gain_ref, router_ref, routes_ref, pay_ref, logit):
    count = pay_ref.shape[0]
    experts, width = router_ref.shape
    _, _, tokens, scale = pooled(quartet_values(embed_ref[...], count), score_ref[...])
    normed = tokens * scale * gain_ref[...]
    high = normed.astype(BF)
    rest = normed - high.astype(F32)
    middle = rest.astype(BF)
    low = (rest - middle.astype(F32)).astype(BF)
    products = lax.dot_general(
        jnp.concatenate([high, middle, low], axis=0), router_ref[...], COLS, preferred_element_type=F32
    )
    logit[...] = jnp.zeros_like(logit)
    logit[:, :experts] = products[:count, :] + (products[count : 2 * count, :] + products[2 * count :, :])
    logits = logit[...]
    sigmoid = 1.0 / (1.0 + jnp.exp(-logits))
    rest = 1.0 / (1.0 + jnp.exp(logits))
    routes_t = routes_ref[...]
    masks = [route_mask(routes_t, k) for k in range(2)]
    group = lax.broadcasted_iota(jnp.int32, masks[0].shape, 1) // GROUP
    once = [jnp.where(group == 0, m, 0.0) for m in masks]
    picked = [jnp.sum(m * sigmoid, axis=1, keepdims=True) for m in once]
    others = [jnp.sum(m * rest, axis=1, keepdims=True) for m in once]
    total = picked[0] + picked[1]
    tail = jnp.zeros_like(masks[0])
    for mask, sig, other in zip(masks, picked, others):
        value = jnp.where(group == 0, 1.0, jnp.where(group == 1, other, jnp.where(group == 2, sig / total, 0.0)))
        tail = tail + mask * value
    pay_ref[:, :width] = high
    pay_ref[:, width:] = tail.astype(BF)


def keep_kernel(embed_ref, score_ref, tok_ref, keep_ref):
    count = tok_ref.shape[0]
    shares, coefs, tokens, scale = pooled(quartet_values(embed_ref[...], count), score_ref[...])
    tok_ref[...] = tokens
    columns = coefs + [s for share in shares for s in share] + [scale]
    lane = lax.broadcasted_iota(jnp.int32, keep_ref.shape, 1)
    kept = jnp.zeros(keep_ref.shape, F32)
    for i, column in enumerate(columns):
        kept = jnp.where(lane == i, column, kept)
    keep_ref[...] = kept


def transpose_kernel(in_ref, out_ref):
    out_ref[...] = in_ref[...].T


def gather_kernel(skipped, *refs):
    ins, out_ref = refs[skipped:-1], refs[-1]
    at = 0
    for r in ins:
        out_ref[at : at + r.shape[0], :] = r[...]
        at += r.shape[0]


def slot_places(tail, columns, count, capacity, my):
    tokens = tail.shape[0]
    at = lax.broadcasted_iota(jnp.int32, (LANES, LANES), 0)
    lane = lax.broadcasted_iota(jnp.int32, (LANES, LANES), 1)
    named_lane = (2 * (at % GROUP)) ^ my
    named_lane = jnp.where(at < GROUP, named_lane, named_lane + 2 * GROUP)
    live = (at % GROUP < columns) & (at < 2 * GROUP)
    order = ((lane == named_lane) & live).astype(F32).astype(BF)
    row = lax.broadcasted_iota(jnp.int32, (tokens, tokens), 0)
    col = lax.broadcasted_iota(jnp.int32, (tokens, tokens), 1)
    before = ((row < col) & (row // count == col // count)).astype(F32).astype(BF)
    ordered_t = lax.dot_general(order, tail, COLS, preferred_element_type=F32)
    named_t = ordered_t[:GROUP, :]
    place_t = jnp.dot(named_t.astype(BF), before, preferred_element_type=F32)
    block = lax.broadcasted_iota(jnp.int32, (GROUP, tokens), 1) // count
    place_t = place_t + (block * capacity).astype(F32)
    return jnp.where(named_t > 0.5, place_t, -1.0), ordered_t[GROUP : 2 * GROUP, :]


def selection(places, values, columns, rows):
    slot = lax.broadcasted_iota(jnp.int32, (rows, places.shape[1]), 0).astype(F32)
    picks = [jnp.where(places[m : m + 1, :] == slot, values[m : m + 1, :], 0.0) for m in range(columns)]
    return jnp.concatenate(picks, axis=0).astype(BF)


def cot_pick_kernel(pieces, capacity, my_ref, cot_ref, token_ref, other_cot_ref, other_token_ref, *outs):
    tokens, full = token_ref.shape
    width = full - LANES
    count = tokens // pieces
    cots = cot_ref.shape[0]
    tail = jnp.concatenate([token_ref[:cots, width:], other_token_ref[:cots, width:]], axis=0)
    places, gates = slot_places(tail, len(outs), count, capacity, my_ref[0])
    picks = selection(places, gates, len(outs), 2 * (pieces // 2) * capacity)
    cot_rows = jnp.concatenate([cot_ref[...], other_cot_ref[...]], axis=0)
    chosen = jnp.dot(picks, cot_rows, preferred_element_type=F32).astype(BF)
    for m, out in enumerate(outs):
        out[...] = chosen[m * out.shape[0] : (m + 1) * out.shape[0], :]


def token_pick_kernel(pieces, capacity, waits, my_ref, *refs):
    token_ref, other_token_ref, *outs, pick_ref = refs[waits:]
    tokens, full = token_ref.shape
    rows = jnp.concatenate([token_ref[...], other_token_ref[...]], axis=0)
    places, gates = slot_places(rows[:, full - LANES :], len(outs), tokens // pieces, capacity, my_ref[0])
    pick_ref[...] = selection(places, jnp.ones_like(gates), len(outs), 2 * pieces * capacity)
    chosen = jnp.dot(pick_ref[...], rows, preferred_element_type=F32).astype(BF)
    for m, out in enumerate(outs):
        out[...] = chosen[m * out.shape[0] : (m + 1) * out.shape[0], :]


def interleave(near, far, owners):
    share = near.shape[0] // owners
    return jnp.concatenate([r[d * share : (d + 1) * share, :] for d in range(owners) for r in (near, far)], axis=0)


def upstream_kernel(owners, waits, *refs):
    near_ref, far_ref, weight_ref, out_ref = refs[waits:]
    rows = jnp.concatenate([near_ref[...], far_ref[...]], axis=0)
    upstream = jnp.dot(rows, weight_ref[...], preferred_element_type=F32)
    half = near_ref.shape[0]
    out_ref[...] = interleave(upstream[:half, :], upstream[half:, :], owners)


def hidden_kernel(chunks, tile, waits, *refs):
    refs = refs[waits:]
    ins, (weight_ref, rows_ref, tail_ref, hidden_ref, slope_ref) = refs[:chunks], refs[chunks:]
    width = rows_ref.shape[1]
    token_rows = jnp.concatenate([r[:, :width] for r in ins], axis=0)
    rows_ref[...] = token_rows
    tail_ref[...] = jnp.concatenate([r[:, width:] for r in ins], axis=0)
    for f in range(weight_ref.shape[1] // tile):
        part = slice(f * tile, (f + 1) * tile)
        preact = jnp.dot(token_rows, weight_ref[:, part], preferred_element_type=F32)
        normal_cdf = 0.5 * (1.0 + lax.erf(preact * SQRT_HALF))
        normal_pdf = INV_ROOT_TWO_PI * jnp.exp(-0.5 * preact * preact)
        hidden_ref[:, part] = (preact * normal_cdf).astype(BF)
        slope_ref[:, part] = normal_cdf + preact * normal_pdf


def grad_kernel(chunks, waits, my_ref, *refs):
    hidden_ref, slope_ref, tail_ref, upstream_ref, weight_ref, router_ref = refs[waits : waits + 6]
    outs, grad_ref = refs[waits + 6 : -1], refs[-1]
    slots = hidden_ref.shape[0]
    experts, width = router_ref.shape
    rows = slots // chunks
    terms = jnp.zeros((slots, LANES), F32)
    for k in range(hidden_ref.shape[1] // LANES):
        part = slice(k * LANES, (k + 1) * LANES)
        upstream = upstream_ref[:, part]
        terms = terms + hidden_ref[:, part].astype(F32) * upstream
        grad_ref[:, part] = (upstream * slope_ref[:, part]).astype(BF)
    term = jnp.sum(terms, axis=1, keepdims=True)
    tail = tail_ref[...].astype(F32)
    lane = lax.broadcasted_iota(jnp.int32, (slots, LANES), 1)
    mine = lane % GROUP == my_ref[0]
    other_gate = jnp.sum(jnp.where((lane // GROUP == 2) & ~mine, tail, 0.0), axis=1, keepdims=True)
    spread = jnp.where(lane // GROUP == 1, jnp.where(mine, tail, -tail), 0.0) * (term * other_gate)
    high = spread.astype(BF)
    low = (spread - high.astype(F32)).astype(BF)
    router = router_ref[...].astype(F32)
    blank = jnp.zeros((GROUP, width), F32)
    padded = [router] if experts == GROUP else [router, jnp.zeros((GROUP - experts, width), F32)]
    router = jnp.concatenate([blank, *padded, blank, blank], axis=0).astype(BF)
    back = jnp.dot(grad_ref[...], weight_ref[...], preferred_element_type=F32)
    back = back + jnp.dot(high, router, preferred_element_type=F32) + jnp.dot(low, router, preferred_element_type=F32)
    back = back.astype(BF)
    for m, out in enumerate(outs):
        out[...] = back[m * rows : (m + 1) * rows, :]


def stack_kernel(owners, *refs):
    ins, outs = refs[:-4], refs[-4:]
    cots = [interleave(a[...].astype(F32), b[...].astype(F32), owners) for a, b in zip(ins[::5], ins[1::5])]
    outs[0][...] = jnp.concatenate(cots, axis=0).astype(BF)
    for i, out in enumerate(outs[1:]):
        out[...] = jnp.concatenate([r[...] for r in ins[2 + i :: 5]], axis=0)


def combine_other_kernel(pick_ref, *refs):
    ins, out_ref = refs[:-1], refs[-1]
    tokens = out_ref.shape[0]
    rows = jnp.concatenate([r[...] for r in ins], axis=0)
    out_ref[...] = lax.dot_general(pick_ref[:, tokens:], rows, ROWS_T, preferred_element_type=F32).astype(BF)


def combine_own_kernel(chunks, pick_ref, *refs):
    ins, other_ref, outs = refs[:chunks], refs[chunks], refs[chunks + 1 :]
    tokens = other_ref.shape[0]
    count = outs[0].shape[0]
    rows = jnp.concatenate([r[...] for r in ins], axis=0)
    back = lax.dot_general(pick_ref[:, :tokens], rows, ROWS_T, preferred_element_type=F32)
    back = (back + other_ref[...].astype(F32)).astype(BF)
    for k, out in enumerate(outs):
        out[...] = back[k * count : (k + 1) * count, :]


def back_kernel(pieces, embed_ref, score_ref, gain_ref, tok_ref, keep_ref, cot_ref, *refs):
    parts, out_ref = refs[:pieces], refs[pieces]
    count, width = tok_ref.shape
    values = quartet_values(embed_ref[...], count)
    kept = keep_ref[...]
    column = [kept[:, i : i + 1] for i in range(17)]
    coefs = column[:4]
    shares = [column[4 + 3 * q : 7 + 3 * q] for q in range(4)]
    scale = column[16]
    normed_grad = parts[0][...].astype(F32)
    for part in parts[1:]:
        normed_grad = normed_grad + part[...].astype(F32)
    tokens = tok_ref[...]
    scaled = gain_ref[...] * normed_grad
    inner = jnp.mean(tokens * scaled, axis=1, keepdims=True)
    token_grad = cot_ref[...].astype(F32) + scale * scaled - tokens * (scale * scale * scale * inner)
    dots = [jnp.sum(token_grad * v, axis=1, keepdims=True) for v in values]
    pairs = [dots[0] + dots[1], dots[2] + dots[3]]
    four = 0.0625 * (pairs[0] + pairs[1])
    score_grads = []
    for q in range(4):
        share = shares[q]
        grads = (0.25 * dots[q], 0.125 * pairs[q // 2], four)
        average = share[0] * grads[0] + share[1] * grads[1] + share[2] * grads[2]
        score_grads.append([s * (g - average) for s, g in zip(share, grads)])
    all_four = 0.25 * (score_grads[0][2] + score_grads[1][2] + score_grads[2][2] + score_grads[3][2])
    weight = score_ref[...]
    ordered = []
    for q in range(4):
        pair = 0.5 * (score_grads[q][1] + score_grads[q ^ 1][1])
        slope = score_grads[q][0] + pair + all_four
        ordered.append((coefs[q] * token_grad + slope * weight).astype(BF))
    out_ref[...] = lax.dot_general(
        quartet_order(count), jnp.concatenate(ordered, axis=0), ROWS_T, preferred_element_type=F32
    ).astype(BF)


def per_device(byte_embed, score_weight, norm_gain, router, routes, expert_in, expert_out, cotangent):
    experts = router.shape[1]
    count = routes.shape[1]
    width = byte_embed.shape[2]
    full = width + LANES
    capacity = max(2, 3 * count // experts)
    pieces = lax.axis_size("seq")
    owners = lax.axis_size("exp")
    chunks = owners // 2
    rows = 2 * pieces * capacity
    slots = chunks * rows
    tokens = pieces * count
    hidden = expert_in.shape[2]
    tile = min(256, hidden)
    my = lax.axis_index("exp").astype(jnp.int32).reshape(1)
    embed = byte_embed[0]
    cot = cotangent[0]
    score_row = score_weight.reshape(1, width)
    gain_row = norm_gain.reshape(1, width)
    router_t = router.T
    routes_t = routes[0].T
    weight_in = expert_in[0]
    weight_out = expert_out[0]

    def shape(*dims, dtype=BF):
        return jax.ShapeDtypeStruct(dims, dtype)

    def over_seq(value, k):
        return lax.ppermute(value, "seq", [(i, i ^ k) for i in range(pieces)])

    def over_exp(values, step):
        moved = list(values)
        for m in sorted(range(1, len(values)), key=lambda m: (m & (2 // step - 1), -m)):
            moved[m] = lax.ppermute(values[m], "exp", [(i, i ^ (m * step)) for i in range(owners)])
        return moved

    def over_cores(value):
        return lax.ppermute(value, "exp", [(i, i ^ 1) for i in range(owners)])

    half = pieces // 2
    places = list(range(0, pieces, 2)) + list(range(1, pieces, 2))
    front_args = (embed, score_row, gain_row, router_t, routes_t)
    cot_far = [over_seq(cot, k) for k in places[1:half]]
    pay = call(
        front_kernel,
        "front",
        shape(count, full),
        front_args,
        us=2.0,
        scratch=[pltpu.VMEM((count, LANES), F32)],
        limit=56,
        held=False,
    )
    tok, keep = call(
        keep_kernel,
        "keep",
        (shape(count, width, dtype=F32), shape(count, LANES, dtype=F32)),
        (embed, score_row),
        us=2.0,
    )
    held_cot = call(functools.partial(gather_kernel, 0), "hold_cot", shape(count, width), (cot,), us=1.0)
    cot_near = call(
        functools.partial(gather_kernel, 0), "cot_near", shape(half * count, width), (held_cot, *cot_far), us=5.0
    )
    held = call(functools.partial(gather_kernel, 0), "hold_own", shape(count, full), (pay,), us=1.0)
    in_across = call(transpose_kernel, "across", shape(hidden, width), (weight_in,), us=2.0, limit=16)
    out_across = call(transpose_kernel, "across", shape(width, hidden), (weight_out,), us=2.0, limit=16)
    token_near = call(
        functools.partial(gather_kernel, 1),
        "token_near",
        shape(tokens, full),
        (cot_near, held, *[over_seq(pay, k) for k in places[1:]]),
    )
    cot_other, token_other = over_cores(cot_near), over_cores(token_near)
    cot_chosen = call(
        functools.partial(cot_pick_kernel, pieces, capacity),
        "cot_pick",
        [shape(rows // 2, width)] * chunks,
        (my, cot_near, token_near, cot_other, token_other),
        scalars=1,
        limit=16,
    )
    cot_chunks = over_exp(cot_chosen, 2)
    *chosen, pick = call(
        functools.partial(token_pick_kernel, pieces, capacity, 1),
        "token_pick",
        [shape(rows, full)] * chunks + [shape(slots, 2 * tokens)],
        (my, cot_chosen[0], token_near, token_other),
        scalars=1,
        limit=16,
    )
    token_chunks = over_exp(chosen, 2)
    order = [0, *range(chunks - 1, 0, -1)]
    groups = (order[: chunks // 2], order[chunks // 2 :])
    part = slots // 2
    near, far, upstream = [], [], []
    for group in groups:
        cot_a = call(
            functools.partial(gather_kernel, 0), "cot_slots", shape(part // 2, width), [cot_chunks[m] for m in group]
        )
        near.append(cot_a)
        far.append(over_seq(cot_a, 1))
    hiddens, upstream = [], []
    for cot_a, cot_b in zip(near, far):
        upstream.append(
            call(
                functools.partial(upstream_kernel, chunks, 0),
                "upstream",
                shape(part, hidden, dtype=F32),
                (cot_a, cot_b, out_across),
                limit=16,
            )
        )
    for g, group in enumerate(groups):
        waits = upstream[1:] if g else []
        hiddens.append(
            call(
                functools.partial(hidden_kernel, len(group), tile, len(waits)),
                "hidden",
                (shape(part, width), shape(part, LANES), shape(part, hidden), shape(part, hidden, dtype=F32)),
                (*waits, *[token_chunks[m] for m in group], weight_in),
                limit=16,
                us=1.0,
            )
        )
    stacked, back_rows = [], [None] * chunks
    for g, group in enumerate(groups):
        waits = upstream[1:] if g == 0 else []
        token_rows, tail, hidden_rows, slope = hiddens[g]
        *outs, hidden_grad = call(
            functools.partial(grad_kernel, len(group), len(waits)),
            "grads",
            [shape(rows, width)] * len(group) + [shape(part, hidden)],
            (my, *waits, hidden_rows, slope, tail, upstream[g], in_across, router_t),
            scalars=1,
            limit=16,
        )
        for m, out in zip(group, outs):
            back_rows[m] = out
        stacked += [near[g], far[g], hidden_rows, token_rows, hidden_grad]
    cot_slots, hidden_rows, token_slots, hidden_grad = call(
        functools.partial(stack_kernel, chunks),
        "stack",
        (shape(slots, width), shape(slots, hidden), shape(slots, width), shape(slots, hidden)),
        stacked,
        limit=16,
    )
    grad_out = lax.dot_general(hidden_rows, cot_slots, ROWS_T, preferred_element_type=F32)
    grad_in = lax.dot_general(token_slots, hidden_grad, ROWS_T, preferred_element_type=F32)
    returned = over_exp(back_rows, 2)
    *returned, grad_out = lax.optimization_barrier((*returned, grad_out))
    other_rows = call(combine_other_kernel, "combine_other", shape(tokens, width), (pick, *returned), limit=16)
    partial_rows = call(
        functools.partial(combine_own_kernel, chunks),
        "combine_own",
        [shape(count, width)] * pieces,
        (pick, *returned, over_cores(other_rows)),
        limit=16,
    )
    parts = [partial_rows[0]] + [over_seq(partial_rows[i], places[i]) for i in range(pieces - 1, 0, -1)]
    embed_grad = call(
        functools.partial(back_kernel, pieces),
        "back",
        shape(4 * count, width),
        (embed, score_row, gain_row, tok, keep, cot, *parts),
    )
    return (embed_grad[None], grad_in[None], grad_out[None])


def solution(mesh):
    in_specs = (
        P("exp", "seq", None),
        P(),
        P(),
        P(),
        P("exp", "seq", None),
        P("exp", None, "seq"),
        P("exp", "seq", None),
        P("exp", "seq", None),
    )
    out_specs = (P("exp", "seq", None), P("exp", None, "seq"), P("exp", "seq", None))
    return jax.shard_map(
        per_device, mesh=mesh, in_specs=in_specs, out_specs=out_specs, check_vma=False
    )
```

```python
import functools
import jax
import jax.numpy as jnp
from jax import lax
from jax.experimental import pallas as pl
from jax.experimental.pallas import tpu as pltpu
from jax.sharding import PartitionSpec as P

SQRT_HALF = 0.7071067811865476
INV_ROOT_TWO_PI = 0.3989422804014327
LANES = 128
GROUP = LANES // 4
BF = jnp.bfloat16
F32 = jnp.float32
HIGHEST = lax.Precision.HIGHEST
ROWS_T = (((0,), (0,)), ((), ()))
COLS = (((1,), (1,)), ((), ()))
MIB = 1024 * 1024
BYTES_PER_US = 3_000_000


def call(body, name, outs, args, us=0.0, scratch=(), limit=8, scalars=0, held=True):
    vmem = pl.BlockSpec(memory_space=pltpu.VMEM)
    smem = pl.BlockSpec(memory_space=pltpu.SMEM)
    rest = vmem if held else pl.BlockSpec()
    return pl.pallas_call(
        body,
        name=name,
        out_shape=outs,
        in_specs=[smem] * scalars + [rest] * (len(args) - scalars),
        out_specs=jax.tree.map(lambda _: vmem, outs),
        scratch_shapes=list(scratch),
        compiler_params=pltpu.CompilerParams(vmem_limit_bytes=limit * MIB),
        cost_estimate=pl.CostEstimate(flops=0, bytes_accessed=int(us * BYTES_PER_US), transcendentals=0),
    )(*args)


def route_mask(routes_t, k):
    count = routes_t.shape[1]
    lane = lax.broadcasted_iota(jnp.int32, (LANES, count), 0) % GROUP
    mask_t = (lane == routes_t[k : k + 1, :]).astype(F32).astype(BF)
    row = lax.broadcasted_iota(jnp.int32, (count, count), 0)
    col = lax.broadcasted_iota(jnp.int32, (count, count), 1)
    eye = (row == col).astype(F32).astype(BF)
    return lax.dot_general(eye, mask_t, COLS, preferred_element_type=F32)


def quartet_order(count):
    row = lax.broadcasted_iota(jnp.int32, (4 * count, 4 * count), 0)
    col = lax.broadcasted_iota(jnp.int32, (4 * count, 4 * count), 1)
    return (4 * (row % count) + row // count == col).astype(F32).astype(BF)


def quartet_values(embed, count):
    ordered = jnp.dot(quartet_order(count), embed, preferred_element_type=F32)
    return [ordered[q * count : (q + 1) * count, :] for q in range(4)]


def quartet_scores(values, weight):
    ones = [jnp.sum(v * weight, axis=1, keepdims=True) for v in values]
    pairs = [0.5 * (ones[0] + ones[1]), 0.5 * (ones[2] + ones[3])]
    four = 0.5 * (pairs[0] + pairs[1])
    shares = []
    for q in range(4):
        scores = (ones[q], pairs[q // 2], four)
        largest = jnp.maximum(jnp.maximum(scores[0], scores[1]), scores[2])
        weights = [jnp.exp(s - largest) for s in scores]
        denominator = weights[0] + weights[1] + weights[2]
        shares.append([w / denominator for w in weights])
    return shares


def pooled(values, weight):
    shares = quartet_scores(values, weight)
    whole = 0.25 * (shares[0][2] + shares[1][2] + shares[2][2] + shares[3][2])
    coefs = []
    for q in range(4):
        pair = 0.5 * (shares[q][1] + shares[q ^ 1][1])
        coefs.append(0.25 * (shares[q][0] + pair + whole))
    tokens = coefs[0] * values[0] + coefs[1] * values[1] + coefs[2] * values[2] + coefs[3] * values[3]
    scale = lax.rsqrt(jnp.mean(tokens * tokens, axis=1, keepdims=True) + 1e-06)
    return shares, coefs, tokens, scale


def front_kernel(embed_ref, score_ref, gain_ref, router_ref, routes_ref, pay_ref, logit):
    count = pay_ref.shape[0]
    experts, width = router_ref.shape
    _, _, tokens, scale = pooled(quartet_values(embed_ref[...], count), score_ref[...])
    normed = tokens * scale * gain_ref[...]
    high = normed.astype(BF)
    rest = normed - high.astype(F32)
    middle = rest.astype(BF)
    low = (rest - middle.astype(F32)).astype(BF)
    products = lax.dot_general(
        jnp.concatenate([high, middle, low], axis=0), router_ref[...], COLS, preferred_element_type=F32
    )
    logit[...] = jnp.zeros_like(logit)
    logit[:, :experts] = products[:count, :] + (products[count : 2 * count, :] + products[2 * count :, :])
    logits = logit[...]
    sigmoid = 1.0 / (1.0 + jnp.exp(-logits))
    rest = 1.0 / (1.0 + jnp.exp(logits))
    routes_t = routes_ref[...]
    masks = [route_mask(routes_t, k) for k in range(2)]
    group = lax.broadcasted_iota(jnp.int32, masks[0].shape, 1) // GROUP
    once = [jnp.where(group == 0, m, 0.0) for m in masks]
    picked = [jnp.sum(m * sigmoid, axis=1, keepdims=True) for m in once]
    others = [jnp.sum(m * rest, axis=1, keepdims=True) for m in once]
    total = picked[0] + picked[1]
    tail = jnp.zeros_like(masks[0])
    for mask, sig, other in zip(masks, picked, others):
        value = jnp.where(group == 0, 1.0, jnp.where(group == 1, other, jnp.where(group == 2, sig / total, 0.0)))
        tail = tail + mask * value
    pay_ref[:, :width] = high
    pay_ref[:, width:] = tail.astype(BF)


def keep_kernel(embed_ref, score_ref, values_ref, tok_ref, keep_ref):
    count = tok_ref.shape[0]
    values = quartet_values(embed_ref[...], count)
    values_ref[...] = jnp.concatenate([v.astype(BF) for v in values], axis=0)
    shares, coefs, tokens, scale = pooled(values, score_ref[...])
    tok_ref[...] = tokens
    columns = coefs + [s for share in shares for s in share] + [scale]
    lane = lax.broadcasted_iota(jnp.int32, keep_ref.shape, 1)
    kept = jnp.zeros(keep_ref.shape, F32)
    for i, column in enumerate(columns):
        kept = jnp.where(lane == i, column, kept)
    keep_ref[...] = kept


def transpose_kernel(in_ref, out_ref):
    out_ref[...] = in_ref[...].T


def gather_kernel(skipped, *refs):
    ins, out_ref = refs[skipped:-1], refs[-1]
    at = 0
    for r in ins:
        out_ref[at : at + r.shape[0], :] = r[...]
        at += r.shape[0]


def slot_places(tail, columns, count, capacity, my):
    tokens = tail.shape[0]
    at = lax.broadcasted_iota(jnp.int32, (LANES, LANES), 0)
    lane = lax.broadcasted_iota(jnp.int32, (LANES, LANES), 1)
    named_lane = (2 * (at % GROUP)) ^ my
    named_lane = jnp.where(at < GROUP, named_lane, named_lane + 2 * GROUP)
    live = (at % GROUP < columns) & (at < 2 * GROUP)
    order = ((lane == named_lane) & live).astype(F32).astype(BF)
    row = lax.broadcasted_iota(jnp.int32, (tokens, tokens), 0)
    col = lax.broadcasted_iota(jnp.int32, (tokens, tokens), 1)
    before = ((row < col) & (row // count == col // count)).astype(F32).astype(BF)
    ordered_t = lax.dot_general(order, tail, COLS, preferred_element_type=F32)
    named_t = ordered_t[:GROUP, :]
    place_t = jnp.dot(named_t.astype(BF), before, preferred_element_type=F32)
    block = lax.broadcasted_iota(jnp.int32, (GROUP, tokens), 1) // count
    place_t = place_t + (block * capacity).astype(F32)
    return jnp.where(named_t > 0.5, place_t, -1.0), ordered_t[GROUP : 2 * GROUP, :]


def selection(places, values, columns, rows):
    slot = lax.broadcasted_iota(jnp.int32, (rows, places.shape[1]), 0).astype(F32)
    picks = [jnp.where(places[m : m + 1, :] == slot, values[m : m + 1, :], 0.0) for m in range(columns)]
    return jnp.concatenate(picks, axis=0).astype(BF)


def near_kernel(cots, *refs):
    ins, out_ref = refs[:-1], refs[-1]
    count, width = ins[0].shape
    for i, r in enumerate(ins):
        at = slice(i * count, (i + 1) * count)
        if i < cots:
            out_ref[at, :width] = r[...]
            out_ref[at, width:] = jnp.zeros((count, out_ref.shape[1] - width), BF)
        else:
            out_ref[at, :] = r[...]


def cot_pick_kernel(near, count, capacity, my_ref, own_ref, other_ref, *outs):
    cots = near * count
    width = own_ref.shape[1] - LANES
    tail = jnp.concatenate([r[cots : 2 * cots, width:] for r in (own_ref, other_ref)], axis=0)
    places, gates = slot_places(tail, len(outs), count, capacity, my_ref[0])
    picks = selection(places, gates, len(outs), 2 * near * capacity)
    cot_rows = jnp.concatenate([r[:cots, :width] for r in (own_ref, other_ref)], axis=0)
    chosen = jnp.dot(picks, cot_rows, preferred_element_type=F32).astype(BF)
    for m, out in enumerate(outs):
        out[...] = chosen[m * out.shape[0] : (m + 1) * out.shape[0], :]


def token_pick_kernel(near, count, capacity, waits, my_ref, *refs):
    own_ref, other_ref, *outs, pick_ref = refs[waits:]
    full = own_ref.shape[1]
    pieces = 2 * near
    rows = jnp.concatenate([r[near * count :, :] for r in (own_ref, other_ref)], axis=0)
    places, gates = slot_places(rows[:, full - LANES :], len(outs), count, capacity, my_ref[0])
    pick_ref[...] = selection(places, jnp.ones_like(gates), len(outs), 2 * pieces * capacity)
    chosen = jnp.dot(pick_ref[...], rows, preferred_element_type=F32).astype(BF)
    for m, out in enumerate(outs):
        out[...] = chosen[m * out.shape[0] : (m + 1) * out.shape[0], :]


def interleave(near, far, owners):
    share = near.shape[0] // owners
    return jnp.concatenate([r[d * share : (d + 1) * share, :] for d in range(owners) for r in (near, far)], axis=0)


def upstream_kernel(owners, waits, *refs):
    near_ref, far_ref, weight_ref, out_ref = refs[waits:]
    rows = jnp.concatenate([near_ref[...], far_ref[...]], axis=0)
    upstream = jnp.dot(rows, weight_ref[...], preferred_element_type=F32)
    half = near_ref.shape[0]
    out_ref[...] = interleave(upstream[:half, :], upstream[half:, :], owners)


def hidden_kernel(chunks, tile, waits, *refs):
    refs = refs[waits:]
    ins, (weight_ref, rows_ref, tail_ref, hidden_ref, slope_ref) = refs[:chunks], refs[chunks:]
    width = rows_ref.shape[1]
    token_rows = jnp.concatenate([r[:, :width] for r in ins], axis=0)
    rows_ref[...] = token_rows
    tail_ref[...] = jnp.concatenate([r[:, width:] for r in ins], axis=0)
    for f in range(weight_ref.shape[1] // tile):
        part = slice(f * tile, (f + 1) * tile)
        preact = jnp.dot(token_rows, weight_ref[:, part], preferred_element_type=F32)
        normal_cdf = 0.5 * (1.0 + lax.erf(preact * SQRT_HALF))
        normal_pdf = INV_ROOT_TWO_PI * jnp.exp(-0.5 * preact * preact)
        hidden_ref[:, part] = (preact * normal_cdf).astype(BF)
        slope_ref[:, part] = normal_cdf + preact * normal_pdf


def grad_kernel(chunks, waits, my_ref, *refs):
    hidden_ref, slope_ref, tail_ref, upstream_ref, weight_ref, router_ref = refs[waits : waits + 6]
    outs, grad_ref = refs[waits + 6 : -1], refs[-1]
    slots = hidden_ref.shape[0]
    experts, width = router_ref.shape
    rows = slots // chunks
    terms = jnp.zeros((slots, LANES), F32)
    for k in range(hidden_ref.shape[1] // LANES):
        part = slice(k * LANES, (k + 1) * LANES)
        upstream = upstream_ref[:, part]
        terms = terms + hidden_ref[:, part].astype(F32) * upstream
        grad_ref[:, part] = (upstream * slope_ref[:, part]).astype(BF)
    term = jnp.sum(terms, axis=1, keepdims=True)
    tail = tail_ref[...].astype(F32)
    lane = lax.broadcasted_iota(jnp.int32, (slots, LANES), 1)
    mine = lane % GROUP == my_ref[0]
    other_gate = jnp.sum(jnp.where((lane // GROUP == 2) & ~mine, tail, 0.0), axis=1, keepdims=True)
    spread = jnp.where(lane // GROUP == 1, jnp.where(mine, tail, -tail), 0.0) * (term * other_gate)
    high = spread.astype(BF)
    low = (spread - high.astype(F32)).astype(BF)
    router = router_ref[...].astype(F32)
    blank = jnp.zeros((GROUP, width), F32)
    padded = [router] if experts == GROUP else [router, jnp.zeros((GROUP - experts, width), F32)]
    router = jnp.concatenate([blank, *padded, blank, blank], axis=0).astype(BF)
    back = jnp.dot(grad_ref[...], weight_ref[...], preferred_element_type=F32)
    back = back + jnp.dot(high, router, preferred_element_type=F32) + jnp.dot(low, router, preferred_element_type=F32)
    back = back.astype(BF)
    for m, out in enumerate(outs):
        out[...] = back[m * rows : (m + 1) * rows, :]


def stack_kernel(owners, *refs):
    ins, outs = refs[:-4], refs[-4:]
    cots = [interleave(a[...].astype(F32), b[...].astype(F32), owners) for a, b in zip(ins[::5], ins[1::5])]
    outs[0][...] = jnp.concatenate(cots, axis=0).astype(BF)
    for i, out in enumerate(outs[1:]):
        out[...] = jnp.concatenate([r[...] for r in ins[2 + i :: 5]], axis=0)


def combine_other_kernel(pick_ref, *refs):
    ins, out_ref = refs[:-1], refs[-1]
    tokens = out_ref.shape[0]
    rows = jnp.concatenate([r[...] for r in ins], axis=0)
    out_ref[...] = lax.dot_general(pick_ref[:, tokens:], rows, ROWS_T, preferred_element_type=F32).astype(BF)


def combine_own_kernel(chunks, pick_ref, *refs):
    ins, other_ref, outs = refs[:chunks], refs[chunks], refs[chunks + 1 :]
    tokens = other_ref.shape[0]
    count = outs[0].shape[0]
    rows = jnp.concatenate([r[...] for r in ins], axis=0)
    back = lax.dot_general(pick_ref[:, :tokens], rows, ROWS_T, preferred_element_type=F32)
    back = (back + other_ref[...].astype(F32)).astype(BF)
    for k, out in enumerate(outs):
        out[...] = back[k * count : (k + 1) * count, :]


def back_kernel(pieces, ordered_ref, score_ref, gain_ref, tok_ref, keep_ref, cot_ref, *refs):
    parts, out_ref = refs[:pieces], refs[pieces]
    count, width = tok_ref.shape
    values = [ordered_ref[q * count : (q + 1) * count, :].astype(F32) for q in range(4)]
    kept = keep_ref[...]
    column = [kept[:, i : i + 1] for i in range(17)]
    coefs = column[:4]
    shares = [column[4 + 3 * q : 7 + 3 * q] for q in range(4)]
    scale = column[16]
    normed_grad = parts[0][...].astype(F32)
    for part in parts[1:]:
        normed_grad = normed_grad + part[...].astype(F32)
    tokens = tok_ref[...]
    scaled = gain_ref[...] * normed_grad
    inner = jnp.mean(tokens * scaled, axis=1, keepdims=True)
    token_grad = cot_ref[...].astype(F32) + scale * scaled - tokens * (scale * scale * scale * inner)
    dots = [jnp.sum(token_grad * v, axis=1, keepdims=True) for v in values]
    pairs = [dots[0] + dots[1], dots[2] + dots[3]]
    four = 0.0625 * (pairs[0] + pairs[1])
    score_grads = []
    for q in range(4):
        share = shares[q]
        grads = (0.25 * dots[q], 0.125 * pairs[q // 2], four)
        average = share[0] * grads[0] + share[1] * grads[1] + share[2] * grads[2]
        score_grads.append([s * (g - average) for s, g in zip(share, grads)])
    all_four = 0.25 * (score_grads[0][2] + score_grads[1][2] + score_grads[2][2] + score_grads[3][2])
    weight = score_ref[...]
    ordered = []
    for q in range(4):
        pair = 0.5 * (score_grads[q][1] + score_grads[q ^ 1][1])
        slope = score_grads[q][0] + pair + all_four
        ordered.append((coefs[q] * token_grad + slope * weight).astype(BF))
    out_ref[...] = lax.dot_general(
        quartet_order(count), jnp.concatenate(ordered, axis=0), ROWS_T, preferred_element_type=F32
    ).astype(BF)


def per_device(byte_embed, score_weight, norm_gain, router, routes, expert_in, expert_out, cotangent):
    experts = router.shape[1]
    count = routes.shape[1]
    width = byte_embed.shape[2]
    full = width + LANES
    capacity = max(2, 3 * count // experts)
    pieces = lax.axis_size("seq")
    owners = lax.axis_size("exp")
    chunks = owners // 2
    rows = 2 * pieces * capacity
    slots = chunks * rows
    tokens = pieces * count
    hidden = expert_in.shape[2]
    tile = min(256, hidden)
    my = lax.axis_index("exp").astype(jnp.int32).reshape(1)
    embed = byte_embed[0]
    cot = cotangent[0]
    score_row = score_weight.reshape(1, width)
    gain_row = norm_gain.reshape(1, width)
    router_t = router.T
    routes_t = routes[0].T
    weight_in = expert_in[0]
    weight_out = expert_out[0]

    def shape(*dims, dtype=BF):
        return jax.ShapeDtypeStruct(dims, dtype)

    def over_seq(value, k):
        return lax.ppermute(value, "seq", [(i, i ^ k) for i in range(pieces)])

    def over_exp(values, step):
        moved = list(values)
        for m in sorted(range(1, len(values)), key=lambda m: (m & (2 // step - 1), -m)):
            moved[m] = lax.ppermute(values[m], "exp", [(i, i ^ (m * step)) for i in range(owners)])
        return moved

    def over_cores(value):
        return lax.ppermute(value, "exp", [(i, i ^ 1) for i in range(owners)])

    half = pieces // 2
    places = list(range(0, pieces, 2)) + list(range(1, pieces, 2))
    front_args = (embed, score_row, gain_row, router_t, routes_t)
    cot_far = [over_seq(cot, k) for k in places[1:half]]
    pay = call(
        front_kernel,
        "front",
        shape(count, full),
        front_args,
        us=2.0,
        scratch=[pltpu.VMEM((count, LANES), F32)],
        limit=56,
        held=False,
    )
    ordered, tok, keep = call(
        keep_kernel,
        "keep",
        (shape(4 * count, width), shape(count, width, dtype=F32), shape(count, LANES, dtype=F32)),
        (embed, score_row),
        us=2.0,
    )
    held_cot = call(functools.partial(gather_kernel, 0), "hold_cot", shape(count, width), (cot,), us=1.0)
    held = call(functools.partial(gather_kernel, 0), "hold_own", shape(count, full), (pay,), us=1.0)
    in_across = call(transpose_kernel, "across", shape(hidden, width), (weight_in,), us=2.0, limit=16)
    out_across = call(transpose_kernel, "across", shape(width, hidden), (weight_out,), us=2.0, limit=16)
    near = call(
        functools.partial(near_kernel, half),
        "near",
        shape(half * count + tokens, full),
        (held_cot, *cot_far, held, *[over_seq(pay, k) for k in places[1:]]),
    )
    other = over_cores(near)
    cot_chosen = call(
        functools.partial(cot_pick_kernel, half, count, capacity),
        "cot_pick",
        [shape(rows // 2, width)] * chunks,
        (my, near, other),
        scalars=1,
        limit=16,
    )
    cot_chunks = over_exp(cot_chosen, 2)
    *chosen, pick = call(
        functools.partial(token_pick_kernel, half, count, capacity, 1),
        "token_pick",
        [shape(rows, full)] * chunks + [shape(slots, 2 * tokens)],
        (my, cot_chosen[0], near, other),
        scalars=1,
        limit=16,
    )
    token_chunks = over_exp(chosen, 2)
    order = [0, *range(chunks - 1, 0, -1)]
    groups = (order[: chunks // 2], order[chunks // 2 :])
    part = slots // 2
    near, far, upstream = [], [], []
    for group in groups:
        cot_a = call(
            functools.partial(gather_kernel, 0), "cot_slots", shape(part // 2, width), [cot_chunks[m] for m in group]
        )
        near.append(cot_a)
        far.append(over_seq(cot_a, 1))
    hiddens, upstream = [], []
    for cot_a, cot_b in zip(near, far):
        upstream.append(
            call(
                functools.partial(upstream_kernel, chunks, 0),
                "upstream",
                shape(part, hidden, dtype=F32),
                (cot_a, cot_b, out_across),
                limit=16,
            )
        )
    for g, group in enumerate(groups):
        waits = upstream[1:] if g else []
        hiddens.append(
            call(
                functools.partial(hidden_kernel, len(group), tile, len(waits)),
                "hidden",
                (shape(part, width), shape(part, LANES), shape(part, hidden), shape(part, hidden, dtype=F32)),
                (*waits, *[token_chunks[m] for m in group], weight_in),
                limit=16,
                us=1.0,
            )
        )
    stacked, back_rows = [], [None] * chunks
    for g, group in enumerate(groups):
        waits = upstream[1:] if g == 0 else []
        token_rows, tail, hidden_rows, slope = hiddens[g]
        *outs, hidden_grad = call(
            functools.partial(grad_kernel, len(group), len(waits)),
            "grads",
            [shape(rows, width)] * len(group) + [shape(part, hidden)],
            (my, *waits, hidden_rows, slope, tail, upstream[g], in_across, router_t),
            scalars=1,
            limit=16,
        )
        for m, out in zip(group, outs):
            back_rows[m] = out
        stacked += [near[g], far[g], hidden_rows, token_rows, hidden_grad]
    cot_slots, hidden_rows, token_slots, hidden_grad = call(
        functools.partial(stack_kernel, chunks),
        "stack",
        (shape(slots, width), shape(slots, hidden), shape(slots, width), shape(slots, hidden)),
        stacked,
        limit=16,
    )
    grad_out = lax.dot_general(hidden_rows, cot_slots, ROWS_T, preferred_element_type=F32)
    grad_in = lax.dot_general(token_slots, hidden_grad, ROWS_T, preferred_element_type=F32)
    returned = over_exp(back_rows, 2)
    *returned, grad_out = lax.optimization_barrier((*returned, grad_out))
    other_rows = call(combine_other_kernel, "combine_other", shape(tokens, width), (pick, *returned), limit=16)
    partial_rows = call(
        functools.partial(combine_own_kernel, chunks),
        "combine_own",
        [shape(count, width)] * pieces,
        (pick, *returned, over_cores(other_rows)),
        limit=16,
    )
    parts = [partial_rows[0]] + [over_seq(partial_rows[i], places[i]) for i in range(pieces - 1, 0, -1)]
    embed_grad = call(
        functools.partial(back_kernel, pieces),
        "back",
        shape(4 * count, width),
        (ordered, score_row, gain_row, tok, keep, cot, *parts),
    )
    return (embed_grad[None], grad_in[None], grad_out[None])


def solution(mesh):
    in_specs = (
        P("exp", "seq", None),
        P(),
        P(),
        P(),
        P("exp", "seq", None),
        P("exp", None, "seq"),
        P("exp", "seq", None),
        P("exp", "seq", None),
    )
    out_specs = (P("exp", "seq", None), P("exp", None, "seq"), P("exp", "seq", None))
    return jax.shard_map(
        per_device, mesh=mesh, in_specs=in_specs, out_specs=out_specs, check_vma=False
    )
```

```python
import functools
import jax
import jax.numpy as jnp
from jax import lax
from jax.experimental import pallas as pl
from jax.experimental.pallas import tpu as pltpu
from jax.sharding import PartitionSpec as P

SQRT_HALF = 0.7071067811865476
INV_ROOT_TWO_PI = 0.3989422804014327
LANES = 128
GROUP = LANES // 4
BF = jnp.bfloat16
F32 = jnp.float32
HIGHEST = lax.Precision.HIGHEST
ROWS_T = (((0,), (0,)), ((), ()))
COLS = (((1,), (1,)), ((), ()))
MIB = 1024 * 1024
BYTES_PER_US = 3_000_000


def call(body, name, outs, args, us=0.0, scratch=(), limit=8, scalars=0, held=True):
    vmem = pl.BlockSpec(memory_space=pltpu.VMEM)
    smem = pl.BlockSpec(memory_space=pltpu.SMEM)
    rest = vmem if held else pl.BlockSpec()
    return pl.pallas_call(
        body,
        name=name,
        out_shape=outs,
        in_specs=[smem] * scalars + [rest] * (len(args) - scalars),
        out_specs=jax.tree.map(lambda _: vmem, outs),
        scratch_shapes=list(scratch),
        compiler_params=pltpu.CompilerParams(vmem_limit_bytes=limit * MIB),
        cost_estimate=pl.CostEstimate(flops=0, bytes_accessed=int(us * BYTES_PER_US), transcendentals=0),
    )(*args)


def route_mask(routes_t, k):
    count = routes_t.shape[1]
    lane = lax.broadcasted_iota(jnp.int32, (LANES, count), 0) % GROUP
    mask_t = (lane == routes_t[k : k + 1, :]).astype(F32).astype(BF)
    row = lax.broadcasted_iota(jnp.int32, (count, count), 0)
    col = lax.broadcasted_iota(jnp.int32, (count, count), 1)
    eye = (row == col).astype(F32).astype(BF)
    return lax.dot_general(eye, mask_t, COLS, preferred_element_type=F32)


def quartet_order(count):
    row = lax.broadcasted_iota(jnp.int32, (4 * count, 4 * count), 0)
    col = lax.broadcasted_iota(jnp.int32, (4 * count, 4 * count), 1)
    return (4 * (row % count) + row // count == col).astype(F32).astype(BF)


def quartet_values(embed, count):
    ordered = jnp.dot(quartet_order(count), embed, preferred_element_type=F32)
    return [ordered[q * count : (q + 1) * count, :] for q in range(4)]


def quartet_scores(values, weight):
    ones = [jnp.sum(v * weight, axis=1, keepdims=True) for v in values]
    pairs = [0.5 * (ones[0] + ones[1]), 0.5 * (ones[2] + ones[3])]
    four = 0.5 * (pairs[0] + pairs[1])
    shares = []
    for q in range(4):
        scores = (ones[q], pairs[q // 2], four)
        largest = jnp.maximum(jnp.maximum(scores[0], scores[1]), scores[2])
        weights = [jnp.exp(s - largest) for s in scores]
        denominator = weights[0] + weights[1] + weights[2]
        shares.append([w / denominator for w in weights])
    return shares


def pooled(values, weight):
    shares = quartet_scores(values, weight)
    whole = 0.25 * (shares[0][2] + shares[1][2] + shares[2][2] + shares[3][2])
    coefs = []
    for q in range(4):
        pair = 0.5 * (shares[q][1] + shares[q ^ 1][1])
        coefs.append(0.25 * (shares[q][0] + pair + whole))
    tokens = coefs[0] * values[0] + coefs[1] * values[1] + coefs[2] * values[2] + coefs[3] * values[3]
    scale = lax.rsqrt(jnp.mean(tokens * tokens, axis=1, keepdims=True) + 1e-06)
    return shares, coefs, tokens, scale


def front_kernel(embed_ref, score_ref, gain_ref, router_ref, routes_ref, pay_ref, logit):
    count = pay_ref.shape[0]
    experts, width = router_ref.shape
    _, _, tokens, scale = pooled(quartet_values(embed_ref[...], count), score_ref[...])
    normed = tokens * scale * gain_ref[...]
    high = normed.astype(BF)
    rest = normed - high.astype(F32)
    middle = rest.astype(BF)
    low = (rest - middle.astype(F32)).astype(BF)
    products = lax.dot_general(
        jnp.concatenate([high, middle, low], axis=0), router_ref[...], COLS, preferred_element_type=F32
    )
    logit[...] = jnp.zeros_like(logit)
    logit[:, :experts] = products[:count, :] + (products[count : 2 * count, :] + products[2 * count :, :])
    logits = logit[...]
    sigmoid = 1.0 / (1.0 + jnp.exp(-logits))
    rest = 1.0 / (1.0 + jnp.exp(logits))
    routes_t = routes_ref[...]
    masks = [route_mask(routes_t, k) for k in range(2)]
    group = lax.broadcasted_iota(jnp.int32, masks[0].shape, 1) // GROUP
    once = [jnp.where(group == 0, m, 0.0) for m in masks]
    picked = [jnp.sum(m * sigmoid, axis=1, keepdims=True) for m in once]
    others = [jnp.sum(m * rest, axis=1, keepdims=True) for m in once]
    total = picked[0] + picked[1]
    tail = jnp.zeros_like(masks[0])
    for mask, sig, other in zip(masks, picked, others):
        value = jnp.where(group == 0, 1.0, jnp.where(group == 1, other, jnp.where(group == 2, sig / total, 0.0)))
        tail = tail + mask * value
    pay_ref[:, :width] = high
    pay_ref[:, width:] = tail.astype(BF)


def keep_kernel(embed_ref, score_ref, tok_ref, keep_ref):
    count = tok_ref.shape[0]
    shares, coefs, tokens, scale = pooled(quartet_values(embed_ref[...], count), score_ref[...])
    tok_ref[...] = tokens
    columns = coefs + [s for share in shares for s in share] + [scale]
    lane = lax.broadcasted_iota(jnp.int32, keep_ref.shape, 1)
    kept = jnp.zeros(keep_ref.shape, F32)
    for i, column in enumerate(columns):
        kept = jnp.where(lane == i, column, kept)
    keep_ref[...] = kept


def transpose_kernel(in_ref, out_ref):
    out_ref[...] = in_ref[...].T


def gather_kernel(skipped, *refs):
    ins, out_ref = refs[skipped:-1], refs[-1]
    at = 0
    for r in ins:
        out_ref[at : at + r.shape[0], :] = r[...]
        at += r.shape[0]


def slot_places(tail, columns, count, capacity, my):
    tokens = tail.shape[0]
    at = lax.broadcasted_iota(jnp.int32, (LANES, LANES), 0)
    lane = lax.broadcasted_iota(jnp.int32, (LANES, LANES), 1)
    named_lane = (2 * (at % GROUP)) ^ my
    named_lane = jnp.where(at < GROUP, named_lane, named_lane + 2 * GROUP)
    live = (at % GROUP < columns) & (at < 2 * GROUP)
    order = ((lane == named_lane) & live).astype(F32).astype(BF)
    row = lax.broadcasted_iota(jnp.int32, (tokens, tokens), 0)
    col = lax.broadcasted_iota(jnp.int32, (tokens, tokens), 1)
    before = ((row < col) & (row // count == col // count)).astype(F32).astype(BF)
    ordered_t = lax.dot_general(order, tail, COLS, preferred_element_type=F32)
    named_t = ordered_t[:GROUP, :]
    place_t = jnp.dot(named_t.astype(BF), before, preferred_element_type=F32)
    block = lax.broadcasted_iota(jnp.int32, (GROUP, tokens), 1) // count
    place_t = place_t + (block * capacity).astype(F32)
    return jnp.where(named_t > 0.5, place_t, -1.0), ordered_t[GROUP : 2 * GROUP, :]


def selection(places, values, columns, rows):
    slot = lax.broadcasted_iota(jnp.int32, (rows, places.shape[1]), 0).astype(F32)
    picks = [jnp.where(places[m : m + 1, :] == slot, values[m : m + 1, :], 0.0) for m in range(columns)]
    return jnp.concatenate(picks, axis=0).astype(BF)


def cot_pick_kernel(pieces, capacity, my_ref, cot_ref, token_ref, other_cot_ref, other_token_ref, *outs):
    tokens, full = token_ref.shape
    width = full - LANES
    count = tokens // pieces
    cots = cot_ref.shape[0]
    tail = jnp.concatenate([token_ref[:cots, width:], other_token_ref[:cots, width:]], axis=0)
    places, gates = slot_places(tail, len(outs), count, capacity, my_ref[0])
    picks = selection(places, gates, len(outs), 2 * (pieces // 2) * capacity)
    cot_rows = jnp.concatenate([cot_ref[...], other_cot_ref[...]], axis=0)
    chosen = jnp.dot(picks, cot_rows, preferred_element_type=F32).astype(BF)
    for m, out in enumerate(outs):
        out[...] = chosen[m * out.shape[0] : (m + 1) * out.shape[0], :]


def token_pick_kernel(pieces, capacity, waits, my_ref, *refs):
    token_ref, other_token_ref, *outs, pick_ref = refs[waits:]
    tokens, full = token_ref.shape
    rows = jnp.concatenate([token_ref[...], other_token_ref[...]], axis=0)
    places, gates = slot_places(rows[:, full - LANES :], len(outs), tokens // pieces, capacity, my_ref[0])
    pick_ref[...] = selection(places, jnp.ones_like(gates), len(outs), 2 * pieces * capacity)
    chosen = jnp.dot(pick_ref[...], rows, preferred_element_type=F32).astype(BF)
    for m, out in enumerate(outs):
        out[...] = chosen[m * out.shape[0] : (m + 1) * out.shape[0], :]


def interleave(near, far, owners):
    share = near.shape[0] // owners
    return jnp.concatenate([r[d * share : (d + 1) * share, :] for d in range(owners) for r in (near, far)], axis=0)


def upstream_kernel(owners, waits, *refs):
    near_ref, far_ref, weight_ref, out_ref = refs[waits:]
    rows = jnp.concatenate([near_ref[...], far_ref[...]], axis=0)
    upstream = jnp.dot(rows, weight_ref[...], preferred_element_type=F32)
    half = near_ref.shape[0]
    out_ref[...] = interleave(upstream[:half, :], upstream[half:, :], owners)


def hidden_kernel(chunks, tile, waits, *refs):
    refs = refs[waits:]
    ins, (weight_ref, rows_ref, tail_ref, hidden_ref, slope_ref) = refs[:chunks], refs[chunks:]
    width = rows_ref.shape[1]
    token_rows = jnp.concatenate([r[:, :width] for r in ins], axis=0)
    rows_ref[...] = token_rows
    tail_ref[...] = jnp.concatenate([r[:, width:] for r in ins], axis=0)
    for f in range(weight_ref.shape[1] // tile):
        part = slice(f * tile, (f + 1) * tile)
        preact = jnp.dot(token_rows, weight_ref[:, part], preferred_element_type=F32)
        normal_cdf = 0.5 * (1.0 + lax.erf(preact * SQRT_HALF))
        normal_pdf = INV_ROOT_TWO_PI * jnp.exp(-0.5 * preact * preact)
        hidden_ref[:, part] = (preact * normal_cdf).astype(BF)
        slope_ref[:, part] = normal_cdf + preact * normal_pdf


def grad_kernel(chunks, waits, my_ref, *refs):
    hidden_ref, slope_ref, tail_ref, upstream_ref, weight_ref, router_ref = refs[waits : waits + 6]
    outs, grad_ref = refs[waits + 6 : -1], refs[-1]
    slots = hidden_ref.shape[0]
    experts, width = router_ref.shape
    rows = slots // chunks
    terms = jnp.zeros((slots, LANES), F32)
    for k in range(hidden_ref.shape[1] // LANES):
        part = slice(k * LANES, (k + 1) * LANES)
        upstream = upstream_ref[:, part]
        terms = terms + hidden_ref[:, part].astype(F32) * upstream
        grad_ref[:, part] = (upstream * slope_ref[:, part]).astype(BF)
    term = jnp.sum(terms, axis=1, keepdims=True)
    tail = tail_ref[...].astype(F32)
    lane = lax.broadcasted_iota(jnp.int32, (slots, LANES), 1)
    mine = lane % GROUP == my_ref[0]
    other_gate = jnp.sum(jnp.where((lane // GROUP == 2) & ~mine, tail, 0.0), axis=1, keepdims=True)
    spread = jnp.where(lane // GROUP == 1, jnp.where(mine, tail, -tail), 0.0) * (term * other_gate)
    high = spread.astype(BF)
    low = (spread - high.astype(F32)).astype(BF)
    router = router_ref[...].astype(F32)
    blank = jnp.zeros((GROUP, width), F32)
    padded = [router] if experts == GROUP else [router, jnp.zeros((GROUP - experts, width), F32)]
    router = jnp.concatenate([blank, *padded, blank, blank], axis=0).astype(BF)
    back = jnp.dot(grad_ref[...], weight_ref[...], preferred_element_type=F32)
    back = back + jnp.dot(high, router, preferred_element_type=F32) + jnp.dot(low, router, preferred_element_type=F32)
    back = back.astype(BF)
    for m, out in enumerate(outs):
        out[...] = back[m * rows : (m + 1) * rows, :]


def stack_kernel(owners, *refs):
    ins, outs = refs[:-4], refs[-4:]
    cots = [interleave(a[...].astype(F32), b[...].astype(F32), owners) for a, b in zip(ins[::5], ins[1::5])]
    outs[0][...] = jnp.concatenate(cots, axis=0).astype(BF)
    for i, out in enumerate(outs[1:]):
        out[...] = jnp.concatenate([r[...] for r in ins[2 + i :: 5]], axis=0)


def combine_other_kernel(pick_ref, *refs):
    ins, out_ref = refs[:-1], refs[-1]
    tokens = out_ref.shape[0]
    rows = jnp.concatenate([r[...] for r in ins], axis=0)
    out_ref[...] = jnp.dot(pick_ref[tokens:, :], rows, preferred_element_type=F32).astype(BF)


def combine_own_kernel(chunks, pick_ref, *refs):
    ins, other_ref, outs = refs[:chunks], refs[chunks], refs[chunks + 1 :]
    tokens = other_ref.shape[0]
    count = outs[0].shape[0]
    rows = jnp.concatenate([r[...] for r in ins], axis=0)
    back = jnp.dot(pick_ref[:tokens, :], rows, preferred_element_type=F32)
    back = (back + other_ref[...].astype(F32)).astype(BF)
    for k, out in enumerate(outs):
        out[...] = back[k * count : (k + 1) * count, :]


def back_kernel(pieces, embed_ref, score_ref, gain_ref, tok_ref, keep_ref, cot_ref, *refs):
    parts, out_ref = refs[:pieces], refs[pieces]
    count, width = tok_ref.shape
    values = quartet_values(embed_ref[...], count)
    kept = keep_ref[...]
    column = [kept[:, i : i + 1] for i in range(17)]
    coefs = column[:4]
    shares = [column[4 + 3 * q : 7 + 3 * q] for q in range(4)]
    scale = column[16]
    normed_grad = parts[0][...].astype(F32)
    for part in parts[1:]:
        normed_grad = normed_grad + part[...].astype(F32)
    tokens = tok_ref[...]
    scaled = gain_ref[...] * normed_grad
    inner = jnp.mean(tokens * scaled, axis=1, keepdims=True)
    token_grad = cot_ref[...].astype(F32) + scale * scaled - tokens * (scale * scale * scale * inner)
    dots = [jnp.sum(token_grad * v, axis=1, keepdims=True) for v in values]
    pairs = [dots[0] + dots[1], dots[2] + dots[3]]
    four = 0.0625 * (pairs[0] + pairs[1])
    score_grads = []
    for q in range(4):
        share = shares[q]
        grads = (0.25 * dots[q], 0.125 * pairs[q // 2], four)
        average = share[0] * grads[0] + share[1] * grads[1] + share[2] * grads[2]
        score_grads.append([s * (g - average) for s, g in zip(share, grads)])
    all_four = 0.25 * (score_grads[0][2] + score_grads[1][2] + score_grads[2][2] + score_grads[3][2])
    weight = score_ref[...]
    ordered = []
    for q in range(4):
        pair = 0.5 * (score_grads[q][1] + score_grads[q ^ 1][1])
        slope = score_grads[q][0] + pair + all_four
        ordered.append((coefs[q] * token_grad + slope * weight).astype(BF))
    out_ref[...] = lax.dot_general(
        quartet_order(count), jnp.concatenate(ordered, axis=0), ROWS_T, preferred_element_type=F32
    ).astype(BF)


def per_device(byte_embed, score_weight, norm_gain, router, routes, expert_in, expert_out, cotangent):
    experts = router.shape[1]
    count = routes.shape[1]
    width = byte_embed.shape[2]
    full = width + LANES
    capacity = max(2, 3 * count // experts)
    pieces = lax.axis_size("seq")
    owners = lax.axis_size("exp")
    chunks = owners // 2
    rows = 2 * pieces * capacity
    slots = chunks * rows
    tokens = pieces * count
    hidden = expert_in.shape[2]
    tile = min(256, hidden)
    my = lax.axis_index("exp").astype(jnp.int32).reshape(1)
    embed = byte_embed[0]
    cot = cotangent[0]
    score_row = score_weight.reshape(1, width)
    gain_row = norm_gain.reshape(1, width)
    router_t = router.T
    routes_t = routes[0].T
    weight_in = expert_in[0]
    weight_out = expert_out[0]

    def shape(*dims, dtype=BF):
        return jax.ShapeDtypeStruct(dims, dtype)

    def over_seq(value, k):
        return lax.ppermute(value, "seq", [(i, i ^ k) for i in range(pieces)])

    def over_exp(values, step):
        moved = list(values)
        for m in sorted(range(1, len(values)), key=lambda m: (m & (2 // step - 1), -m)):
            moved[m] = lax.ppermute(values[m], "exp", [(i, i ^ (m * step)) for i in range(owners)])
        return moved

    def over_cores(value):
        return lax.ppermute(value, "exp", [(i, i ^ 1) for i in range(owners)])

    half = pieces // 2
    places = list(range(0, pieces, 2)) + list(range(1, pieces, 2))
    front_args = (embed, score_row, gain_row, router_t, routes_t)
    cot_far = [over_seq(cot, k) for k in places[1:half]]
    pay = call(
        front_kernel,
        "front",
        shape(count, full),
        front_args,
        us=2.0,
        scratch=[pltpu.VMEM((count, LANES), F32)],
        limit=56,
        held=False,
    )
    tok, keep = call(
        keep_kernel,
        "keep",
        (shape(count, width, dtype=F32), shape(count, LANES, dtype=F32)),
        (embed, score_row),
        us=2.0,
    )
    held_cot = call(functools.partial(gather_kernel, 0), "hold_cot", shape(count, width), (cot,), us=1.0)
    cot_near = call(
        functools.partial(gather_kernel, 0), "cot_near", shape(half * count, width), (held_cot, *cot_far), us=5.0
    )
    held = call(functools.partial(gather_kernel, 0), "hold_own", shape(count, full), (pay,), us=1.0)
    in_across = call(transpose_kernel, "across", shape(hidden, width), (weight_in,), us=2.0, limit=16)
    out_across = call(transpose_kernel, "across", shape(width, hidden), (weight_out,), us=2.0, limit=16)
    token_near = call(
        functools.partial(gather_kernel, 1),
        "token_near",
        shape(tokens, full),
        (cot_near, held, *[over_seq(pay, k) for k in places[1:]]),
    )
    cot_other, token_other = over_cores(cot_near), over_cores(token_near)
    cot_chosen = call(
        functools.partial(cot_pick_kernel, pieces, capacity),
        "cot_pick",
        [shape(rows // 2, width)] * chunks,
        (my, cot_near, token_near, cot_other, token_other),
        scalars=1,
        limit=16,
    )
    cot_chunks = over_exp(cot_chosen, 2)
    *chosen, pick = call(
        functools.partial(token_pick_kernel, pieces, capacity, 1),
        "token_pick",
        [shape(rows, full)] * chunks + [shape(slots, 2 * tokens)],
        (my, cot_chosen[0], token_near, token_other),
        scalars=1,
        limit=16,
    )
    token_chunks = over_exp(chosen, 2)
    pick_across = call(transpose_kernel, "across", shape(2 * tokens, slots), (pick,), us=1.0)
    order = [0, *range(chunks - 1, 0, -1)]
    groups = (order[: chunks // 2], order[chunks // 2 :])
    part = slots // 2
    near, far, upstream = [], [], []
    for group in groups:
        cot_a = call(
            functools.partial(gather_kernel, 0), "cot_slots", shape(part // 2, width), [cot_chunks[m] for m in group]
        )
        near.append(cot_a)
        far.append(over_seq(cot_a, 1))
    hiddens, upstream = [], []
    for cot_a, cot_b in zip(near, far):
        upstream.append(
            call(
                functools.partial(upstream_kernel, chunks, 0),
                "upstream",
                shape(part, hidden, dtype=F32),
                (cot_a, cot_b, out_across),
                limit=16,
            )
        )
    for g, group in enumerate(groups):
        waits = upstream[1:] if g else []
        hiddens.append(
            call(
                functools.partial(hidden_kernel, len(group), tile, len(waits)),
                "hidden",
                (shape(part, width), shape(part, LANES), shape(part, hidden), shape(part, hidden, dtype=F32)),
                (*waits, *[token_chunks[m] for m in group], weight_in),
                limit=16,
                us=1.0,
            )
        )
    stacked, back_rows = [], [None] * chunks
    for g, group in enumerate(groups):
        waits = upstream[1:] if g == 0 else []
        token_rows, tail, hidden_rows, slope = hiddens[g]
        *outs, hidden_grad = call(
            functools.partial(grad_kernel, len(group), len(waits)),
            "grads",
            [shape(rows, width)] * len(group) + [shape(part, hidden)],
            (my, *waits, hidden_rows, slope, tail, upstream[g], in_across, router_t),
            scalars=1,
            limit=16,
        )
        for m, out in zip(group, outs):
            back_rows[m] = out
        stacked += [near[g], far[g], hidden_rows, token_rows, hidden_grad]
    cot_slots, hidden_rows, token_slots, hidden_grad = call(
        functools.partial(stack_kernel, chunks),
        "stack",
        (shape(slots, width), shape(slots, hidden), shape(slots, width), shape(slots, hidden)),
        stacked,
        limit=16,
    )
    grad_out = lax.dot_general(hidden_rows, cot_slots, ROWS_T, preferred_element_type=F32)
    grad_in = lax.dot_general(token_slots, hidden_grad, ROWS_T, preferred_element_type=F32)
    returned = over_exp(back_rows, 2)
    *returned, grad_out = lax.optimization_barrier((*returned, grad_out))
    other_rows = call(combine_other_kernel, "combine_other", shape(tokens, width), (pick_across, *returned), limit=16)
    partial_rows = call(
        functools.partial(combine_own_kernel, chunks),
        "combine_own",
        [shape(count, width)] * pieces,
        (pick_across, *returned, over_cores(other_rows)),
        limit=16,
    )
    parts = [partial_rows[0]] + [over_seq(partial_rows[i], places[i]) for i in range(pieces - 1, 0, -1)]
    embed_grad = call(
        functools.partial(back_kernel, pieces),
        "back",
        shape(4 * count, width),
        (embed, score_row, gain_row, tok, keep, cot, *parts),
    )
    return (embed_grad[None], grad_in[None], grad_out[None])


def solution(mesh):
    in_specs = (
        P("exp", "seq", None),
        P(),
        P(),
        P(),
        P("exp", "seq", None),
        P("exp", None, "seq"),
        P("exp", "seq", None),
        P("exp", "seq", None),
    )
    out_specs = (P("exp", "seq", None), P("exp", None, "seq"), P("exp", "seq", None))
    return jax.shard_map(
        per_device, mesh=mesh, in_specs=in_specs, out_specs=out_specs, check_vma=False
    )
```

```python
import functools
import jax
import jax.numpy as jnp
from jax import lax
from jax.experimental import pallas as pl
from jax.experimental.pallas import tpu as pltpu
from jax.sharding import PartitionSpec as P

SQRT_HALF = 0.7071067811865476
INV_ROOT_TWO_PI = 0.3989422804014327
LANES = 128
GROUP = LANES // 4
BF = jnp.bfloat16
F32 = jnp.float32
HIGHEST = lax.Precision.HIGHEST
ROWS_T = (((0,), (0,)), ((), ()))
COLS = (((1,), (1,)), ((), ()))
MIB = 1024 * 1024
BYTES_PER_US = 3_000_000


def call(body, name, outs, args, us=0.0, scratch=(), limit=8, scalars=0, held=True):
    vmem = pl.BlockSpec(memory_space=pltpu.VMEM)
    smem = pl.BlockSpec(memory_space=pltpu.SMEM)
    rest = vmem if held else pl.BlockSpec()
    return pl.pallas_call(
        body,
        name=name,
        out_shape=outs,
        in_specs=[smem] * scalars + [rest] * (len(args) - scalars),
        out_specs=jax.tree.map(lambda _: vmem, outs),
        scratch_shapes=list(scratch),
        compiler_params=pltpu.CompilerParams(vmem_limit_bytes=limit * MIB),
        cost_estimate=pl.CostEstimate(flops=0, bytes_accessed=int(us * BYTES_PER_US), transcendentals=0),
    )(*args)


def route_mask(routes_t, k):
    count = routes_t.shape[1]
    lane = lax.broadcasted_iota(jnp.int32, (LANES, count), 0) % GROUP
    mask_t = (lane == routes_t[k : k + 1, :]).astype(F32).astype(BF)
    row = lax.broadcasted_iota(jnp.int32, (count, count), 0)
    col = lax.broadcasted_iota(jnp.int32, (count, count), 1)
    eye = (row == col).astype(F32).astype(BF)
    return lax.dot_general(eye, mask_t, COLS, preferred_element_type=F32)


def quartet_order(count):
    row = lax.broadcasted_iota(jnp.int32, (4 * count, 4 * count), 0)
    col = lax.broadcasted_iota(jnp.int32, (4 * count, 4 * count), 1)
    return (4 * (row % count) + row // count == col).astype(F32).astype(BF)


def quartet_values(embed, count):
    ordered = jnp.dot(quartet_order(count), embed, preferred_element_type=F32)
    return [ordered[q * count : (q + 1) * count, :] for q in range(4)]


def quartet_scores(values, weight):
    ones = [jnp.sum(v * weight, axis=1, keepdims=True) for v in values]
    pairs = [0.5 * (ones[0] + ones[1]), 0.5 * (ones[2] + ones[3])]
    four = 0.5 * (pairs[0] + pairs[1])
    shares = []
    for q in range(4):
        scores = (ones[q], pairs[q // 2], four)
        largest = jnp.maximum(jnp.maximum(scores[0], scores[1]), scores[2])
        weights = [jnp.exp(s - largest) for s in scores]
        denominator = weights[0] + weights[1] + weights[2]
        shares.append([w / denominator for w in weights])
    return shares


def pooled(values, weight):
    shares = quartet_scores(values, weight)
    whole = 0.25 * (shares[0][2] + shares[1][2] + shares[2][2] + shares[3][2])
    coefs = []
    for q in range(4):
        pair = 0.5 * (shares[q][1] + shares[q ^ 1][1])
        coefs.append(0.25 * (shares[q][0] + pair + whole))
    tokens = coefs[0] * values[0] + coefs[1] * values[1] + coefs[2] * values[2] + coefs[3] * values[3]
    scale = lax.rsqrt(jnp.mean(tokens * tokens, axis=1, keepdims=True) + 1e-06)
    return shares, coefs, tokens, scale


def front_kernel(embed_ref, score_ref, gain_ref, router_ref, routes_ref, pay_ref, logit):
    count = pay_ref.shape[0]
    experts, width = router_ref.shape
    _, _, tokens, scale = pooled(quartet_values(embed_ref[...], count), score_ref[...])
    normed = tokens * scale * gain_ref[...]
    high = normed.astype(BF)
    rest = normed - high.astype(F32)
    middle = rest.astype(BF)
    low = (rest - middle.astype(F32)).astype(BF)
    products = lax.dot_general(
        jnp.concatenate([high, middle, low], axis=0), router_ref[...], COLS, preferred_element_type=F32
    )
    logit[...] = jnp.zeros_like(logit)
    logit[:, :experts] = products[:count, :] + (products[count : 2 * count, :] + products[2 * count :, :])
    logits = logit[...]
    sigmoid = 1.0 / (1.0 + jnp.exp(-logits))
    rest = 1.0 / (1.0 + jnp.exp(logits))
    routes_t = routes_ref[...]
    masks = [route_mask(routes_t, k) for k in range(2)]
    group = lax.broadcasted_iota(jnp.int32, masks[0].shape, 1) // GROUP
    once = [jnp.where(group == 0, m, 0.0) for m in masks]
    picked = [jnp.sum(m * sigmoid, axis=1, keepdims=True) for m in once]
    others = [jnp.sum(m * rest, axis=1, keepdims=True) for m in once]
    total = picked[0] + picked[1]
    tail = jnp.zeros_like(masks[0])
    for mask, sig, other in zip(masks, picked, others):
        value = jnp.where(group == 0, 1.0, jnp.where(group == 1, other, jnp.where(group == 2, sig / total, 0.0)))
        tail = tail + mask * value
    pay_ref[:, :width] = high
    pay_ref[:, width:] = tail.astype(BF)


def keep_kernel(embed_ref, score_ref, tok_ref, keep_ref):
    count = tok_ref.shape[0]
    shares, coefs, tokens, scale = pooled(quartet_values(embed_ref[...], count), score_ref[...])
    tok_ref[...] = tokens
    columns = coefs + [s for share in shares for s in share] + [scale]
    lane = lax.broadcasted_iota(jnp.int32, keep_ref.shape, 1)
    kept = jnp.zeros(keep_ref.shape, F32)
    for i, column in enumerate(columns):
        kept = jnp.where(lane == i, column, kept)
    keep_ref[...] = kept


def transpose_kernel(in_ref, out_ref):
    out_ref[...] = in_ref[...].T


def gather_kernel(skipped, *refs):
    ins, out_ref = refs[skipped:-1], refs[-1]
    at = 0
    for r in ins:
        out_ref[at : at + r.shape[0], :] = r[...]
        at += r.shape[0]


def slot_places(tail, columns, count, capacity, my):
    tokens = tail.shape[0]
    at = lax.broadcasted_iota(jnp.int32, (LANES, LANES), 0)
    lane = lax.broadcasted_iota(jnp.int32, (LANES, LANES), 1)
    named_lane = (2 * (at % GROUP)) ^ my
    named_lane = jnp.where(at < GROUP, named_lane, named_lane + 2 * GROUP)
    live = (at % GROUP < columns) & (at < 2 * GROUP)
    order = ((lane == named_lane) & live).astype(F32).astype(BF)
    row = lax.broadcasted_iota(jnp.int32, (tokens, tokens), 0)
    col = lax.broadcasted_iota(jnp.int32, (tokens, tokens), 1)
    before = ((row < col) & (row // count == col // count)).astype(F32).astype(BF)
    ordered_t = lax.dot_general(order, tail, COLS, preferred_element_type=F32)
    named_t = ordered_t[:GROUP, :]
    place_t = jnp.dot(named_t.astype(BF), before, preferred_element_type=F32)
    block = lax.broadcasted_iota(jnp.int32, (GROUP, tokens), 1) // count
    place_t = place_t + (block * capacity).astype(F32)
    return jnp.where(named_t > 0.5, place_t, -1.0), ordered_t[GROUP : 2 * GROUP, :]


def selection(places, values, columns, rows):
    slot = lax.broadcasted_iota(jnp.int32, (rows, places.shape[1]), 0).astype(F32)
    picks = [jnp.where(places[m : m + 1, :] == slot, values[m : m + 1, :], 0.0) for m in range(columns)]
    return jnp.concatenate(picks, axis=0).astype(BF)


def cot_pick_kernel(pieces, capacity, my_ref, cot_ref, token_ref, other_cot_ref, other_token_ref, *outs):
    tokens, full = token_ref.shape
    width = full - LANES
    count = tokens // pieces
    cots = cot_ref.shape[0]
    tail = jnp.concatenate([token_ref[:cots, width:], other_token_ref[:cots, width:]], axis=0)
    places, gates = slot_places(tail, len(outs), count, capacity, my_ref[0])
    picks = selection(places, gates, len(outs), 2 * (pieces // 2) * capacity)
    cot_rows = jnp.concatenate([cot_ref[...], other_cot_ref[...]], axis=0)
    chosen = jnp.dot(picks, cot_rows, preferred_element_type=F32).astype(BF)
    for m, out in enumerate(outs):
        out[...] = chosen[m * out.shape[0] : (m + 1) * out.shape[0], :]


def token_pick_kernel(pieces, capacity, waits, my_ref, *refs):
    token_ref, other_token_ref, *outs, pick_ref = refs[waits:]
    tokens, full = token_ref.shape
    rows = jnp.concatenate([token_ref[...], other_token_ref[...]], axis=0)
    places, gates = slot_places(rows[:, full - LANES :], len(outs), tokens // pieces, capacity, my_ref[0])
    pick_ref[...] = selection(places, jnp.ones_like(gates), len(outs), 2 * pieces * capacity)
    chosen = jnp.dot(pick_ref[...], rows, preferred_element_type=F32).astype(BF)
    for m, out in enumerate(outs):
        out[...] = chosen[m * out.shape[0] : (m + 1) * out.shape[0], :]


def interleave(near, far, owners):
    share = near.shape[0] // owners
    return jnp.concatenate([r[d * share : (d + 1) * share, :] for d in range(owners) for r in (near, far)], axis=0)


def upstream_kernel(owners, waits, *refs):
    near_ref, far_ref, weight_ref, out_ref = refs[waits:]
    rows = jnp.concatenate([near_ref[...], far_ref[...]], axis=0)
    upstream = jnp.dot(rows, weight_ref[...], preferred_element_type=F32)
    half = near_ref.shape[0]
    out_ref[...] = interleave(upstream[:half, :], upstream[half:, :], owners)


def hidden_kernel(chunks, tile, waits, *refs):
    refs = refs[waits:]
    ins, (weight_ref, rows_ref, tail_ref, hidden_ref, slope_ref) = refs[:chunks], refs[chunks:]
    width = rows_ref.shape[1]
    token_rows = jnp.concatenate([r[:, :width] for r in ins], axis=0)
    rows_ref[...] = token_rows
    tail_ref[...] = jnp.concatenate([r[:, width:] for r in ins], axis=0)
    for f in range(weight_ref.shape[1] // tile):
        part = slice(f * tile, (f + 1) * tile)
        preact = jnp.dot(token_rows, weight_ref[:, part], preferred_element_type=F32)
        normal_cdf = 0.5 * (1.0 + lax.erf(preact * SQRT_HALF))
        normal_pdf = INV_ROOT_TWO_PI * jnp.exp(-0.5 * preact * preact)
        hidden_ref[:, part] = (preact * normal_cdf).astype(BF)
        slope_ref[:, part] = normal_cdf + preact * normal_pdf


def grad_kernel(chunks, waits, my_ref, *refs):
    hidden_ref, slope_ref, tail_ref, upstream_ref, weight_ref, router_ref = refs[waits : waits + 6]
    outs, grad_ref = refs[waits + 6 : -1], refs[-1]
    slots = hidden_ref.shape[0]
    experts, width = router_ref.shape
    rows = slots // chunks
    terms = jnp.zeros((slots, LANES), F32)
    for k in range(hidden_ref.shape[1] // LANES):
        part = slice(k * LANES, (k + 1) * LANES)
        upstream = upstream_ref[:, part]
        terms = terms + hidden_ref[:, part].astype(F32) * upstream
        grad_ref[:, part] = (upstream * slope_ref[:, part]).astype(BF)
    term = jnp.sum(terms, axis=1, keepdims=True)
    tail = tail_ref[...].astype(F32)
    lane = lax.broadcasted_iota(jnp.int32, (slots, LANES), 1)
    mine = lane % GROUP == my_ref[0]
    other_gate = jnp.sum(jnp.where((lane // GROUP == 2) & ~mine, tail, 0.0), axis=1, keepdims=True)
    spread = jnp.where(lane // GROUP == 1, jnp.where(mine, tail, -tail), 0.0) * (term * other_gate)
    high = spread.astype(BF)
    low = (spread - high.astype(F32)).astype(BF)
    router = router_ref[...].astype(F32)
    blank = jnp.zeros((GROUP, width), F32)
    padded = [router] if experts == GROUP else [router, jnp.zeros((GROUP - experts, width), F32)]
    router = jnp.concatenate([blank, *padded, blank, blank], axis=0).astype(BF)
    back = jnp.dot(grad_ref[...], weight_ref[...], preferred_element_type=F32)
    back = back + jnp.dot(high, router, preferred_element_type=F32) + jnp.dot(low, router, preferred_element_type=F32)
    back = back.astype(BF)
    for m, out in enumerate(outs):
        out[...] = back[m * rows : (m + 1) * rows, :]


def stack_kernel(owners, *refs):
    ins, outs = refs[:-4], refs[-4:]
    cots = [interleave(a[...].astype(F32), b[...].astype(F32), owners) for a, b in zip(ins[::5], ins[1::5])]
    outs[0][...] = jnp.concatenate(cots, axis=0).astype(BF)
    for i, out in enumerate(outs[1:]):
        out[...] = jnp.concatenate([r[...] for r in ins[2 + i :: 5]], axis=0)


def combine_other_kernel(pick_ref, *refs):
    ins, out_ref = refs[:-1], refs[-1]
    tokens = out_ref.shape[0]
    rows = jnp.concatenate([r[...] for r in ins], axis=0)
    out_ref[...] = lax.dot_general(pick_ref[:, tokens:], rows, ROWS_T, preferred_element_type=F32).astype(BF)


def combine_own_kernel(chunks, pick_ref, *refs):
    ins, other_ref, outs = refs[:chunks], refs[chunks], refs[chunks + 1 :]
    tokens = other_ref.shape[0]
    count = outs[0].shape[0]
    rows = jnp.concatenate([r[...] for r in ins], axis=0)
    back = lax.dot_general(pick_ref[:, :tokens], rows, ROWS_T, preferred_element_type=F32)
    back = (back + other_ref[...].astype(F32)).astype(BF)
    for k, out in enumerate(outs):
        out[...] = back[k * count : (k + 1) * count, :]


def back_kernel(pieces, embed_ref, score_ref, gain_ref, tok_ref, keep_ref, cot_ref, *refs):
    parts, out_ref = refs[:pieces], refs[pieces]
    count, width = tok_ref.shape
    values = quartet_values(embed_ref[...], count)
    kept = keep_ref[...]
    column = [kept[:, i : i + 1] for i in range(17)]
    coefs = column[:4]
    shares = [column[4 + 3 * q : 7 + 3 * q] for q in range(4)]
    scale = column[16]
    normed_grad = parts[0][...].astype(F32)
    for part in parts[1:]:
        normed_grad = normed_grad + part[...].astype(F32)
    tokens = tok_ref[...]
    scaled = gain_ref[...] * normed_grad
    inner = jnp.mean(tokens * scaled, axis=1, keepdims=True)
    token_grad = cot_ref[...].astype(F32) + scale * scaled - tokens * (scale * scale * scale * inner)
    dots = [jnp.sum(token_grad * v, axis=1, keepdims=True) for v in values]
    pairs = [dots[0] + dots[1], dots[2] + dots[3]]
    four = 0.0625 * (pairs[0] + pairs[1])
    score_grads = []
    for q in range(4):
        share = shares[q]
        grads = (0.25 * dots[q], 0.125 * pairs[q // 2], four)
        average = share[0] * grads[0] + share[1] * grads[1] + share[2] * grads[2]
        score_grads.append([s * (g - average) for s, g in zip(share, grads)])
    all_four = 0.25 * (score_grads[0][2] + score_grads[1][2] + score_grads[2][2] + score_grads[3][2])
    weight = score_ref[...]
    ordered = []
    for q in range(4):
        pair = 0.5 * (score_grads[q][1] + score_grads[q ^ 1][1])
        slope = score_grads[q][0] + pair + all_four
        ordered.append((coefs[q] * token_grad + slope * weight).astype(BF))
    out_ref[...] = lax.dot_general(
        quartet_order(count), jnp.concatenate(ordered, axis=0), ROWS_T, preferred_element_type=F32
    ).astype(BF)


def per_device(byte_embed, score_weight, norm_gain, router, routes, expert_in, expert_out, cotangent):
    experts = router.shape[1]
    count = routes.shape[1]
    width = byte_embed.shape[2]
    full = width + LANES
    capacity = max(2, 3 * count // experts)
    pieces = lax.axis_size("seq")
    owners = lax.axis_size("exp")
    chunks = owners // 2
    rows = 2 * pieces * capacity
    slots = chunks * rows
    tokens = pieces * count
    hidden = expert_in.shape[2]
    tile = min(256, hidden)
    my = lax.axis_index("exp").astype(jnp.int32).reshape(1)
    embed = byte_embed[0]
    cot = cotangent[0]
    score_row = score_weight.reshape(1, width)
    gain_row = norm_gain.reshape(1, width)
    router_t = router.T
    routes_t = routes[0].T
    weight_in = expert_in[0]
    weight_out = expert_out[0]

    def shape(*dims, dtype=BF):
        return jax.ShapeDtypeStruct(dims, dtype)

    def over_seq(value, k):
        return lax.ppermute(value, "seq", [(i, i ^ k) for i in range(pieces)])

    def over_exp(values, step):
        moved = list(values)
        for m in sorted(range(1, len(values)), key=lambda m: (m & (2 // step - 1), -m)):
            moved[m] = lax.ppermute(values[m], "exp", [(i, i ^ (m * step)) for i in range(owners)])
        return moved

    def over_cores(value):
        return lax.ppermute(value, "exp", [(i, i ^ 1) for i in range(owners)])

    half = pieces // 2
    places = list(range(0, pieces, 2)) + list(range(1, pieces, 2))
    front_args = (embed, score_row, gain_row, router_t, routes_t)
    cot_far = [over_seq(cot, k) for k in places[1:half]]
    pay = call(
        front_kernel,
        "front",
        shape(count, full),
        front_args,
        us=2.0,
        scratch=[pltpu.VMEM((count, LANES), F32)],
        limit=56,
        held=False,
    )
    tok, keep = call(
        keep_kernel,
        "keep",
        (shape(count, width, dtype=F32), shape(count, LANES, dtype=F32)),
        (embed, score_row),
        us=2.0,
    )
    held_cot = call(functools.partial(gather_kernel, 0), "hold_cot", shape(count, width), (cot,), us=1.0)
    cot_near = call(
        functools.partial(gather_kernel, 0), "cot_near", shape(half * count, width), (held_cot, *cot_far), us=0.0
    )
    held = call(functools.partial(gather_kernel, 0), "hold_own", shape(count, full), (pay,), us=1.0)
    in_across = call(transpose_kernel, "across", shape(hidden, width), (weight_in,), us=2.0, limit=16)
    out_across = call(transpose_kernel, "across", shape(width, hidden), (weight_out,), us=2.0, limit=16)
    token_near = call(
        functools.partial(gather_kernel, 1),
        "token_near",
        shape(tokens, full),
        (cot_near, held, *[over_seq(pay, k) for k in places[1:]]),
    )
    cot_other, token_other = over_cores(cot_near), over_cores(token_near)
    cot_chosen = call(
        functools.partial(cot_pick_kernel, pieces, capacity),
        "cot_pick",
        [shape(rows // 2, width)] * chunks,
        (my, cot_near, token_near, cot_other, token_other),
        scalars=1,
        limit=16,
    )
    cot_chunks = over_exp(cot_chosen, 2)
    *chosen, pick = call(
        functools.partial(token_pick_kernel, pieces, capacity, 1),
        "token_pick",
        [shape(rows, full)] * chunks + [shape(slots, 2 * tokens)],
        (my, cot_chosen[0], token_near, token_other),
        scalars=1,
        limit=16,
    )
    token_chunks = over_exp(chosen, 2)
    order = [0, *range(chunks - 1, 0, -1)]
    groups = (order[: chunks // 2], order[chunks // 2 :])
    part = slots // 2
    near, far, upstream = [], [], []
    for group in groups:
        cot_a = call(
            functools.partial(gather_kernel, 0), "cot_slots", shape(part // 2, width), [cot_chunks[m] for m in group]
        )
        near.append(cot_a)
        far.append(over_seq(cot_a, 1))
    hiddens, upstream = [], []
    for cot_a, cot_b in zip(near, far):
        upstream.append(
            call(
                functools.partial(upstream_kernel, chunks, 0),
                "upstream",
                shape(part, hidden, dtype=F32),
                (cot_a, cot_b, out_across),
                limit=16,
            )
        )
    for g, group in enumerate(groups):
        waits = upstream[1:] if g else []
        hiddens.append(
            call(
                functools.partial(hidden_kernel, len(group), tile, len(waits)),
                "hidden",
                (shape(part, width), shape(part, LANES), shape(part, hidden), shape(part, hidden, dtype=F32)),
                (*waits, *[token_chunks[m] for m in group], weight_in),
                limit=16,
                us=1.0,
            )
        )
    stacked, back_rows = [], [None] * chunks
    for g, group in enumerate(groups):
        waits = upstream[1:] if g == 0 else []
        token_rows, tail, hidden_rows, slope = hiddens[g]
        *outs, hidden_grad = call(
            functools.partial(grad_kernel, len(group), len(waits)),
            "grads",
            [shape(rows, width)] * len(group) + [shape(part, hidden)],
            (my, *waits, hidden_rows, slope, tail, upstream[g], in_across, router_t),
            scalars=1,
            limit=16,
        )
        for m, out in zip(group, outs):
            back_rows[m] = out
        stacked += [near[g], far[g], hidden_rows, token_rows, hidden_grad]
    cot_slots, hidden_rows, token_slots, hidden_grad = call(
        functools.partial(stack_kernel, chunks),
        "stack",
        (shape(slots, width), shape(slots, hidden), shape(slots, width), shape(slots, hidden)),
        stacked,
        limit=16,
    )
    grad_out = lax.dot_general(hidden_rows, cot_slots, ROWS_T, preferred_element_type=F32)
    grad_in = lax.dot_general(token_slots, hidden_grad, ROWS_T, preferred_element_type=F32)
    returned = over_exp(back_rows, 2)
    *returned, grad_out = lax.optimization_barrier((*returned, grad_out))
    other_rows = call(combine_other_kernel, "combine_other", shape(tokens, width), (pick, *returned), limit=16)
    partial_rows = call(
        functools.partial(combine_own_kernel, chunks),
        "combine_own",
        [shape(count, width)] * pieces,
        (pick, *returned, over_cores(other_rows)),
        limit=16,
    )
    parts = [partial_rows[0]] + [over_seq(partial_rows[i], places[i]) for i in range(pieces - 1, 0, -1)]
    embed_grad = call(
        functools.partial(back_kernel, pieces),
        "back",
        shape(4 * count, width),
        (embed, score_row, gain_row, tok, keep, cot, *parts),
    )
    return (embed_grad[None], grad_in[None], grad_out[None])


def solution(mesh):
    in_specs = (
        P("exp", "seq", None),
        P(),
        P(),
        P(),
        P("exp", "seq", None),
        P("exp", None, "seq"),
        P("exp", "seq", None),
        P("exp", "seq", None),
    )
    out_specs = (P("exp", "seq", None), P("exp", None, "seq"), P("exp", "seq", None))
    return jax.shard_map(
        per_device, mesh=mesh, in_specs=in_specs, out_specs=out_specs, check_vma=False
    )
```
